32 devices in a mesh: grp: 2 (over core), dev: 16 (over z, y, x).
Axes of the slice: x: 2, y: 2, z: 4, core: 2. Of those that a mesh axis runs over, the one named last changes fastest.
Arguments:
- features: bfloat16 [2, 256, 128, 256], P('grp', 'dev'), may hold values from -6 to 6
- offsets: float32 [2, 256, 3, 128], P('grp', 'dev'), may hold values from 0 to 1
- radial: bfloat16 [2, 256, 8, 128, 128], P('grp', 'dev'), may hold values from -0.25 to 0.25
- neighbours: int32 [2, 256, 8], P('grp', 'dev'), may hold values from 0 to 8, as said below
- counts: int32 [2, 256], P('grp', 'dev'), may hold values from 16 to 128
- wavevectors: int32 [3, 1024], replicated, may hold values from -8 to 8
- w_msg: bfloat16 [256, 256], replicated, may hold values from -0.375 to 0.375
- w_mix: bfloat16 [256, 256], replicated, may hold values from -0.375 to 0.375
Outputs:
- updated: bfloat16 [2, 256, 128, 256], P('grp', 'dev')
The draws below stay inside these ranges and needn't reach their ends.
Inputs may be any that keep to these rules, and one draw needn't show every extreme that they name: `neighbours`: A cell's 8 codes are distinct; code c names the cell at (c // 3 - 1) slabs and (c % 3 - 1) cells away along the slab.
All inputs are finite; a program needn't handle non-finite values.
Results may differ from the reference program's by a relative error of at most 0.018.
Values may be sent and summed in bfloat16 or wider, within the bound.
No kernel may reach another device: no remote copies, remote signals or barrier semaphores. Data moves between devices by JAX's collectives and lax.ppermute only.
A program may use at most 128 MiB of HBM per device.

```python
import math
import jax
import jax.numpy as jnp
from jax import lax

CHANNELS = 256
WAVES = 1024
ATOMS = 128
PAIRS = 8
GRID_Z = 2
CELL_LINE = 256
TOTAL_SLOTS = 65536


def draw_neighbours(key, part):
    scores = jax.random.randint(key, (GRID_Z, CELL_LINE, 9), 0, 1 << 20) * 16 + jnp.arange(9, dtype=jnp.int32)
    values, picked = lax.top_k(scores, PAIRS)
    return picked.astype(jnp.int32)


def set_ends(values, rng, least, largest):
    dims = values.shape
    place = [jax.random.randint(jax.random.fold_in(rng, axis), (), 0, dims[axis]) for axis in range(len(dims))]
    values = values.at[tuple(place)].set(least)
    longest = dims.index(max(dims))
    place[longest] = (place[longest] + 1) % dims[longest]
    return values.at[tuple(place)].set(largest)


def block_levels(own_key, shape, split, smallest, largest):
    def one(dim, shards_of):
        draws = jax.random.uniform(jax.random.fold_in(jax.random.fold_in(own_key, 6), dim), (shards_of,), jnp.float32, smallest / len(split), largest / len(split))
        return jnp.repeat(jnp.exp(draws), shape[dim] // shards_of).reshape((-1,) + (1,) * (len(shape) - dim - 1))

    gain = one(*split[0])
    for cut in split[1:]:
        gain = gain * one(*cut)
    return gain


def gaussian(own_key, extent, spread, most, shards=(), held_as=jnp.bfloat16):
    drawn = spread * jax.random.normal(own_key, extent, jnp.float32)
    if shards:
        drawn = drawn * block_levels(own_key, extent, shards, -0.22, 0.18)
    return jnp.clip(drawn, -most, most).astype(held_as)


def setup_inputs(seed: int = 0) -> dict:
    seeds = jax.random.split(jax.random.key(seed), 9)
    features = gaussian(seeds[0], (GRID_Z, CELL_LINE, ATOMS, CHANNELS), 1.0, 6.0, ((0, 2), (1, 16)))
    offsets = jnp.clip(1.0 * jax.random.uniform(seeds[1], (GRID_Z, CELL_LINE, 3, ATOMS), jnp.float32) ** block_levels(seeds[1], (GRID_Z, CELL_LINE, 3, ATOMS), ((0, 2), (1, 16)), -0.2, 0.2), 0.0, 1.0)
    radial = gaussian(seeds[2], (GRID_Z, CELL_LINE, PAIRS, ATOMS, ATOMS), (ATOMS * PAIRS // 2) ** -0.5, 0.25, ((0, 2), (1, 16)))
    neighbours = draw_neighbours(jax.random.fold_in(seeds[8], 71), 0)
    counts = set_ends(jax.random.randint(seeds[4], (GRID_Z, CELL_LINE), ATOMS // 8, ATOMS + 1), jax.random.fold_in(seeds[4], 1), ATOMS // 8, ATOMS).astype(jnp.int32)
    wavevectors = set_ends(jax.random.randint(seeds[5], (3, WAVES), -8, 9), jax.random.fold_in(seeds[5], 1), -8, 8).astype(jnp.int32)
    w_msg = gaussian(seeds[6], (CHANNELS, CHANNELS), CHANNELS ** -0.5, 0.375)
    w_mix = gaussian(seeds[7], (CHANNELS, CHANNELS), CHANNELS ** -0.5, 0.375)
    return {"features": features, "offsets": offsets, "radial": radial, "neighbours": neighbours, "counts": counts, "wavevectors": wavevectors, "w_msg": w_msg, "w_mix": w_mix}


def wave_kernel(wavevectors):
    waves = wavevectors.astype(jnp.float32)
    square = lax.optimization_barrier(jnp.sum(waves * waves, axis=0))
    kernel = jnp.exp(-square / 128.0) / (1.0 + square / 64.0)
    return jnp.concatenate([kernel, kernel])

def trig_rows(offsets, group, wavevectors):
    waves = wavevectors.astype(jnp.float32)
    cell_pos = jnp.arange(CELL_LINE, dtype=jnp.int32).astype(jnp.float32)
    along_x = (cell_pos[:, None] + offsets[:, 0, :]) / CELL_LINE
    along_y = offsets[:, 1, :]
    along_z = (group.astype(jnp.float32) + offsets[:, 2, :]) / GRID_Z
    phase = 2.0 * math.pi * (along_x[..., None] * waves[0] + along_y[..., None] * waves[1] + along_z[..., None] * waves[2])
    table = jnp.concatenate([jnp.cos(phase), jnp.sin(phase)], axis=-1).astype(jnp.bfloat16)
    return table.reshape(CELL_LINE * ATOMS, 2 * WAVES)

def reference(features, offsets, radial, neighbours, counts, wavevectors, w_msg, w_mix):
    slot_ids = jnp.arange(ATOMS, dtype=jnp.int32)
    masking = (slot_ids[None, None, :] < counts[:, :, None]).astype(jnp.bfloat16)
    masked = features * masking[..., None]
    padded = jnp.pad(masked, ((1, 1), (1, 1), (0, 0), (0, 0)))
    cell_ids = jnp.arange(CELL_LINE, dtype=jnp.int32)
    groups = jnp.arange(GRID_Z, dtype=jnp.int32)

    def short_group(group):
        window = lax.dynamic_slice_in_dim(padded, group, 3, 0)
        codes = neighbours[group]
        blocks = radial[group]
        total = jnp.zeros((CELL_LINE, ATOMS, CHANNELS), jnp.float32)
        for neighbour in range(PAIRS):
            code = codes[:, neighbour]
            picked = window[code // 3, cell_ids + code % 3]
            total = total + jnp.einsum('kab,kbc->kac', blocks[:, neighbour].astype(jnp.float32), picked.astype(jnp.float32))
        return total
    gathered = lax.map(short_group, groups)

    def factor_group(group):
        table = trig_rows(offsets[group], group, wavevectors)
        return lax.dot_general(table, masked[group].reshape(CELL_LINE * ATOMS, CHANNELS), (((0,), (0,)), ((), ())), preferred_element_type=jnp.float32)
    sums = lax.optimization_barrier(jnp.sum(lax.map(factor_group, groups), axis=0))
    factors = (sums * (1.0 / math.sqrt(TOTAL_SLOTS))).astype(jnp.bfloat16)
    energy = (jnp.dot(factors, w_mix, preferred_element_type=jnp.float32) * wave_kernel(wavevectors)[:, None]).astype(jnp.bfloat16)

    def finish_group(group):
        table = trig_rows(offsets[group], group, wavevectors)
        longrange = jnp.dot(table, energy, preferred_element_type=jnp.float32) * (8.0 / math.sqrt(WAVES))
        message = jnp.dot(gathered[group].reshape(CELL_LINE * ATOMS, CHANNELS).astype(jnp.bfloat16), w_msg, preferred_element_type=jnp.float32)
        own = masked[group].reshape(CELL_LINE * ATOMS, CHANNELS).astype(jnp.float32)
        result = own + jax.nn.silu(message + longrange)
        result = result * masking[group].reshape(CELL_LINE * ATOMS, 1).astype(jnp.float32)
        return result.astype(jnp.bfloat16).reshape(CELL_LINE, ATOMS, CHANNELS)
    return lax.map(finish_group, groups)
```

```python
import functools
import math

import jax
import jax.numpy as jnp
from jax import lax
from jax.experimental import pallas as pl
from jax.experimental.pallas import tpu as pltpu
from jax.sharding import PartitionSpec as P

F32 = jnp.float32
BF16 = jnp.bfloat16
VMEM = pl.BlockSpec(memory_space=pltpu.VMEM)
SMEM = pl.BlockSpec(memory_space=pltpu.SMEM)
PARAMS = pltpu.CompilerParams(vmem_limit_bytes=56 * 1024 * 1024)
SIN = (4.44287957, -7.30781668, 3.59777418, -0.79119939)
COS = (1.41420401, -6.97763732, 5.71518787, -1.72821389)


def radices(count):
    digits = []
    stride = 1
    while stride < count:
        rest = count // stride
        radix = 4 if rest % 4 == 0 else 2 if rest % 2 == 0 else rest
        digits.append((stride, radix))
        stride *= radix
    return digits


def to_offset(axis, stride, radix, offset):
    pairs = []
    for place in range(lax.axis_size(axis)):
        digit = place // stride % radix
        pairs.append((place, place + ((digit + offset) % radix - digit) * stride))
    return pairs


def cosine_sine(turns):
    part = turns - jnp.round(turns)
    square = part * part
    sine = part * (SIN[0] + square * (SIN[1] + square * (SIN[2] + square * SIN[3])))
    cosine = COS[0] + square * (COS[1] + square * (COS[2] + square * COS[3]))
    return 1.0 - sine * sine, sine * cosine


def table_kernel(tile, lengths, has_rows, has_start, keeps, *refs):
    refs = list(refs)
    place_ref, offsets_ref, waves_ref = refs[:3]
    refs = refs[3:]
    rows_ref = refs.pop(0) if has_rows else None
    start_ref = refs.pop(0) if has_start else None
    table_ref = refs.pop(0) if keeps else None
    sums_ref = refs.pop(0) if has_rows else None
    places_ref = refs.pop(0)
    cell_line, slabs = lengths
    cells, _, slots = offsets_ref.shape

    @pl.when(pl.program_id(0) == 0)
    def _():
        line = lax.broadcasted_iota(jnp.int32, (8, slots), 0)
        for cell in range(cells):
            own = offsets_ref[cell]
            first = (place_ref[0] + cell).astype(F32)
            along_x = (first + own[0:1]) / cell_line
            along_z = (place_ref[1].astype(F32) + own[2:3]) / slabs
            full = jnp.where(
                line == 0, along_x, jnp.where(line == 1, own[1:2], jnp.where(line == 2, along_z, 0.0))
            )
            high = full.astype(BF16).astype(F32)
            middle = (full - high).astype(BF16).astype(F32)
            low = full - high - middle
            parts = jnp.concatenate([high, middle, low, jnp.zeros_like(low)], axis=0)
            places_ref[:, cell * slots : (cell + 1) * slots] = parts.astype(BF16)

    waves = waves_ref[...]
    block = waves.shape[0]
    total = start_ref[0] if has_start else None
    for first in range(0, cells * slots, tile):
        span = slice(first, first + tile)
        turns = jnp.dot(waves, places_ref[:, span], preferred_element_type=F32)
        cosine, sine = cosine_sine(turns)
        both = jnp.concatenate([cosine.astype(BF16), sine.astype(BF16)], axis=0)
        if keeps:
            table_ref[0, :, span] = both
        if has_rows:
            part = jnp.dot(both, rows_ref[span, :], preferred_element_type=F32)
            total = part if total is None else total + part
    if has_rows:
        sums_ref[0] = total.astype(sums_ref.dtype)


def table_call(place, offsets, waves, blocks, lengths, rows=None, start=None, keeps=True, sums_type=F32):
    cells, _, slots = offsets.shape
    atoms = cells * slots
    block = waves.shape[0] // blocks
    operands = [place, offsets, waves]
    in_specs = [
        SMEM,
        pl.BlockSpec(offsets.shape, lambda i: (0, 0, 0)),
        pl.BlockSpec((block, waves.shape[1]), lambda i: (i, 0)),
    ]
    out_shape, out_specs = [], []
    if keeps:
        out_shape.append(jax.ShapeDtypeStruct((blocks, 2 * block, atoms), BF16))
        out_specs.append(pl.BlockSpec((1, 2 * block, atoms), lambda i: (i, 0, 0)))
    if rows is not None:
        channels = rows.shape[1]
        operands.append(rows)
        in_specs.append(pl.BlockSpec(rows.shape, lambda i: (0, 0)))
        sums_spec = pl.BlockSpec((1, 2 * block, channels), lambda i: (i, 0, 0))
        if start is not None:
            operands.append(start)
            in_specs.append(sums_spec)
        out_shape.append(jax.ShapeDtypeStruct((blocks, 2 * block, channels), sums_type))
        out_specs.append(sums_spec)
    tile = math.gcd(atoms, 256)
    return pl.pallas_call(
        functools.partial(table_kernel, tile, lengths, rows is not None, start is not None, keeps),
        grid=(blocks,),
        in_specs=in_specs,
        out_specs=out_specs,
        out_shape=out_shape,
        scratch_shapes=[pltpu.VMEM((32, atoms), BF16)],
        compiler_params=PARAMS,
    )(*operands)


def short_kernel(groups, lines, picks_ref, radial_ref, *refs):
    row_refs = refs[:lines]
    before_ref, after_ref, w_ref, message_ref, window_ref = refs[lines:]
    cells, slots, channels = row_refs[0].shape
    step = pl.program_id(0)

    @pl.when(step == 0)
    def _():
        for line in range(lines):
            base = line * (cells + 2)
            window_ref[base] = before_ref[line]
            for cell in range(cells):
                window_ref[base + 1 + cell] = row_refs[line][cell]
            window_ref[base + 1 + cells] = after_ref[line]
        window_ref[lines * (cells + 2)] = jnp.zeros((slots, channels), BF16)

    pairs = radial_ref.shape[1]
    for cell in range(groups):
        total = None
        for pair in range(0, pairs, 2):
            here = list(range(pair, min(pair + 2, pairs)))
            blocks = [radial_ref[cell, p] for p in here]
            taken = [window_ref[picks_ref[(step * groups + cell) * pairs + p]] for p in here]
            left = jnp.concatenate(blocks, axis=1)
            right = jnp.concatenate(taken, axis=0)
            part = jnp.dot(left, right, preferred_element_type=F32)
            total = part if total is None else total + part
        message_ref[cell] = jnp.dot(total.astype(BF16), w_ref[...], preferred_element_type=F32)


def short_call(picks, radial, rows, before, after, w_msg):
    cells, slots, channels = rows[0].shape
    groups = math.gcd(cells, 2)
    lines = len(rows)
    return pl.pallas_call(
        functools.partial(short_kernel, groups, lines),
        grid=(cells // groups,),
        in_specs=[
            SMEM,
            pl.BlockSpec((groups,) + radial.shape[1:], lambda i: (i, 0, 0, 0)),
            *[pl.BlockSpec(rows[0].shape, lambda i: (0, 0, 0))] * lines,
            *[pl.BlockSpec(before.shape, lambda i: (0, 0, 0))] * 2,
            pl.BlockSpec(w_msg.shape, lambda i: (0, 0)),
        ],
        out_specs=pl.BlockSpec((groups, slots, channels), lambda i: (i, 0, 0)),
        out_shape=jax.ShapeDtypeStruct((cells, slots, channels), F32),
        scratch_shapes=[pltpu.VMEM((lines * (cells + 2) + 1, slots, channels), BF16)],
        compiler_params=PARAMS,
    )(picks, radial, *rows, before, after, w_msg)


def add_kernel(count, radix, *refs):
    pieces, outs = refs[:count], refs[count:]
    total = pieces[0][...].astype(F32)
    for piece in pieces[1:]:
        total = total + piece[...].astype(F32)
    rows = total.shape[1] // radix
    for place, out in enumerate(outs):
        out[...] = total[:, place * rows : (place + 1) * rows].astype(out.dtype)


def add_and_cut(pieces, radix):
    trig, rows, channels = pieces[0].shape
    part = (trig, rows // radix, channels)
    types = [F32] + [BF16] * (radix - 1)
    if part[1] % 16:
        total = functools.reduce(jnp.add, [piece.astype(F32) for piece in pieces])
        return [
            total[:, place * part[1] : (place + 1) * part[1]].astype(kind) for place, kind in enumerate(types)
        ]
    return pl.pallas_call(
        functools.partial(add_kernel, len(pieces), radix),
        in_specs=[VMEM] * len(pieces),
        out_specs=[VMEM] * radix,
        out_shape=[jax.ShapeDtypeStruct(part, kind) for kind in types],
        compiler_params=PARAMS,
    )(*pieces)


def final_kernel(blocks, scale, energies, counts_ref, mine_ref, other_ref, message_ref, masked_ref, *refs):
    energy_refs = refs[:energies]
    out_ref, turned_ref = refs[energies:]
    cells, slots, channels = masked_ref.shape
    step = pl.program_id(0)

    @pl.when(step == 0)
    def _():
        for place, energy in enumerate(energy_refs):
            turned_ref[place] = energy[...].astype(F32).T.astype(BF16)

    total = None
    for place in range(blocks):
        part = jnp.dot(turned_ref[place], mine_ref[place], preferred_element_type=F32)
        total = part if total is None else total + part
    for place in range(blocks):
        total = total + jnp.dot(turned_ref[blocks + place], other_ref[place], preferred_element_type=F32)
    slot_ids = lax.broadcasted_iota(jnp.int32, (slots, channels), 0)
    for cell in range(cells):
        value = total[:, cell * slots : (cell + 1) * slots].T * scale + message_ref[cell]
        value = value * (0.5 + 0.5 * jnp.tanh(0.5 * value))
        result = masked_ref[cell].astype(F32) + value
        result = jnp.where(slot_ids < counts_ref[step * cells + cell], result, 0.0)
        out_ref[cell] = result.astype(BF16)


def final_call(counts, mine, other, message, masked, energies, scale):
    cells, slots, channels = masked.shape
    blocks, rows, _ = mine.shape
    group = math.gcd(cells, 4)
    table_spec = pl.BlockSpec((blocks, rows, group * slots), lambda i: (0, 0, i))
    cell_spec = pl.BlockSpec((group, slots, channels), lambda i: (i, 0, 0))
    return pl.pallas_call(
        functools.partial(final_kernel, blocks, scale, len(energies)),
        grid=(cells // group,),
        in_specs=[
            SMEM,
            table_spec,
            table_spec,
            cell_spec,
            cell_spec,
            *[pl.BlockSpec((rows, channels), lambda i: (0, 0))] * len(energies),
        ],
        out_specs=cell_spec,
        out_shape=jax.ShapeDtypeStruct(masked.shape, BF16),
        scratch_shapes=[pltpu.VMEM((len(energies), channels, rows), BF16)],
        compiler_params=PARAMS,
    )(counts, mine, other, message, masked, *energies)


def body(features, offsets, radial, neighbours, counts, wavevectors, w_msg, w_mix):
    _, cells, slots, channels = features.shape
    wave_count = wavevectors.shape[1]
    slabs, dev_count = lax.axis_size("grp"), lax.axis_size("dev")
    slab, dev = lax.axis_index("grp"), lax.axis_index("dev")
    cell_line = cells * dev_count
    total_slots = slabs * cell_line * slots
    atoms = cells * slots
    lengths = (float(cell_line), float(slabs))

    slot_ids = jnp.arange(slots, dtype=jnp.int32)
    masking = slot_ids[None, :] < counts[0][:, None]
    masked = jnp.where(masking[..., None], features[0], jnp.bfloat16(0))
    offsets = offsets[0]

    swap = to_offset("grp", 1, 2, 1)
    sibling_offsets = lax.ppermute(offsets, "grp", swap)
    if slabs == 2:
        sibling = lax.ppermute(masked, "grp", swap)
        lines = [masked, sibling]
    else:
        up = [(i, i + 1) for i in range(slabs - 1)]
        below = lax.ppermute(masked, "grp", up)
        above = lax.ppermute(masked, "grp", [(j, i) for i, j in up])
        sibling = jnp.where(slab % 2 == 0, above, below)
        lines = [masked, below, above]

    stages = [("dev", *digit) for digit in radices(dev_count)]
    stages += [("grp", 2 * stride, radix) for stride, radix in radices(slabs // 2)]
    digits = [("grp", 1, 2)] + stages

    waves = wavevectors.astype(F32).T.reshape(*[radix for _, _, radix in digits], -1, 3)
    for dim, (axis, stride, radix) in enumerate(digits):
        digit = (slab if axis == "grp" else dev) // stride % radix
        waves = jnp.roll(waves, -digit, axis=dim)
    waves = waves.reshape(wave_count, 3)
    owned_waves = wave_count // (slabs * dev_count)
    square = jnp.sum(waves[:owned_waves] ** 2, axis=1)
    kernel = jnp.exp(-square / 128.0) / (1.0 + square / 64.0)
    thrice = jnp.pad(waves, ((0, 0), (0, 5))).astype(BF16)
    thrice = jnp.concatenate([thrice, thrice, thrice, jnp.zeros_like(thrice)], axis=1)
    half = wave_count // 2
    blocks = stages[0][2]

    own_place = jnp.stack([dev * cells, slab]).astype(jnp.int32)
    other_place = jnp.stack([dev * cells, slab ^ 1]).astype(jnp.int32)
    own_rows = masked.reshape(atoms, channels)
    mine, sums = table_call(own_place, offsets, thrice[:half], blocks, lengths, rows=own_rows)
    (sums,) = table_call(
        other_place, sibling_offsets, thrice[:half], blocks, lengths,
        rows=sibling.reshape(atoms, channels), start=sums, keeps=False,
    )

    rows = half // blocks
    parts = [sums[0].reshape(2, rows, channels)]
    parts += [sums[place].astype(BF16).reshape(2, rows, channels) for place in range(1, blocks)]
    for stage, (axis, stride, radix) in enumerate(stages):
        received = [
            lax.ppermute(parts[place], axis, to_offset(axis, stride, radix, place)) for place in range(1, radix)
        ]
        cut = stages[stage + 1][2] if stage + 1 < len(stages) else 1
        parts = add_and_cut([parts[0], *received], cut)
    owned = parts[0].reshape(2 * owned_waves, channels)
    factors = (owned * (1.0 / math.sqrt(total_slots))).astype(BF16)
    energy = jnp.dot(factors, w_mix, preferred_element_type=F32).reshape(2, owned_waves, channels)
    energy = (energy * kernel[None, :, None]).astype(BF16)

    (other,) = table_call(own_place, offsets, thrice[half:], blocks, lengths)
    first = jnp.stack([line[0] for line in lines])
    last = jnp.stack([line[cells - 1] for line in lines])
    right = [(i, i + 1) for i in range(dev_count - 1)]
    before = lax.ppermute(last, "dev", right)
    after = lax.ppermute(first, "dev", [(j, i) for i, j in right])
    codes = neighbours[0]
    level = codes // 3 - 1
    if slabs == 2:
        line = jnp.where(level == 0, 0, 1)
    else:
        line = jnp.where(level == 0, 0, jnp.where(level < 0, 1, 2))
    inside = (slab + level >= 0) & (slab + level < slabs)
    picks = line * (cells + 2) + jnp.arange(cells, dtype=jnp.int32)[:, None] + codes % 3
    picks = jnp.where(inside, picks, len(lines) * (cells + 2)).reshape(-1)
    message = short_call(picks, radial[0], lines, before, after, w_msg)

    for axis, stride, radix in reversed(stages[1:]):
        pieces = [energy]
        for place in range(1, radix):
            pieces.append(lax.ppermute(energy, axis, to_offset(axis, stride, radix, -place)))
        energy = jnp.concatenate(pieces, axis=1)
    axis, stride, radix = stages[0]
    energies = [energy]
    for place in range(1, radix):
        energies.append(lax.ppermute(energy, axis, to_offset(axis, stride, radix, -place)))
    energies += [lax.ppermute(piece, "grp", swap) for piece in energies]
    energies = [piece.reshape(2 * rows, channels) for piece in energies]

    scale = 8.0 / math.sqrt(wave_count)
    result = final_call(counts[0], mine, other, message, masked, energies, scale)
    return result[None]


def solution(mesh):
    in_specs = (
        P("grp", "dev", None, None),
        P("grp", "dev", None, None),
        P("grp", "dev", None, None, None),
        P("grp", "dev", None),
        P("grp", "dev"),
        P(),
        P(),
        P(),
    )
    out_specs = P("grp", "dev", None, None)
    return jax.shard_map(body, mesh=mesh, in_specs=in_specs, out_specs=out_specs, check_vma=False)
```

```python
import functools
import math

import jax
import jax.numpy as jnp
from jax import lax
from jax.experimental import pallas as pl
from jax.experimental.pallas import tpu as pltpu
from jax.sharding import PartitionSpec as P

F32 = jnp.float32
BF16 = jnp.bfloat16
VMEM = pl.BlockSpec(memory_space=pltpu.VMEM)
SMEM = pl.BlockSpec(memory_space=pltpu.SMEM)
PARAMS = pltpu.CompilerParams(vmem_limit_bytes=16 * 1024 * 1024)
LANES = 128
SIN = (4.44287957, -7.30781668, 3.59777418, -0.79119939)
COS = (1.41420401, -6.97763732, 5.71518787, -1.72821389)


def here(array):
    return pltpu.with_memory_space_constraint(array, pltpu.VMEM)


def call(kernel, outs, vmem, smem=(), scratch=()):
    return pl.pallas_call(
        kernel,
        in_specs=[SMEM] * len(smem) + [VMEM] * len(vmem),
        out_specs=[VMEM] * len(outs),
        out_shape=[pltpu.VMEM(shape, kind) for shape, kind in outs],
        scratch_shapes=list(scratch),
        compiler_params=PARAMS,
    )(*smem, *[here(array) for array in vmem])


def radices(count):
    digits = []
    stride = 1
    while stride < count:
        radix = 4 if count // stride % 4 == 0 else 2
        digits.append((stride, radix))
        stride *= radix
    return digits


def pairs_at(axis, stride, offset):
    return [(place, place ^ (offset * stride)) for place in range(lax.axis_size(axis))]


def fill_places(offsets_ref, places_ref, first, slab, cell_line, slabs):
    cells, _, slots = offsets_ref.shape
    line = lax.broadcasted_iota(jnp.int32, (8, slots), 0)
    along_z_base = slab.astype(F32)
    for cell in range(cells):
        own = offsets_ref[cell]
        along_x = ((first + cell).astype(F32) + own[0:1]) / cell_line
        along_z = (along_z_base + own[2:3]) / slabs
        full = jnp.where(line == 0, along_x, jnp.where(line == 1, own[1:2], jnp.where(line == 2, along_z, 0.0)))
        high = full.astype(BF16).astype(F32)
        middle = (full - high).astype(BF16).astype(F32)
        low = full - high - middle
        parts = jnp.concatenate([high, middle, low, jnp.zeros_like(low)], axis=0)
        places_ref[:, cell * slots : (cell + 1) * slots] = parts.astype(BF16)


def fill_masked(counts_ref, features_ref, masked_ref):
    cells, slots, channels = features_ref.shape
    slot_ids = lax.broadcasted_iota(jnp.int32, (slots, channels), 0)
    for cell in range(cells):
        kept = jnp.where(slot_ids < counts_ref[cell], features_ref[cell].astype(F32), 0.0)
        masked_ref[cell * slots : (cell + 1) * slots, :] = kept.astype(BF16)


def fill_waves(waves_ref, padded_ref, turned_ref, flips):
    count = waves_ref.shape[1]
    waves = waves_ref[...].astype(F32)
    padded_ref[...] = jnp.zeros_like(padded_ref)
    for part in range(3):
        padded_ref[8 * part : 8 * part + 3, :] = waves
    rows = lax.broadcasted_iota(jnp.int32, (LANES, LANES), 0)
    columns = lax.broadcasted_iota(jnp.int32, (LANES, LANES), 1)
    order = jnp.where((rows ^ (flips & (LANES - 1))) == columns, 1.0, 0.0).astype(BF16)
    for block in range(count // LANES):
        source = pl.multiple_of((block ^ (flips // LANES)) * LANES, LANES)
        taken = padded_ref[:, pl.ds(source, LANES)].astype(BF16)
        turned = lax.dot_general(order, taken, (((1,), (1,)), ((), ())), preferred_element_type=F32)
        turned_ref[block * LANES : (block + 1) * LANES, :] = turned.astype(BF16)


def fill_table(waves, places_ref, table_ref):
    block = waves.shape[0]
    atoms = places_ref.shape[1]
    tile = math.gcd(atoms, 256)
    for start in range(0, atoms, tile):
        span = slice(start, start + tile)
        turns = jnp.dot(waves, places_ref[:, span], preferred_element_type=F32)
        part = turns - jnp.round(turns)
        square = part * part
        sine = part * (SIN[0] + square * (SIN[1] + square * (SIN[2] + square * SIN[3])))
        cosine = COS[0] + square * (COS[1] + square * (COS[2] + square * COS[3]))
        table_ref[:block, span] = (1.0 - sine * sine).astype(BF16)
        table_ref[block:, span] = (sine * cosine).astype(BF16)


def sums_of(table_ref, rows_ref):
    return jnp.dot(table_ref[...], rows_ref[...], preferred_element_type=F32)


def own_kernel(early, block, digits, lengths, counts_ref, features_ref, offsets_ref, waves_ref, *refs):
    masked_ref, places_ref, turned_ref = refs[:3]
    tables, sums = refs[3 : 3 + len(early)], refs[3 + len(early) : 3 + 2 * len(early)]
    padded_ref = refs[-1]
    cells = features_ref.shape[0]
    dev, slab = lax.axis_index("dev"), lax.axis_index("grp")
    flips = jnp.int32(0)
    weight = waves_ref.shape[1]
    for axis, stride, radix in digits:
        weight //= radix
        flips += ((slab if axis == "grp" else dev) // stride % radix) * weight
    fill_waves(waves_ref, padded_ref, turned_ref, flips)
    fill_places(offsets_ref, places_ref, dev * cells, slab, *lengths)
    fill_masked(counts_ref, features_ref, masked_ref)
    for place, table_ref, sums_ref in zip(early, tables, sums):
        fill_table(turned_ref[place * block : (place + 1) * block, :], places_ref, table_ref)
        sums_ref[...] = sums_of(table_ref, masked_ref)


def sibling_kernel(
    place, block, lengths, counts_ref, features_ref, offsets_ref, turned_ref, own_ref, start_ref,
    masked_ref, places_ref, first_ref, last_ref, piece_ref, table_ref,
):
    cells, slots, _ = features_ref.shape
    fill_places(offsets_ref, places_ref, lax.axis_index("dev") * cells, lax.axis_index("grp") ^ 1, *lengths)
    fill_masked(counts_ref, features_ref, masked_ref)
    for line, rows_ref in enumerate((own_ref, masked_ref)):
        first_ref[line] = rows_ref[:slots, :]
        last_ref[line] = rows_ref[(cells - 1) * slots :, :]
    fill_table(turned_ref[place * block : (place + 1) * block, :], places_ref, table_ref)
    piece_ref[...] = (start_ref[...] + sums_of(table_ref, masked_ref)).astype(piece_ref.dtype)


def continued_kernel(place, block, turned_ref, places_ref, masked_ref, start_ref, piece_ref, table_ref):
    fill_table(turned_ref[place * block : (place + 1) * block, :], places_ref, table_ref)
    piece_ref[...] = (start_ref[...] + sums_of(table_ref, masked_ref)).astype(piece_ref.dtype)


def both_kernel(
    place, block, turned_ref, own_places_ref, own_ref, places_ref, masked_ref, kept_ref, piece_ref, table_ref
):
    waves = turned_ref[place * block : (place + 1) * block, :]
    fill_table(waves, own_places_ref, kept_ref)
    total = sums_of(kept_ref, own_ref)
    fill_table(waves, places_ref, table_ref)
    piece_ref[...] = (total + sums_of(table_ref, masked_ref)).astype(piece_ref.dtype)


def rest_kernel(first, block, turned_ref, places_ref, _, *tables):
    for place, table_ref in enumerate(tables):
        start = first + place * block
        fill_table(turned_ref[start : start + block, :], places_ref, table_ref)


def short_kernel(lines, codes_ref, radial_ref, *refs):
    row_refs = refs[:lines]
    before_ref, after_ref, w_ref, _, message_ref, window_ref, starts_ref = refs[lines:]
    cells, slots, channels = message_ref.shape
    pairs = radial_ref.shape[1]
    slab, slabs = lax.axis_index("grp"), lax.axis_size("grp")
    for line in range(lines):
        base = line * (cells + 2)
        window_ref[base] = before_ref[line]
        for cell in range(cells):
            window_ref[base + 1 + cell] = row_refs[line][cell * slots : (cell + 1) * slots, :]
        window_ref[base + 1 + cells] = after_ref[line]
    nothing = lines * (cells + 2)
    window_ref[nothing] = jnp.zeros((slots, channels), BF16)
    for level in range(3):
        line = 0 if level == 1 else 1 if lines == 2 else 1 + level // 2
        inside = (slab + level >= 1) & (slab + level - 1 < slabs)
        for along in range(3):
            starts_ref[3 * level + along] = jnp.where(inside, line * (cells + 2) + along, -1)

    for cell in range(cells):
        total = None
        for pair in range(0, pairs, 2):
            blocks, taken = [], []
            for p in range(pair, min(pair + 2, pairs)):
                start = starts_ref[codes_ref[cell, p]]
                blocks.append(radial_ref[cell, p])
                taken.append(window_ref[jnp.where(start < 0, nothing, start + cell)])
            part = jnp.dot(
                jnp.concatenate(blocks, axis=1), jnp.concatenate(taken, axis=0), preferred_element_type=F32
            )
            total = part if total is None else total + part
        message_ref[cell] = jnp.dot(total.astype(BF16), w_ref[...], preferred_element_type=F32)


def add_kernel(count, radix, *refs):
    pieces, outs = refs[:count], refs[count:]
    total = pieces[0][...].astype(F32)
    for piece in pieces[1:]:
        total = total + piece[...].astype(F32)
    rows = total.shape[1] // radix
    for place, out in enumerate(outs):
        out[...] = total[:, place * rows : (place + 1) * rows].astype(out.dtype)


def add_and_cut(pieces, radix):
    trig, rows, channels = pieces[0].shape
    part = (trig, rows // radix, channels)
    types = [F32] + [BF16] * (radix - 1)
    if part[1] % 16:
        total = functools.reduce(jnp.add, [piece.astype(F32) for piece in pieces])
        return [
            total[:, place * part[1] : (place + 1) * part[1]].astype(kind) for place, kind in enumerate(types)
        ]
    return call(functools.partial(add_kernel, len(pieces), radix), [(part, kind) for kind in types], pieces)


def mixed(owned, waves, w_mix, factor_scale):
    waves = jnp.where(lax.broadcasted_iota(jnp.int32, waves.shape, 1) < 3, waves, 0.0)
    square = jnp.sum(waves * waves, axis=1, keepdims=True)
    kernel = jnp.exp(-square / 128.0) / (1.0 + square / 64.0)
    factors = (owned * factor_scale).astype(BF16)
    energy = jnp.dot(factors, w_mix, preferred_element_type=F32)
    return (energy * jnp.concatenate([kernel, kernel], axis=0)).astype(BF16)


def energy_kernel(count, factor_scale, *refs):
    pieces = refs[:count]
    turned_ref, w_mix_ref, _, energy_ref = refs[count:]
    trig, rows, channels = energy_ref.shape
    total = pieces[0][...].astype(F32)
    for piece in pieces[1:]:
        total = total + piece[...].astype(F32)
    owned = total.reshape(trig * rows, channels)
    energy = mixed(owned, turned_ref[:rows, :].astype(F32), w_mix_ref[...], factor_scale)
    energy_ref[...] = energy.reshape(trig, rows, channels)


def energy_of(pieces, turned, w_mix, factor_scale, after):
    trig, rows, channels = pieces[0].shape
    if rows % 16:
        total = functools.reduce(jnp.add, [piece.astype(F32) for piece in pieces])
        energy = mixed(total.reshape(trig * rows, channels), turned[:rows].astype(F32), w_mix, factor_scale)
        return energy.reshape(trig, rows, channels)
    (energy,) = call(
        functools.partial(energy_kernel, len(pieces), factor_scale),
        [((trig, rows, channels), BF16)],
        [*pieces, turned, w_mix, after],
    )
    return energy


def join_kernel(*refs):
    pieces, out_ref = refs[:-2], refs[-1]
    rows = pieces[0].shape[1]
    for place, piece in enumerate(pieces):
        out_ref[:, place * rows : (place + 1) * rows, :] = piece[...]


def joined(pieces, after):
    trig, rows, channels = pieces[0].shape
    if rows % 16:
        return jnp.concatenate(pieces, axis=1)
    (whole,) = call(join_kernel, [((trig, rows * len(pieces), channels), BF16)], [*pieces, after])
    return whole


def near_kernel(blocks, *refs):
    energies, tables = refs[:blocks], refs[blocks : 2 * blocks]
    out_ref, turned_ref = refs[2 * blocks :]
    for place, energy in enumerate(energies):
        turned_ref[place] = energy[...].astype(F32).T.astype(BF16)
    atoms = out_ref.shape[1]
    tile = math.gcd(atoms, 512)
    for start in range(0, atoms, tile):
        total = None
        for place, table_ref in enumerate(tables):
            part = jnp.dot(turned_ref[place], table_ref[:, start : start + tile], preferred_element_type=F32)
            total = part if total is None else total + part
        out_ref[:, start : start + tile] = total


def final_kernel(blocks, scale, counts_ref, near_ref, message_ref, masked_ref, *refs):
    energies, tables = refs[:blocks], refs[blocks : 2 * blocks]
    out_ref, turned_ref = refs[2 * blocks :]
    cells, slots, channels = out_ref.shape
    step = pl.program_id(0)

    @pl.when(step == 0)
    def _():
        for place, energy in enumerate(energies):
            turned_ref[place] = energy[...].astype(F32).T.astype(BF16)

    atoms = cells * slots
    span = pl.ds(pl.multiple_of(step * atoms, atoms), atoms)
    total = near_ref[:, span]
    for place, table_ref in enumerate(tables):
        total = total + jnp.dot(turned_ref[place], table_ref[:, span], preferred_element_type=F32)
    slot_ids = lax.broadcasted_iota(jnp.int32, (slots, channels), 0)
    for cell in range(cells):
        index = step * cells + cell
        rows = pl.ds(pl.multiple_of(index * slots, slots), slots)
        value = total[:, cell * slots : (cell + 1) * slots].T * scale + message_ref[index]
        value = value * (0.5 + 0.5 * jnp.tanh(0.5 * value))
        result = masked_ref[rows, :].astype(F32) + value
        out_ref[cell] = jnp.where(slot_ids < counts_ref[index], result, 0.0).astype(BF16)


def final_call(counts, near, message, masked, energies, tables, scale):
    cells, slots, channels = message.shape
    rows = tables[0].shape[0]
    blocks = len(tables)
    group = math.gcd(cells, 4)
    operands = [near, message, masked, *energies, *tables]
    return pl.pallas_call(
        functools.partial(final_kernel, blocks, scale),
        grid=(cells // group,),
        in_specs=[SMEM] + [VMEM] * len(operands),
        out_specs=pl.BlockSpec((group, slots, channels), lambda i: (i, 0, 0)),
        out_shape=jax.ShapeDtypeStruct(message.shape, BF16),
        scratch_shapes=[pltpu.VMEM((blocks, channels, rows), BF16)],
        compiler_params=PARAMS,
    )(counts, *[here(array) for array in operands])


def body(features, offsets, radial, neighbours, counts, wavevectors, w_msg, w_mix):
    _, cells, slots, channels = features.shape
    wave_count = wavevectors.shape[1]
    slabs, dev_count = lax.axis_size("grp"), lax.axis_size("dev")
    slab = lax.axis_index("grp")
    cell_line = cells * dev_count
    total_slots = slabs * cell_line * slots
    atoms = cells * slots
    lengths = (float(cell_line), float(slabs))
    features, offsets, counts = features[0], offsets[0], counts[0]

    swap = pairs_at("grp", 1, 1)
    sibling_offsets = lax.ppermute(offsets, "grp", swap)
    if slabs == 2:
        sibling_counts = lax.ppermute(counts, "grp", swap)
        sibling_features = lax.ppermute(features, "grp", swap)
    else:
        up = [(i, i + 1) for i in range(slabs - 1)]
        down = [(j, i) for i, j in up]
        near = [(lax.ppermute(counts, "grp", way), lax.ppermute(features, "grp", way)) for way in (up, down)]
        even = slab % 2 == 0
        sibling_counts = jnp.where(even, near[1][0], near[0][0])
        sibling_features = jnp.where(even, near[1][1], near[0][1])

    stages = [("dev", *digit) for digit in radices(dev_count)]
    stages += [("grp", 2 * stride, radix) for stride, radix in radices(slabs // 2)]
    digits = [("grp", 1, 2)] + stages
    half = wave_count // 2
    axis, stride, blocks = stages[0]
    block = half // blocks
    table = ((2 * block, atoms), BF16)
    sums = ((2 * block, channels), F32)
    piece = ((2 * block, channels), BF16)
    places_type = ((32, atoms), BF16)
    rows_type = ((atoms, channels), BF16)
    edge = ((2, slots, channels), BF16)
    scratch = [pltpu.VMEM(*table)]

    def sent(part, place):
        return lax.ppermute(part.reshape(2, block, channels), axis, pairs_at(axis, stride, place))

    early = list(range(1, blocks))[:2]
    masked, places, turned, *outs = call(
        functools.partial(own_kernel, early, block, digits, lengths),
        [rows_type, places_type, ((wave_count, 32), BF16)] + [table] * len(early) + [sums] * len(early),
        [features, offsets, wavevectors],
        [counts],
        [pltpu.VMEM((32, wave_count), F32)],
    )
    tables = dict(zip(early, outs))
    started = dict(zip(early, outs[len(early) :]))
    sibling, sibling_places, first, last, part = call(
        functools.partial(sibling_kernel, early[0], block, lengths),
        [rows_type, places_type, edge, edge, piece],
        [sibling_features, sibling_offsets, turned, masked, started[early[0]]],
        [sibling_counts],
        scratch,
    )
    received = {early[0]: sent(part, early[0])}
    for place in early[1:]:
        (part,) = call(
            functools.partial(continued_kernel, place, block),
            [piece],
            [turned, sibling_places, sibling, started[place]],
            scratch=scratch,
        )
        received[place] = sent(part, place)
    for place in [*range(1 + len(early), blocks), 0]:
        tables[place], part = call(
            functools.partial(both_kernel, place, block),
            [table, piece if place else sums],
            [turned, places, masked, sibling_places, sibling],
            scratch=scratch,
        )
        if place:
            received[place] = sent(part, place)
    pieces = [part.reshape(2, block, channels)] + [received[place] for place in range(1, blocks)]

    for axis, stride, radix in stages[1:]:
        parts = add_and_cut(pieces, radix)
        pieces = [parts[0]] + [
            lax.ppermute(parts[place], axis, pairs_at(axis, stride, place)) for place in range(1, radix)
        ]

    others = call(
        functools.partial(rest_kernel, half, block), [table] * blocks, [turned, places, parts[0]]
    )
    energy = energy_of(pieces, turned, w_mix, 1.0 / math.sqrt(total_slots), others[0])

    right = [(i, i + 1) for i in range(dev_count - 1)]
    if slabs == 2:
        lines = [masked, sibling]
    else:
        kept = [
            jnp.where(jnp.arange(slots)[None, :, None] < count[:, None, None], cell, jnp.bfloat16(0))
            for count, cell in near
        ]
        first = jnp.stack([masked[:slots]] + [line[0] for line in kept])
        last = jnp.stack([masked[-slots:]] + [line[-1] for line in kept])
        lines = [masked] + [line.reshape(atoms, channels) for line in kept]
    before = lax.ppermute(last, "dev", right)
    after = lax.ppermute(first, "dev", [(j, i) for i, j in right])
    window = (len(lines) * (cells + 2) + 1, slots, channels)
    (message,) = call(
        functools.partial(short_kernel, len(lines)),
        [((cells, slots, channels), F32)],
        [radial[0], *lines, before, after, w_msg, energy],
        [neighbours[0]],
        [pltpu.VMEM(window, BF16), pltpu.SMEM((9,), jnp.int32)],
    )

    for axis, stride, radix in reversed(stages[1:]):
        gathered = [energy] + [
            lax.ppermute(energy, axis, pairs_at(axis, stride, place)) for place in range(1, radix)
        ]
        energy = joined(gathered, message)
    axis, stride, blocks = stages[0]
    energies = [energy] + [
        lax.ppermute(energy, axis, pairs_at(axis, stride, place)) for place in range(1, blocks)
    ]
    others_energies = [lax.ppermute(part, "grp", swap) for part in energies]
    energies = [part.reshape(2 * block, channels) for part in energies]
    others_energies = [part.reshape(2 * block, channels) for part in others_energies]
    turned_energies = [pltpu.VMEM((blocks, channels, 2 * block), BF16)]
    (near_sum,) = call(
        functools.partial(near_kernel, blocks),
        [((channels, atoms), F32)],
        [*energies, *[tables[place] for place in range(blocks)]],
        scratch=turned_energies,
    )
    scale = 8.0 / math.sqrt(wave_count)
    result = final_call(counts, near_sum, message, masked, others_energies, others, scale)
    return result[None]


def solution(mesh):
    in_specs = (
        P("grp", "dev", None, None),
        P("grp", "dev", None, None),
        P("grp", "dev", None, None, None),
        P("grp", "dev", None),
        P("grp", "dev"),
        P(),
        P(),
        P(),
    )
    out_specs = P("grp", "dev", None, None)
    return jax.shard_map(body, mesh=mesh, in_specs=in_specs, out_specs=out_specs, check_vma=False)
```

```python
import functools
import math

import jax
import jax.numpy as jnp
from jax import lax
from jax.experimental import pallas as pl
from jax.experimental.pallas import tpu as pltpu
from jax.sharding import PartitionSpec as P

F32 = jnp.float32
BF16 = jnp.bfloat16
VMEM = pl.BlockSpec(memory_space=pltpu.VMEM)
SMEM = pl.BlockSpec(memory_space=pltpu.SMEM)
HBM = pl.BlockSpec(memory_space=pltpu.HBM)
PARAMS = pltpu.CompilerParams(vmem_limit_bytes=14 * 1024 * 1024)
LANES = 128
COST = 0
SIN = (4.44287957, -7.30781668, 3.59777418, -0.79119939)
COS = (1.41420401, -6.97763732, 5.71518787, -1.72821389)


def call(kernel, outs, operands, scratch=(), held=(), flops=0):
    ahead = len(operands)
    operands = list(operands) + [(VMEM, array) for array in held]

    def without_held(*refs):
        kernel(*refs[:ahead], *refs[len(operands) :])

    return pl.pallas_call(
        without_held,
        in_specs=[place for place, _ in operands],
        out_specs=[place for place, _ in outs],
        out_shape=[place.memory_space(*kind) for place, kind in outs],
        scratch_shapes=list(scratch),
        compiler_params=PARAMS,
        cost_estimate=pl.CostEstimate(flops=flops, bytes_accessed=flops // 300, transcendentals=0),
    )(
        *[
            array if place is SMEM else pltpu.with_memory_space_constraint(array, place.memory_space)
            for place, array in operands
        ]
    )


def in_vmem(arrays):
    return [(VMEM, array) for array in arrays]


def in_hbm(arrays):
    return [(HBM, array) for array in arrays]


def begin(sources, targets, semaphores, first=0):
    copies = [
        pltpu.make_async_copy(source, target, semaphores.at[first + index])
        for index, (source, target) in enumerate(zip(sources, targets))
    ]
    for copy in copies:
        copy.start()
    return copies


def finish(copies):
    for copy in copies:
        copy.wait()


def radices(count):
    digits = []
    stride = 1
    while stride < count:
        radix = 4 if count // stride % 4 == 0 else 2
        digits.append((stride, radix))
        stride *= radix
    return digits


def pairs_at(axis, stride, offset):
    return [(place, place ^ (offset * stride)) for place in range(lax.axis_size(axis))]


def fill_places(offsets_ref, places_ref, first, slab, cell_line, slabs):
    cells, _, slots = offsets_ref.shape
    line = lax.broadcasted_iota(jnp.int32, (8, slots), 0)
    along_z_base = slab.astype(F32)
    for cell in range(cells):
        own = offsets_ref[cell]
        along_x = ((first + cell).astype(F32) + own[0:1]) / cell_line
        along_z = (along_z_base + own[2:3]) / slabs
        full = jnp.where(line == 0, along_x, jnp.where(line == 1, own[1:2], jnp.where(line == 2, along_z, 0.0)))
        high = full.astype(BF16).astype(F32)
        middle = (full - high).astype(BF16).astype(F32)
        low = full - high - middle
        parts = jnp.concatenate([high, middle, low, jnp.zeros_like(low)], axis=0)
        places_ref[:, cell * slots : (cell + 1) * slots] = parts.astype(BF16)


def fill_masked(counts_ref, features_ref, masked_ref):
    cells, slots, channels = features_ref.shape
    slot_ids = lax.broadcasted_iota(jnp.int32, (slots, channels), 0)
    for cell in range(cells):
        kept = jnp.where(slot_ids < counts_ref[cell], features_ref[cell].astype(F32), 0.0)
        masked_ref[cell * slots : (cell + 1) * slots, :] = kept.astype(BF16)


def fill_waves(waves_ref, padded_ref, turned_ref, flips):
    count = waves_ref.shape[1]
    waves = waves_ref[...].astype(F32)
    padded_ref[...] = jnp.zeros_like(padded_ref)
    for part in range(3):
        padded_ref[8 * part : 8 * part + 3, :] = waves
    rows = lax.broadcasted_iota(jnp.int32, (LANES, LANES), 0)
    columns = lax.broadcasted_iota(jnp.int32, (LANES, LANES), 1)
    order = jnp.where((rows ^ (flips & (LANES - 1))) == columns, 1.0, 0.0).astype(BF16)
    for block in range(count // LANES):
        source = pl.multiple_of((block ^ (flips // LANES)) * LANES, LANES)
        taken = padded_ref[:, pl.ds(source, LANES)].astype(BF16)
        turned = lax.dot_general(order, taken, (((1,), (1,)), ((), ())), preferred_element_type=F32)
        turned_ref[block * LANES : (block + 1) * LANES, :] = turned.astype(BF16)


def fill_table(waves, places_ref, table_ref):
    block = waves.shape[0]
    atoms = places_ref.shape[1]
    tile = math.gcd(atoms, 256)
    for start in range(0, atoms, tile):
        span = slice(start, start + tile)
        turns = jnp.dot(waves, places_ref[:, span], preferred_element_type=F32)
        part = turns - jnp.round(turns)
        square = part * part
        sine = part * (SIN[0] + square * (SIN[1] + square * (SIN[2] + square * SIN[3])))
        cosine = COS[0] + square * (COS[1] + square * (COS[2] + square * COS[3]))
        table_ref[:block, span] = (1.0 - sine * sine).astype(BF16)
        table_ref[block:, span] = (sine * cosine).astype(BF16)


def sums_of(table_ref, rows_ref):
    return jnp.dot(table_ref[...], rows_ref[...], preferred_element_type=F32)


def own_kernel(early, block, digits, lengths, *refs):
    sources, refs = refs[:4], refs[4:]
    masked_ref, places_ref, turned_ref = refs[:3]
    tables, sums = refs[3 : 3 + len(early)], refs[3 + len(early) : 3 + 2 * len(early)]
    padded_ref, waves_ref, offsets_ref, counts_ref, features_ref, kept_ref, semaphores, kept_semaphores = refs[
        3 + 2 * len(early) :
    ]
    copies = begin(sources, (waves_ref, offsets_ref, counts_ref, features_ref), semaphores)
    cells = features_ref.shape[0]
    dev, slab = lax.axis_index("dev"), lax.axis_index("grp")
    flips = jnp.int32(0)
    weight = waves_ref.shape[1]
    for axis, stride, radix in digits:
        weight //= radix
        flips += ((slab if axis == "grp" else dev) // stride % radix) * weight
    copies[0].wait()
    fill_waves(waves_ref, padded_ref, turned_ref, flips)
    copies[1].wait()
    fill_places(offsets_ref, places_ref, dev * cells, slab, *lengths)
    copies[2].wait()
    copies[3].wait()
    fill_masked(counts_ref, features_ref, masked_ref)
    leaving = []
    for index, (place, sums_ref) in enumerate(zip(early, sums)):
        table_ref = kept_ref.at[index]
        fill_table(turned_ref[place * block : (place + 1) * block, :], places_ref, table_ref)
        leaving += begin([table_ref], [tables[index]], kept_semaphores, index)
        sums_ref[...] = sums_of(table_ref, masked_ref)
    finish(leaving)


def sibling_kernel(
    place, block, lengths, counts_ref, features_ref, offsets_ref, turned_ref, start_ref,
    masked_ref, places_ref, piece_ref, table_ref,
):
    cells = features_ref.shape[0]
    fill_places(offsets_ref, places_ref, lax.axis_index("dev") * cells, lax.axis_index("grp") ^ 1, *lengths)
    fill_masked(counts_ref, features_ref, masked_ref)
    fill_table(turned_ref[place * block : (place + 1) * block, :], places_ref, table_ref)
    piece_ref[...] = (start_ref[...] + sums_of(table_ref, masked_ref)).astype(piece_ref.dtype)


def continued_kernel(place, block, turned_ref, places_ref, masked_ref, start_ref, piece_ref, table_ref):
    fill_table(turned_ref[place * block : (place + 1) * block, :], places_ref, table_ref)
    piece_ref[...] = (start_ref[...] + sums_of(table_ref, masked_ref)).astype(piece_ref.dtype)


def both_kernel(
    place, block, turned_ref, own_places_ref, own_ref, places_ref, masked_ref, kept_ref, piece_ref, table_ref, semaphores
):
    waves = turned_ref[place * block : (place + 1) * block, :]
    fill_table(waves, own_places_ref, table_ref.at[0])
    leaving = begin([table_ref.at[0]], [kept_ref], semaphores)
    total = sums_of(table_ref.at[0], own_ref)
    fill_table(waves, places_ref, table_ref.at[1])
    piece_ref[...] = (total + sums_of(table_ref.at[1], masked_ref)).astype(piece_ref.dtype)
    finish(leaving)


def rest_kernel(first, block, turned_ref, places_ref, mark_ref, *refs):
    *tables, table_ref, semaphores = refs
    mark_ref[...] = jnp.zeros_like(mark_ref)
    leaving = []
    for place, target_ref in enumerate(tables):
        start = first + place * block
        fill_table(turned_ref[start : start + block, :], places_ref, table_ref.at[place])
        leaving += begin([table_ref.at[place]], [target_ref], semaphores, place)
    finish(leaving)


def fill_edges(lines, outs):
    slots = outs[0].shape[1]
    end = lines[0].shape[0] - slots
    if len(outs) == 1:
        start = pl.multiple_of(jnp.where(lax.axis_index("grp") == 0, end, 0), slots)
        for line, rows_ref in enumerate(lines):
            outs[0][line] = rows_ref[pl.ds(start, slots), :]
        return
    for line, rows_ref in enumerate(lines):
        outs[0][line] = rows_ref[end:, :]
        outs[1][line] = rows_ref[:slots, :]


def short_kernel(lines, chunks, codes_ref, source_ref, *refs):
    line_refs, refs = refs[:lines], refs[lines:]
    one_ref, two_ref, w_ref, message_ref = refs[:4]
    window_ref, starts_ref, radial_ref, semaphores = refs[4:]
    cells, slots, channels = message_ref.shape
    pairs = radial_ref.shape[1]
    slab, slabs = lax.axis_index("grp"), lax.axis_size("grp")
    share = cells // chunks
    edges = []
    for line in range(lines):
        if slabs == 2:
            near = slab * (cells + 1)
            edges.append((one_ref.at[line], window_ref.at[line * (cells + 2) + near]))
            edges.append((two_ref.at[line], window_ref.at[(1 - line) * (cells + 2) + cells + 1 - near]))
        else:
            edges.append((one_ref.at[line], window_ref.at[line * (cells + 2)]))
            edges.append((two_ref.at[line], window_ref.at[line * (cells + 2) + cells + 1]))
    edges = begin(*zip(*edges), semaphores)
    parts = []
    for chunk in range(chunks):
        span = pl.ds(chunk * share, share)
        moves = [(source_ref.at[span], radial_ref.at[span])]
        for line, line_ref in enumerate(line_refs):
            moves.append((line_ref.at[span], window_ref.at[pl.ds(line * (cells + 2) + 1 + chunk * share, share)]))
        parts.append(begin(*zip(*moves), semaphores, 2 * lines + chunk * (1 + lines)))
    nothing = lines * (cells + 2)
    window_ref[nothing] = jnp.zeros((slots, channels), BF16)
    for level in range(3):
        line = 0 if level == 1 else 1 if lines == 2 else 1 + level // 2
        inside = (slab + level >= 1) & (slab + level - 1 < slabs)
        for along in range(3):
            starts_ref[3 * level + along] = jnp.where(inside, line * (cells + 2) + along, -1)

    for cell in range(cells):
        if cell == 0:
            finish(edges)
            finish(parts[0])
        if cell % share == 0 and cell // share + 1 < chunks:
            finish(parts[cell // share + 1])
        total = None
        for pair in range(0, pairs, 2):
            blocks, taken = [], []
            for p in range(pair, min(pair + 2, pairs)):
                start = starts_ref[codes_ref[cell, p]]
                blocks.append(radial_ref[cell, p])
                taken.append(window_ref[jnp.where(start < 0, nothing, start + cell)])
            part = jnp.dot(
                jnp.concatenate(blocks, axis=1), jnp.concatenate(taken, axis=0), preferred_element_type=F32
            )
            total = part if total is None else total + part
        message_ref[cell] = jnp.dot(total.astype(BF16), w_ref[...], preferred_element_type=F32)


def add_kernel(count, radix, *refs):
    pieces, outs = refs[:count], refs[count:]
    total = pieces[0][...].astype(F32)
    for piece in pieces[1:]:
        total = total + piece[...].astype(F32)
    rows = total.shape[1] // radix
    for place, out in enumerate(outs):
        out[...] = total[:, place * rows : (place + 1) * rows].astype(out.dtype)


def add_and_cut(pieces, radix, held):
    trig, rows, channels = pieces[0].shape
    part = (trig, rows // radix, channels)
    types = [F32] + [BF16] * (radix - 1)
    if part[1] % 16:
        total = functools.reduce(jnp.add, [piece.astype(F32) for piece in pieces])
        return [
            total[:, place * part[1] : (place + 1) * part[1]].astype(kind) for place, kind in enumerate(types)
        ]
    kernel = functools.partial(add_kernel, len(pieces), radix)
    return call(kernel, [(VMEM, (part, kind)) for kind in types], in_vmem(pieces), held=held)


def mixed(owned, waves, w_mix, factor_scale):
    waves = jnp.where(lax.broadcasted_iota(jnp.int32, waves.shape, 1) < 3, waves, 0.0)
    square = jnp.sum(waves * waves, axis=1, keepdims=True)
    kernel = jnp.exp(-square / 128.0) / (1.0 + square / 64.0)
    factors = (owned * factor_scale).astype(BF16)
    energy = jnp.dot(factors, w_mix, preferred_element_type=F32)
    return (energy * jnp.concatenate([kernel, kernel], axis=0)).astype(BF16)


def energy_kernel(count, lines, factor_scale, *refs):
    pieces = refs[:count]
    turned_ref, w_mix_ref = refs[count : count + 2]
    energy_ref, *edges = refs[count + 2 + lines :]
    if edges:
        fill_edges(refs[count + 2 : count + 2 + lines], edges)
    trig, rows, channels = energy_ref.shape
    total = pieces[0][...].astype(F32)
    for piece in pieces[1:]:
        total = total + piece[...].astype(F32)
    owned = total.reshape(trig * rows, channels)
    energy = mixed(owned, turned_ref[:rows, :].astype(F32), w_mix_ref[...], factor_scale)
    energy_ref[...] = energy.reshape(trig, rows, channels)


def energy_of(pieces, turned, w_mix, factor_scale, lines, slots, held):
    trig, rows, channels = pieces[0].shape
    if rows % 16:
        total = functools.reduce(jnp.add, [piece.astype(F32) for piece in pieces])
        energy = mixed(total.reshape(trig * rows, channels), turned[:rows].astype(F32), w_mix, factor_scale)
        edges = [jnp.stack([line[-slots:] for line in lines]), jnp.stack([line[:slots] for line in lines])]
        return energy.reshape(trig, rows, channels), edges
    edge = (VMEM, ((len(lines), slots, channels), BF16))
    energy, *edges = call(
        functools.partial(energy_kernel, len(pieces), len(lines), factor_scale),
        [(VMEM, ((trig, rows, channels), BF16))] + [edge] * (1 if lax.axis_size("grp") == 2 else 2),
        in_vmem([*pieces, turned, w_mix, *lines]),
        held=held,
    )
    return energy, edges


def join_kernel(*refs):
    pieces, out_ref = refs[:-1], refs[-1]
    rows = pieces[0].shape[1]
    for place, piece in enumerate(pieces):
        out_ref[:, place * rows : (place + 1) * rows, :] = piece[...]


def joined(pieces, held):
    trig, rows, channels = pieces[0].shape
    if rows % 16:
        return jnp.concatenate(pieces, axis=1)
    whole = (VMEM, ((trig, rows * len(pieces), channels), BF16))
    (whole,) = call(join_kernel, [whole], in_vmem(pieces), held=held)
    return whole


def near_kernel(blocks, *refs):
    energies, tables, (out_ref, turned_ref) = refs[:blocks], refs[blocks : 2 * blocks], refs[2 * blocks :]
    for place, energy in enumerate(energies):
        turned_ref[place] = energy[...].astype(F32).T.astype(BF16)
    atoms = out_ref.shape[1]
    tile = math.gcd(atoms, 512)
    for start in range(0, atoms, tile):
        total = None
        for place, table_ref in enumerate(tables):
            part = jnp.dot(turned_ref[place], table_ref[:, start : start + tile], preferred_element_type=F32)
            total = part if total is None else total + part
        out_ref[:, start : start + tile] = total


def final_kernel(scale, counts_ref, masked_ref, near_ref, message_ref, energy_ref, rest_ref, *refs):
    tables, (out_ref, turned_ref) = refs[:-2], refs[-2:]
    cells, slots, channels = out_ref.shape
    step = pl.program_id(0)

    @pl.when(step == 0)
    def _():
        rows = energy_ref.shape[0]
        half = rows // 2
        turned_ref[0] = energy_ref[...].astype(F32).T.astype(BF16)
        for place in range(1, len(tables)):
            taken = rest_ref[:, (place - 1) * half : place * half, :].reshape(rows, channels)
            turned_ref[place] = taken.astype(F32).T.astype(BF16)

    atoms = cells * slots
    span = pl.ds(pl.multiple_of(step * atoms, atoms), atoms)
    total = near_ref[:, span]
    for place, table_ref in enumerate(tables):
        total = total + jnp.dot(turned_ref[place], table_ref[:, span], preferred_element_type=F32)
    slot_ids = lax.broadcasted_iota(jnp.int32, (slots, channels), 0)
    for cell in range(cells):
        index = step * cells + cell
        value = total[:, cell * slots : (cell + 1) * slots].T * scale + message_ref[index]
        value = value * (0.5 + 0.5 * jnp.tanh(0.5 * value))
        result = masked_ref[index].astype(F32) + value
        out_ref[cell] = jnp.where(slot_ids < counts_ref[index], result, 0.0).astype(BF16)


def final_call(counts, near, message, masked, energy, rest, tables, scale):
    cells, slots, channels = message.shape
    rows = tables[0].shape[0]
    blocks = len(tables)
    group = math.gcd(cells, 4)
    cells_spec = pl.BlockSpec((group, slots, channels), lambda i: (i, 0, 0))
    operands = [masked, near, message, energy, rest, *tables]
    return pl.pallas_call(
        functools.partial(final_kernel, scale),
        grid=(cells // group,),
        in_specs=[SMEM] + [VMEM] * len(operands),
        out_specs=cells_spec,
        out_shape=jax.ShapeDtypeStruct(message.shape, BF16),
        scratch_shapes=[pltpu.VMEM((blocks, channels, rows), BF16)],
        compiler_params=PARAMS,
    )(counts, *[pltpu.with_memory_space_constraint(array, pltpu.VMEM) for array in operands])


def body(features, offsets, radial, neighbours, counts, wavevectors, w_msg, w_mix):
    _, cells, slots, channels = features.shape
    wave_count = wavevectors.shape[1]
    slabs, dev_count = lax.axis_size("grp"), lax.axis_size("dev")
    slab = lax.axis_index("grp")
    cell_line = cells * dev_count
    total_slots = slabs * cell_line * slots
    atoms = cells * slots
    lengths = (float(cell_line), float(slabs))
    features, offsets, counts = features[0], offsets[0], counts[0]

    swap = pairs_at("grp", 1, 1)
    sibling_offsets = lax.ppermute(offsets, "grp", swap)
    if slabs == 2:
        sibling_counts = lax.ppermute(counts, "grp", swap)
        sibling_features = lax.ppermute(features, "grp", swap)
    else:
        up = [(i, i + 1) for i in range(slabs - 1)]
        down = [(j, i) for i, j in up]
        near = [(lax.ppermute(counts, "grp", way), lax.ppermute(features, "grp", way)) for way in (up, down)]
        even = slab % 2 == 0
        sibling_counts = jnp.where(even, near[1][0], near[0][0])
        sibling_features = jnp.where(even, near[1][1], near[0][1])

    stages = [("dev", *digit) for digit in radices(dev_count)]
    stages += [("grp", 2 * stride, radix) for stride, radix in radices(slabs // 2)]
    digits = [("grp", 1, 2)] + stages
    half = wave_count // 2
    axis, stride, blocks = stages[0]
    block = half // blocks
    table = ((2 * block, atoms), BF16)
    sums = ((2 * block, channels), F32)
    piece = ((2 * block, channels), BF16)
    places_type = ((32, atoms), BF16)
    rows_type = ((atoms, channels), BF16)
    edge = ((2, slots, channels), BF16)
    scratch = [pltpu.VMEM(*table)]
    block_flops = 2 * 2 * block * atoms * channels * COST

    def several(count):
        return [pltpu.VMEM((count,) + table[0], BF16), pltpu.SemaphoreType.DMA((count,))]

    def sent(part, place):
        return lax.ppermute(part.reshape(2, block, channels), axis, pairs_at(axis, stride, place))

    order = [*range(blocks - 1, 0, -1), 0]
    early = order[: min(2, blocks - 1)]
    masked, places, turned, *outs = call(
        functools.partial(own_kernel, early, block, digits, lengths),
        [(VMEM, rows_type), (VMEM, places_type), (VMEM, ((wave_count, 32), BF16))]
        + [(HBM, table)] * len(early)
        + [(VMEM, sums)] * len(early),
        in_hbm([wavevectors, offsets, counts, features]),
        [
            pltpu.VMEM((32, wave_count), F32),
            pltpu.VMEM(wavevectors.shape, jnp.int32),
            pltpu.VMEM(offsets.shape, F32),
            pltpu.SMEM(counts.shape, jnp.int32),
            pltpu.VMEM(features.shape, BF16),
            pltpu.VMEM((len(early),) + table[0], BF16),
            pltpu.SemaphoreType.DMA((4,)),
            pltpu.SemaphoreType.DMA((len(early),)),
        ],
    )
    tables = dict(zip(early, outs))
    started = dict(zip(early, outs[len(early) :]))
    sibling, sibling_places, part = call(
        functools.partial(sibling_kernel, early[0], block, lengths),
        [(VMEM, rows_type), (VMEM, places_type), (VMEM, piece)],
        [(SMEM, sibling_counts)] + in_vmem([sibling_features, sibling_offsets, turned, started[early[0]]]),
        scratch,
    )
    received = {early[0]: sent(part, early[0])}
    for place in early[1:]:
        (part,) = call(
            functools.partial(continued_kernel, place, block),
            [(VMEM, piece)],
            in_vmem([turned, sibling_places, sibling, started[place]]),
            scratch,
            flops=block_flops,
        )
        received[place] = sent(part, place)
    for place in order[len(early) :]:
        tables[place], part = call(
            functools.partial(both_kernel, place, block),
            [(HBM, table), (VMEM, piece if place else sums)],
            in_vmem([turned, places, masked, sibling_places, sibling]),
            [pltpu.VMEM((2,) + table[0], BF16), pltpu.SemaphoreType.DMA((1,))],
            [part] if place else [],
            2 * block_flops,
        )
        if place:
            received[place] = sent(part, place)
    pieces = [part.reshape(2, block, channels)] + [received[place] for place in range(1, blocks)]
    tables = [tables[place] for place in range(blocks)]

    def rest_of_tables(first, count, held):
        return call(
            functools.partial(rest_kernel, half + first * block, block),
            [(VMEM, ((8, LANES), F32))] + [(HBM, table)] * count,
            in_vmem([turned, places]),
            several(count),
            held,
            block_flops * count,
        )

    share = blocks // 2
    mark, *others = rest_of_tables(0, share, [part])

    for axis, stride, radix in stages[1:]:
        parts = add_and_cut(pieces, radix, [mark])
        pieces = [parts[0]] + [
            lax.ppermute(parts[place], axis, pairs_at(axis, stride, place)) for place in range(1, radix)
        ]

    mark, *more = rest_of_tables(share, blocks - share, [parts[0]])
    others += more

    if slabs == 2:
        lines = [masked, sibling]
    else:
        lines = [masked] + [
            jnp.where(jnp.arange(slots)[None, :, None] < count[:, None, None], cell, jnp.bfloat16(0)).reshape(
                atoms, channels
            )
            for count, cell in near
        ]
    energy, edges = energy_of(pieces, turned, w_mix, 1.0 / math.sqrt(total_slots), lines, slots, [mark])

    right = [(i, i + 1) for i in range(dev_count - 1)]
    left = [(j, i) for i, j in right]
    if slabs == 2:
        ways = right + [(dev_count + i, dev_count + j) for i, j in left]
        one = lax.ppermute(edges[0], ("grp", "dev"), ways)
        two = lax.ppermute(one, "grp", swap)
    else:
        one = lax.ppermute(edges[0], "dev", right)
        two = lax.ppermute(edges[1], "dev", left)

    for axis, stride, radix in reversed(stages[1:]):
        energy = joined(
            [energy] + [lax.ppermute(energy, axis, pairs_at(axis, stride, place)) for place in range(1, radix)],
            [],
        )
    axis, stride, blocks = stages[0]
    energies = [energy] + [
        lax.ppermute(energy, axis, pairs_at(axis, stride, place)) for place in range(1, blocks)
    ]
    other_energy = lax.ppermute(energy, "grp", swap)

    chunks = math.gcd(cells, 4)
    (message,) = call(
        functools.partial(short_kernel, len(lines), chunks),
        [(VMEM, ((cells, slots, channels), F32))],
        [(SMEM, neighbours[0])]
        + in_hbm([radial[0], *[line.reshape(cells, slots, channels) for line in lines], one, two])
        + in_vmem([w_msg]),
        [
            pltpu.VMEM((len(lines) * (cells + 2) + 1, slots, channels), BF16),
            pltpu.SMEM((9,), jnp.int32),
            pltpu.VMEM(radial.shape[1:], BF16),
            pltpu.SemaphoreType.DMA((2 * len(lines) + chunks * (1 + len(lines)),)),
        ],
        [energy, other_energy],
        6 * block_flops,
    )
    rest = lax.ppermute(joined(energies[1:], [message]), "grp", swap)
    energies = [part.reshape(2 * block, channels) for part in energies]
    other_energy = other_energy.reshape(2 * block, channels)
    (near_sum,) = call(
        functools.partial(near_kernel, blocks),
        [(VMEM, ((channels, atoms), F32))],
        in_vmem([*energies, *tables]),
        [pltpu.VMEM((blocks, channels, 2 * block), BF16)],
        [message],
        2 * block_flops,
    )
    masked = masked.reshape(cells, slots, channels)
    scale = 8.0 / math.sqrt(wave_count)
    result = final_call(counts, near_sum, message, masked, other_energy, rest, others, scale)
    return result[None]


def solution(mesh):
    in_specs = (
        P("grp", "dev", None, None),
        P("grp", "dev", None, None),
        P("grp", "dev", None, None, None),
        P("grp", "dev", None),
        P("grp", "dev"),
        P(),
        P(),
        P(),
    )
    out_specs = P("grp", "dev", None, None)
    return jax.shard_map(body, mesh=mesh, in_specs=in_specs, out_specs=out_specs, check_vma=False)
```

```python
import functools
import math

import jax
import jax.numpy as jnp
from jax import lax
from jax.experimental import pallas as pl
from jax.experimental.pallas import tpu as pltpu
from jax.sharding import PartitionSpec as P

F32 = jnp.float32
BF16 = jnp.bfloat16
VMEM = pl.BlockSpec(memory_space=pltpu.VMEM)
SMEM = pl.BlockSpec(memory_space=pltpu.SMEM)
HBM = pl.BlockSpec(memory_space=pltpu.HBM)
PARAMS = pltpu.CompilerParams(vmem_limit_bytes=14 * 1024 * 1024)
LANES = 128
COST = 0
SIN = (4.44287957, -7.30781668, 3.59777418, -0.79119939)
COS = (1.41420401, -6.97763732, 5.71518787, -1.72821389)


def call(kernel, outs, operands, scratch=(), held=(), flops=0, same=()):
    ahead = len(operands)
    operands = list(operands) + [(VMEM, array) for array in held]

    def without_held(*refs):
        kernel(*refs[:ahead], *refs[len(operands) :])

    return pl.pallas_call(
        without_held,
        in_specs=[place for place, _ in operands],
        out_specs=[place for place, _ in outs],
        out_shape=[place.memory_space(*kind) for place, kind in outs],
        scratch_shapes=list(scratch),
        input_output_aliases=dict(same),
        compiler_params=PARAMS,
        cost_estimate=pl.CostEstimate(flops=flops, bytes_accessed=flops // 300, transcendentals=0),
    )(
        *[
            array if place is SMEM else pltpu.with_memory_space_constraint(array, place.memory_space)
            for place, array in operands
        ]
    )


def in_vmem(arrays):
    return [(VMEM, array) for array in arrays]


def in_hbm(arrays):
    return [(HBM, array) for array in arrays]


def begin(sources, targets, semaphores, first=0):
    copies = [
        pltpu.make_async_copy(source, target, semaphores.at[first + index])
        for index, (source, target) in enumerate(zip(sources, targets))
    ]
    for copy in copies:
        copy.start()
    return copies


def finish(copies):
    for copy in copies:
        copy.wait()


def radices(count):
    digits = []
    stride = 1
    while stride < count:
        radix = 4 if count // stride % 4 == 0 else 2
        digits.append((stride, radix))
        stride *= radix
    return digits


def pairs_at(axis, stride, offset):
    return [(place, place ^ (offset * stride)) for place in range(lax.axis_size(axis))]


def fill_places(offsets_ref, places_ref, first, slab, cell_line, slabs):
    _, cells, slots = offsets_ref.shape
    line = lax.broadcasted_iota(jnp.int32, (8, slots), 0)
    along_z_base = slab.astype(F32)
    for cell in range(cells):
        along_x = ((first + cell).astype(F32) + offsets_ref[0, cell : cell + 1]) / cell_line
        along_y = offsets_ref[1, cell : cell + 1]
        along_z = (along_z_base + offsets_ref[2, cell : cell + 1]) / slabs
        full = jnp.where(line == 0, along_x, jnp.where(line == 1, along_y, jnp.where(line == 2, along_z, 0.0)))
        high = full.astype(BF16).astype(F32)
        middle = (full - high).astype(BF16).astype(F32)
        low = full - high - middle
        parts = jnp.concatenate([high, middle, low, jnp.zeros_like(low)], axis=0)
        places_ref[:, cell * slots : (cell + 1) * slots] = parts.astype(BF16)


def fill_masked(counts_ref, features_ref, masked_ref):
    cells, slots, channels = features_ref.shape
    slot_ids = lax.broadcasted_iota(jnp.int32, (slots, channels), 0)
    for cell in range(cells):
        kept = jnp.where(slot_ids < counts_ref[cell], features_ref[cell].astype(F32), 0.0)
        masked_ref[cell * slots : (cell + 1) * slots, :] = kept.astype(BF16)


def fill_waves(waves_ref, padded_ref, turned_ref, flips):
    count = waves_ref.shape[1]
    waves = waves_ref[...].astype(F32)
    padded_ref[...] = jnp.zeros_like(padded_ref)
    for part in range(3):
        padded_ref[8 * part : 8 * part + 3, :] = waves
    rows = lax.broadcasted_iota(jnp.int32, (LANES, LANES), 0)
    columns = lax.broadcasted_iota(jnp.int32, (LANES, LANES), 1)
    order = jnp.where((rows ^ (flips & (LANES - 1))) == columns, 1.0, 0.0).astype(BF16)
    for block in range(count // LANES):
        source = pl.multiple_of((block ^ (flips // LANES)) * LANES, LANES)
        taken = padded_ref[:, pl.ds(source, LANES)].astype(BF16)
        turned = lax.dot_general(order, taken, (((1,), (1,)), ((), ())), preferred_element_type=F32)
        turned_ref[block * LANES : (block + 1) * LANES, :] = turned.astype(BF16)


def fill_table(waves, places_ref, table_ref):
    block = waves.shape[0]
    atoms = places_ref.shape[1]
    tile = math.gcd(atoms, 256)
    for start in range(0, atoms, tile):
        span = slice(start, start + tile)
        turns = jnp.dot(waves, places_ref[:, span], preferred_element_type=F32)
        part = turns - jnp.round(turns)
        square = part * part
        sine = part * (SIN[0] + square * (SIN[1] + square * (SIN[2] + square * SIN[3])))
        cosine = COS[0] + square * (COS[1] + square * (COS[2] + square * COS[3]))
        table_ref[:block, span] = (1.0 - sine * sine).astype(BF16)
        table_ref[block:, span] = (sine * cosine).astype(BF16)


def sums_of(table_ref, rows_ref):
    return jnp.dot(table_ref[...], rows_ref[...], preferred_element_type=F32)


def own_kernel(early, block, digits, lengths, *refs):
    sources, refs = refs[:4], refs[4:]
    masked_ref, places_ref, turned_ref, table_ref = refs[:4]
    sums = refs[4 : 4 + len(early)]
    padded_ref, waves_ref, offsets_ref, counts_ref, features_ref, semaphores = refs[4 + len(early) :]
    copies = begin(sources, (waves_ref, offsets_ref, counts_ref, features_ref), semaphores)
    cells = features_ref.shape[0]
    dev, slab = lax.axis_index("dev"), lax.axis_index("grp")
    flips = jnp.int32(0)
    weight = waves_ref.shape[1]
    for axis, stride, radix in digits:
        weight //= radix
        flips += ((slab if axis == "grp" else dev) // stride % radix) * weight
    copies[0].wait()
    fill_waves(waves_ref, padded_ref, turned_ref, flips)
    copies[1].wait()
    fill_places(offsets_ref, places_ref, dev * cells, slab, *lengths)
    copies[2].wait()
    copies[3].wait()
    fill_masked(counts_ref, features_ref, masked_ref)
    for place, sums_ref in zip(early, sums):
        fill_table(turned_ref[place * block : (place + 1) * block, :], places_ref, table_ref.at[place])
        sums_ref[...] = sums_of(table_ref.at[place], masked_ref)


def sibling_kernel(
    place, block, lengths, counts_ref, features_ref, offsets_ref, turned_ref, start_ref,
    masked_ref, places_ref, piece_ref, table_ref,
):
    cells = features_ref.shape[0]
    fill_places(offsets_ref, places_ref, lax.axis_index("dev") * cells, lax.axis_index("grp") ^ 1, *lengths)
    fill_masked(counts_ref, features_ref, masked_ref)
    fill_table(turned_ref[place * block : (place + 1) * block, :], places_ref, table_ref)
    piece_ref[...] = (start_ref[...] + sums_of(table_ref, masked_ref)).astype(piece_ref.dtype)


def continued_kernel(place, block, turned_ref, places_ref, masked_ref, start_ref, piece_ref, table_ref):
    fill_table(turned_ref[place * block : (place + 1) * block, :], places_ref, table_ref)
    piece_ref[...] = (start_ref[...] + sums_of(table_ref, masked_ref)).astype(piece_ref.dtype)


def both_kernel(
    place, block, turned_ref, own_places_ref, own_ref, places_ref, masked_ref, _, kept_ref, piece_ref, table_ref
):
    waves = turned_ref[place * block : (place + 1) * block, :]
    fill_table(waves, own_places_ref, kept_ref.at[place])
    total = sums_of(kept_ref.at[place], own_ref)
    fill_table(waves, places_ref, table_ref)
    piece_ref[...] = (total + sums_of(table_ref, masked_ref)).astype(piece_ref.dtype)


def fill_edges(lines, outs):
    slots = outs[0].shape[1]
    end = lines[0].shape[0] - slots
    if len(outs) == 1:
        start = pl.multiple_of(jnp.where(lax.axis_index("grp") == 0, end, 0), slots)
        for line, rows_ref in enumerate(lines):
            outs[0][line] = rows_ref[pl.ds(start, slots), :]
        return
    for line, rows_ref in enumerate(lines):
        outs[0][line] = rows_ref[end:, :]
        outs[1][line] = rows_ref[:slots, :]


def rest_kernel(blocks, block, lines, turned_ref, places_ref, _, *refs):
    kept_ref, *edges = refs[lines:]
    if edges:
        fill_edges(refs[:lines], edges)
    for place in blocks:
        fill_table(turned_ref[place * block : (place + 1) * block, :], places_ref, kept_ref.at[place])


def short_kernel(lines, chunks, codes_ref, source_ref, *refs):
    line_refs, refs = refs[:lines], refs[lines:]
    one_ref, two_ref, w_ref, message_ref = refs[:4]
    window_ref, found_ref, radial_ref, semaphores = refs[4:]
    cells, slots, channels = message_ref.shape
    pairs = codes_ref.shape[0]
    slab, slabs = lax.axis_index("grp"), lax.axis_size("grp")
    share = cells // chunks
    edges = []
    for line in range(lines):
        if slabs == 2:
            near = slab * (cells + 1)
            edges.append((one_ref.at[line], window_ref.at[line * (cells + 2) + near]))
            edges.append((two_ref.at[line], window_ref.at[(1 - line) * (cells + 2) + cells + 1 - near]))
        else:
            edges.append((one_ref.at[line], window_ref.at[line * (cells + 2)]))
            edges.append((two_ref.at[line], window_ref.at[line * (cells + 2) + cells + 1]))
    edges = begin(*zip(*edges), semaphores)
    parts = []
    for chunk in range(chunks):
        span = pl.ds(chunk * share * pairs, share * pairs)
        moves = [(source_ref.at[span], radial_ref.at[span])]
        for line, line_ref in enumerate(line_refs):
            base = line * (cells + 2) + 1 + chunk * share
            moves.append((line_ref.at[pl.ds(chunk * share, share)], window_ref.at[pl.ds(base, share)]))
        parts.append(begin(*zip(*moves), semaphores, 2 * lines + chunk * (1 + lines)))
    nothing = cells * pairs
    radial_ref[nothing] = jnp.zeros((slots, slots), BF16)
    for cell in range(cells):
        for code in range(9):
            found_ref[9 * cell + code] = nothing
        for pair in range(pairs):
            found_ref[9 * cell + codes_ref[pair, cell]] = cell * pairs + pair
    levels = [1, 2 - 2 * slab] if slabs == 2 else [1, 0, 2]
    finish(edges)
    ready = 0
    carried = None
    for start in range(0, cells + 2, 2):
        takers = [cell for cell in range(start - 2, start + 2) if 0 <= cell < cells]
        while ready <= takers[-1] // share:
            finish(parts[ready])
            ready += 1
        total = None
        for line, level in enumerate(levels):
            rows = []
            for cell in takers:
                halves = []
                for place in (start, start + 1):
                    along = place - cell
                    index = found_ref[9 * cell + 3 * level + along] if 0 <= along < 3 else nothing
                    halves.append(radial_ref[index])
                rows.append(jnp.concatenate(halves, axis=1))
            base = line * (cells + 2) + start
            taken = window_ref[base : base + 2].reshape(2 * slots, channels)
            part = jnp.dot(jnp.concatenate(rows, axis=0), taken, preferred_element_type=F32)
            total = part if total is None else total + part
        if start:
            gathered = (carried + total[: 2 * slots]).astype(BF16)
            message = jnp.dot(gathered, w_ref[...], preferred_element_type=F32)
            message_ref[start - 2 : start] = message.reshape(2, slots, channels)
            total = total[2 * slots :]
        carried = total


def add_kernel(count, radix, *refs):
    pieces, outs = refs[:count], refs[count:]
    total = pieces[0][...].astype(F32)
    for piece in pieces[1:]:
        total = total + piece[...].astype(F32)
    rows = total.shape[1] // radix
    for place, out in enumerate(outs):
        out[...] = total[:, place * rows : (place + 1) * rows].astype(out.dtype)


def add_and_cut(pieces, radix, held):
    trig, rows, channels = pieces[0].shape
    part = (trig, rows // radix, channels)
    types = [F32] + [BF16] * (radix - 1)
    if part[1] % 16:
        total = functools.reduce(jnp.add, [piece.astype(F32) for piece in pieces])
        return [
            total[:, place * part[1] : (place + 1) * part[1]].astype(kind) for place, kind in enumerate(types)
        ]
    kernel = functools.partial(add_kernel, len(pieces), radix)
    return call(kernel, [(VMEM, (part, kind)) for kind in types], in_vmem(pieces), held=held)


def mixed(owned, waves, w_mix, factor_scale):
    waves = jnp.where(lax.broadcasted_iota(jnp.int32, waves.shape, 1) < 3, waves, 0.0)
    square = jnp.sum(waves * waves, axis=1, keepdims=True)
    kernel = jnp.exp(-square / 128.0) / (1.0 + square / 64.0)
    factors = (owned * factor_scale).astype(BF16)
    energy = jnp.dot(factors, w_mix, preferred_element_type=F32)
    return (energy * jnp.concatenate([kernel, kernel], axis=0)).astype(BF16)


def energy_kernel(count, factor_scale, *refs):
    pieces = refs[:count]
    turned_ref, w_mix_ref, energy_ref = refs[count:]
    trig, rows, channels = energy_ref.shape
    total = pieces[0][...].astype(F32)
    for piece in pieces[1:]:
        total = total + piece[...].astype(F32)
    owned = total.reshape(trig * rows, channels)
    energy = mixed(owned, turned_ref[:rows, :].astype(F32), w_mix_ref[...], factor_scale)
    energy_ref[...] = energy.reshape(trig, rows, channels)


def energy_of(pieces, turned, w_mix, factor_scale, held):
    trig, rows, channels = pieces[0].shape
    if rows % 16:
        total = functools.reduce(jnp.add, [piece.astype(F32) for piece in pieces])
        energy = mixed(total.reshape(trig * rows, channels), turned[:rows].astype(F32), w_mix, factor_scale)
        return energy.reshape(trig, rows, channels)
    (energy,) = call(
        functools.partial(energy_kernel, len(pieces), factor_scale),
        [(VMEM, ((trig, rows, channels), BF16))],
        in_vmem([*pieces, turned, w_mix]),
        held=held,
    )
    return energy


def join_kernel(*refs):
    pieces, out_ref = refs[:-1], refs[-1]
    rows = pieces[0].shape[1]
    for place, piece in enumerate(pieces):
        out_ref[:, place * rows : (place + 1) * rows, :] = piece[...]


def joined(pieces, held):
    trig, rows, channels = pieces[0].shape
    if rows % 16:
        return jnp.concatenate(pieces, axis=1)
    whole = (VMEM, ((trig, rows * len(pieces), channels), BF16))
    (whole,) = call(join_kernel, [whole], in_vmem(pieces), held=held)
    return whole


def near_kernel(blocks, *refs):
    energies, (table_ref, out_ref, turned_ref) = refs[:blocks], refs[blocks:]
    for place, energy in enumerate(energies):
        turned_ref[place] = energy[...].astype(F32).T.astype(BF16)
    atoms = out_ref.shape[1]
    tile = math.gcd(atoms, 512)
    for start in range(0, atoms, tile):
        total = None
        for place in range(blocks):
            part = jnp.dot(turned_ref[place], table_ref[place, :, start : start + tile], preferred_element_type=F32)
            total = part if total is None else total + part
        out_ref[:, start : start + tile] = total


def final_kernel(
    blocks, scale, counts_ref, masked_ref, near_ref, message_ref, energy_ref, rest_ref, table_ref, out_ref, turned_ref
):
    cells, slots, channels = out_ref.shape
    step = pl.program_id(0)

    @pl.when(step == 0)
    def _():
        rows = energy_ref.shape[0]
        half = rows // 2
        turned_ref[0] = energy_ref[...].astype(F32).T.astype(BF16)
        for place in range(1, blocks):
            taken = rest_ref[:, (place - 1) * half : place * half, :].reshape(rows, channels)
            turned_ref[place] = taken.astype(F32).T.astype(BF16)

    atoms = cells * slots
    span = pl.ds(pl.multiple_of(step * atoms, atoms), atoms)
    total = near_ref[:, span]
    for place in range(blocks):
        total = total + jnp.dot(turned_ref[place], table_ref[blocks + place, :, span], preferred_element_type=F32)
    slot_ids = lax.broadcasted_iota(jnp.int32, (slots, channels), 0)
    for cell in range(cells):
        index = step * cells + cell
        value = total[:, cell * slots : (cell + 1) * slots].T * scale + message_ref[index]
        value = value * (0.5 + 0.5 * jnp.tanh(0.5 * value))
        result = masked_ref[index].astype(F32) + value
        out_ref[cell] = jnp.where(slot_ids < counts_ref[index], result, 0.0).astype(BF16)


def final_call(counts, near, message, masked, energy, rest, table, scale):
    cells, slots, channels = message.shape
    blocks, rows = table.shape[0] // 2, table.shape[1]
    group = math.gcd(cells, 4)
    cells_spec = pl.BlockSpec((group, slots, channels), lambda i: (i, 0, 0))
    operands = [masked, near, message, energy, rest, table]
    return pl.pallas_call(
        functools.partial(final_kernel, blocks, scale),
        grid=(cells // group,),
        in_specs=[SMEM] + [VMEM] * len(operands),
        out_specs=cells_spec,
        out_shape=jax.ShapeDtypeStruct(message.shape, BF16),
        scratch_shapes=[pltpu.VMEM((blocks, channels, rows), BF16)],
        compiler_params=PARAMS,
    )(counts, *[pltpu.with_memory_space_constraint(array, pltpu.VMEM) for array in operands])


def body(features, offsets, radial, neighbours, counts, wavevectors, w_msg, w_mix):
    _, cells, slots, channels = features.shape
    wave_count = wavevectors.shape[1]
    slabs, dev_count = lax.axis_size("grp"), lax.axis_size("dev")
    slab = lax.axis_index("grp")
    cell_line = cells * dev_count
    total_slots = slabs * cell_line * slots
    atoms = cells * slots
    lengths = (float(cell_line), float(slabs))
    features, offsets, counts = features[0], offsets[0].transpose(1, 0, 2), counts[0]

    swap = pairs_at("grp", 1, 1)
    sibling_offsets = lax.ppermute(offsets, "grp", swap)
    if slabs == 2:
        sibling_counts = lax.ppermute(counts, "grp", swap)
        sibling_features = lax.ppermute(features, "grp", swap)
    else:
        up = [(i, i + 1) for i in range(slabs - 1)]
        down = [(j, i) for i, j in up]
        near = [(lax.ppermute(counts, "grp", way), lax.ppermute(features, "grp", way)) for way in (up, down)]
        even = slab % 2 == 0
        sibling_counts = jnp.where(even, near[1][0], near[0][0])
        sibling_features = jnp.where(even, near[1][1], near[0][1])

    stages = [("dev", *digit) for digit in radices(dev_count)]
    stages += [("grp", 2 * stride, radix) for stride, radix in radices(slabs // 2)]
    digits = [("grp", 1, 2)] + stages
    half = wave_count // 2
    axis, stride, blocks = stages[0]
    block = half // blocks
    table = ((2 * block, atoms), BF16)
    sums = ((2 * block, channels), F32)
    piece = ((2 * block, channels), BF16)
    places_type = ((32, atoms), BF16)
    rows_type = ((atoms, channels), BF16)
    whole_table = (VMEM, ((2 * blocks,) + table[0], BF16))
    scratch = [pltpu.VMEM(*table)]
    block_flops = 2 * 2 * block * atoms * channels * COST

    def sent(part, place):
        return lax.ppermute(part.reshape(2, block, channels), axis, pairs_at(axis, stride, place))

    order = [*range(blocks - 1, 0, -1), 0]
    early = order[: min(2, blocks - 1)]
    masked, places, turned, tables, *outs = call(
        functools.partial(own_kernel, early, block, digits, lengths),
        [(VMEM, rows_type), (VMEM, places_type), (VMEM, ((wave_count, 32), BF16)), whole_table]
        + [(VMEM, sums)] * len(early),
        in_hbm([wavevectors, offsets, counts, features]),
        [
            pltpu.VMEM((32, wave_count), F32),
            pltpu.VMEM(wavevectors.shape, jnp.int32),
            pltpu.VMEM(offsets.shape, F32),
            pltpu.SMEM(counts.shape, jnp.int32),
            pltpu.VMEM(features.shape, BF16),
            pltpu.SemaphoreType.DMA((4,)),
        ],
    )
    started = dict(zip(early, outs))
    sibling, sibling_places, part = call(
        functools.partial(sibling_kernel, early[0], block, lengths),
        [(VMEM, rows_type), (VMEM, places_type), (VMEM, piece)],
        [(SMEM, sibling_counts)] + in_vmem([sibling_features, sibling_offsets, turned, started[early[0]]]),
        scratch,
    )
    received = {early[0]: sent(part, early[0])}
    for place in early[1:]:
        (part,) = call(
            functools.partial(continued_kernel, place, block),
            [(VMEM, piece)],
            in_vmem([turned, sibling_places, sibling, started[place]]),
            scratch,
            flops=block_flops,
        )
        received[place] = sent(part, place)
    for place in order[len(early) :]:
        tables, part = call(
            functools.partial(both_kernel, place, block),
            [whole_table, (VMEM, piece if place else sums)],
            in_vmem([turned, places, masked, sibling_places, sibling, tables]),
            scratch,
            [part] if place else [],
            2 * block_flops,
            {5: 0},
        )
        if place:
            received[place] = sent(part, place)
    pieces = [part.reshape(2, block, channels)] + [received[place] for place in range(1, blocks)]

    if slabs == 2:
        lines = [masked, sibling]
    else:
        lines = [masked] + [
            jnp.where(jnp.arange(slots)[None, :, None] < count[:, None, None], cell, jnp.bfloat16(0)).reshape(
                atoms, channels
            )
            for count, cell in near
        ]
    edge = (VMEM, ((len(lines), slots, channels), BF16))

    def rest_of(tables, first, last, lines, edges, held):
        return call(
            functools.partial(rest_kernel, range(first, last), block, len(lines)),
            [whole_table, *edges],
            in_vmem([turned, places, tables, *lines]),
            held=held,
            flops=block_flops * (last - first),
            same={2: 0},
        )

    middle = blocks + blocks // 2
    tables, *edges = rest_of(tables, blocks, middle, lines, [edge] * (1 if slabs == 2 else 2), [part])

    for axis, stride, radix in stages[1:]:
        parts = add_and_cut(pieces, radix, [tables])
        pieces = [parts[0]] + [
            lax.ppermute(parts[place], axis, pairs_at(axis, stride, place)) for place in range(1, radix)
        ]

    (tables,) = rest_of(tables, middle, 2 * blocks, [], [], [parts[0]])

    right = [(i, i + 1) for i in range(dev_count - 1)]
    left = [(j, i) for i, j in right]
    if slabs == 2:
        ways = right + [(dev_count + i, dev_count + j) for i, j in left]
        one = lax.ppermute(edges[0], ("grp", "dev"), ways)
        two = lax.ppermute(one, "grp", swap)
    else:
        one = lax.ppermute(edges[0], "dev", right)
        two = lax.ppermute(edges[1], "dev", left)

    energy = energy_of(pieces, turned, w_mix, 1.0 / math.sqrt(total_slots), [tables, one])

    for axis, stride, radix in reversed(stages[1:]):
        energy = joined(
            [energy] + [lax.ppermute(energy, axis, pairs_at(axis, stride, place)) for place in range(1, radix)],
            [tables],
        )
    axis, stride, blocks = stages[0]
    energies = [energy] + [
        lax.ppermute(energy, axis, pairs_at(axis, stride, place)) for place in range(1, blocks)
    ]
    other_energy = lax.ppermute(energy, "grp", swap)

    chunks = math.gcd(cells, 4)
    (message,) = call(
        functools.partial(short_kernel, len(lines), chunks),
        [(VMEM, ((cells, slots, channels), F32))],
        [(SMEM, neighbours[0].T)]
        + in_hbm([radial.reshape(-1, slots, slots), *[line.reshape(cells, slots, channels) for line in lines], one, two])
        + in_vmem([w_msg]),
        [
            pltpu.VMEM((len(lines) * (cells + 2), slots, channels), BF16),
            pltpu.SMEM((9 * cells,), jnp.int32),
            pltpu.VMEM((cells * radial.shape[2] + 1, slots, slots), BF16),
            pltpu.SemaphoreType.DMA((2 * len(lines) + chunks * (1 + len(lines)),)),
        ],
        [energy, other_energy, tables],
        6 * block_flops,
    )
    rest = lax.ppermute(joined(energies[1:], [message]), "grp", swap)
    energies = [part.reshape(2 * block, channels) for part in energies]
    other_energy = other_energy.reshape(2 * block, channels)
    (near_sum,) = call(
        functools.partial(near_kernel, blocks),
        [(VMEM, ((channels, atoms), F32))],
        in_vmem([*energies, tables]),
        [pltpu.VMEM((blocks, channels, 2 * block), BF16)],
        [message],
        2 * block_flops,
    )
    masked = masked.reshape(cells, slots, channels)
    scale = 8.0 / math.sqrt(wave_count)
    result = final_call(counts, near_sum, message, masked, other_energy, rest, tables, scale)
    return result[None]


def solution(mesh):
    in_specs = (
        P("grp", "dev", None, None),
        P("grp", "dev", None, None),
        P("grp", "dev", None, None, None),
        P("grp", "dev", None),
        P("grp", "dev"),
        P(),
        P(),
        P(),
    )
    out_specs = P("grp", "dev", None, None)
    return jax.shard_map(body, mesh=mesh, in_specs=in_specs, out_specs=out_specs, check_vma=False)
```

```python
import functools
import math

import jax
import jax.numpy as jnp
from jax import lax
from jax.experimental import pallas as pl
from jax.experimental.pallas import tpu as pltpu
from jax.sharding import PartitionSpec as P

F32 = jnp.float32
BF16 = jnp.bfloat16
VMEM = pl.BlockSpec(memory_space=pltpu.VMEM)
SMEM = pl.BlockSpec(memory_space=pltpu.SMEM)
HBM = pl.BlockSpec(memory_space=pltpu.HBM)
PARAMS = pltpu.CompilerParams(vmem_limit_bytes=14 * 1024 * 1024)
LANES = 128
COST = 0
WEIGHT = 4
SIN = (4.44287957, -7.30781668, 3.59777418, -0.79119939)
COS = (1.41420401, -6.97763732, 5.71518787, -1.72821389)


def call(kernel, outs, operands, scratch=(), held=(), flops=0, same=()):
    ahead = len(operands)
    operands = list(operands) + [(VMEM, array) for array in held]

    def without_held(*refs):
        kernel(*refs[:ahead], *refs[len(operands) :])

    return pl.pallas_call(
        without_held,
        in_specs=[place for place, _ in operands],
        out_specs=[place for place, _ in outs],
        out_shape=[place.memory_space(*kind) for place, kind in outs],
        scratch_shapes=list(scratch),
        input_output_aliases=dict(same),
        compiler_params=PARAMS,
        cost_estimate=pl.CostEstimate(flops=flops, bytes_accessed=flops // 300, transcendentals=0),
    )(
        *[
            array if place is SMEM else pltpu.with_memory_space_constraint(array, place.memory_space)
            for place, array in operands
        ]
    )


def in_vmem(arrays):
    return [(VMEM, array) for array in arrays]


def in_hbm(arrays):
    return [(HBM, array) for array in arrays]


def begin(sources, targets, semaphores, first=0):
    copies = [
        pltpu.make_async_copy(source, target, semaphores.at[first + index])
        for index, (source, target) in enumerate(zip(sources, targets))
    ]
    for copy in copies:
        copy.start()
    return copies


def finish(copies):
    for copy in copies:
        copy.wait()


def radices(count):
    digits = []
    stride = 1
    while stride < count:
        radix = 4 if count // stride % 4 == 0 else 2
        digits.append((stride, radix))
        stride *= radix
    return digits


def pairs_at(axis, stride, offset):
    return [(place, place ^ (offset * stride)) for place in range(lax.axis_size(axis))]


def fill_places(offsets_ref, places_ref, first, slab, cell_line, slabs):
    _, cells, slots = offsets_ref.shape
    line = lax.broadcasted_iota(jnp.int32, (8, slots), 0)
    along_z_base = slab.astype(F32)
    for cell in range(cells):
        along_x = ((first + cell).astype(F32) + offsets_ref[0, cell : cell + 1]) / cell_line
        along_y = offsets_ref[1, cell : cell + 1]
        along_z = (along_z_base + offsets_ref[2, cell : cell + 1]) / slabs
        full = jnp.where(line == 0, along_x, jnp.where(line == 1, along_y, jnp.where(line == 2, along_z, 0.0)))
        high = full.astype(BF16).astype(F32)
        middle = (full - high).astype(BF16).astype(F32)
        low = full - high - middle
        parts = jnp.concatenate([high, middle, low, jnp.zeros_like(low)], axis=0)
        places_ref[:, cell * slots : (cell + 1) * slots] = parts.astype(BF16)


def fill_masked(counts_ref, features_ref, masked_ref):
    cells, slots, channels = features_ref.shape
    slot_ids = lax.broadcasted_iota(jnp.int32, (slots, channels), 0)
    for cell in range(cells):
        kept = jnp.where(slot_ids < counts_ref[cell], features_ref[cell].astype(F32), 0.0)
        masked_ref[cell * slots : (cell + 1) * slots, :] = kept.astype(BF16)


def fill_waves(waves_ref, padded_ref, turned_ref, flips):
    count = waves_ref.shape[1]
    waves = waves_ref[...].astype(F32)
    padded_ref[...] = jnp.zeros_like(padded_ref)
    for part in range(3):
        padded_ref[8 * part : 8 * part + 3, :] = waves
    rows = lax.broadcasted_iota(jnp.int32, (LANES, LANES), 0)
    columns = lax.broadcasted_iota(jnp.int32, (LANES, LANES), 1)
    order = jnp.where((rows ^ (flips & (LANES - 1))) == columns, 1.0, 0.0).astype(BF16)
    for block in range(count // LANES):
        source = pl.multiple_of((block ^ (flips // LANES)) * LANES, LANES)
        taken = padded_ref[:, pl.ds(source, LANES)].astype(BF16)
        turned = lax.dot_general(order, taken, (((1,), (1,)), ((), ())), preferred_element_type=F32)
        turned_ref[block * LANES : (block + 1) * LANES, :] = turned.astype(BF16)


def fill_table(waves, places_ref, table_ref):
    block = waves.shape[0]
    atoms = places_ref.shape[1]
    tile = math.gcd(atoms, 256)
    for start in range(0, atoms, tile):
        span = slice(start, start + tile)
        turns = jnp.dot(waves, places_ref[:, span], preferred_element_type=F32)
        part = turns - jnp.round(turns)
        square = part * part
        sine = part * (SIN[0] + square * (SIN[1] + square * (SIN[2] + square * SIN[3])))
        cosine = COS[0] + square * (COS[1] + square * (COS[2] + square * COS[3]))
        table_ref[:block, span] = (1.0 - sine * sine).astype(BF16)
        table_ref[block:, span] = (sine * cosine).astype(BF16)


def sums_of(table_ref, rows_ref):
    return jnp.dot(table_ref[...], rows_ref[...], preferred_element_type=F32)


def own_kernel(early, block, digits, lengths, *refs):
    sources, refs = refs[:4], refs[4:]
    masked_ref, places_ref, turned_ref, table_ref = refs[:4]
    sums = refs[4 : 4 + len(early)]
    padded_ref, waves_ref, offsets_ref, counts_ref, features_ref, semaphores = refs[4 + len(early) :]
    copies = begin(sources, (waves_ref, offsets_ref, counts_ref, features_ref), semaphores)
    cells = features_ref.shape[0]
    dev, slab = lax.axis_index("dev"), lax.axis_index("grp")
    flips = jnp.int32(0)
    weight = waves_ref.shape[1]
    for axis, stride, radix in digits:
        weight //= radix
        flips += ((slab if axis == "grp" else dev) // stride % radix) * weight
    copies[0].wait()
    fill_waves(waves_ref, padded_ref, turned_ref, flips)
    copies[1].wait()
    fill_places(offsets_ref, places_ref, dev * cells, slab, *lengths)
    copies[2].wait()
    copies[3].wait()
    fill_masked(counts_ref, features_ref, masked_ref)
    for place, sums_ref in zip(early, sums):
        fill_table(turned_ref[place * block : (place + 1) * block, :], places_ref, table_ref.at[place])
        sums_ref[...] = sums_of(table_ref.at[place], masked_ref)


def sibling_kernel(
    place, block, lengths, counts_ref, features_ref, offsets_ref, turned_ref, start_ref,
    masked_ref, places_ref, piece_ref, table_ref,
):
    cells = features_ref.shape[0]
    fill_places(offsets_ref, places_ref, lax.axis_index("dev") * cells, lax.axis_index("grp") ^ 1, *lengths)
    fill_masked(counts_ref, features_ref, masked_ref)
    fill_table(turned_ref[place * block : (place + 1) * block, :], places_ref, table_ref)
    piece_ref[...] = (start_ref[...] + sums_of(table_ref, masked_ref)).astype(piece_ref.dtype)


def continued_kernel(place, block, turned_ref, places_ref, masked_ref, start_ref, piece_ref, table_ref):
    fill_table(turned_ref[place * block : (place + 1) * block, :], places_ref, table_ref)
    piece_ref[...] = (start_ref[...] + sums_of(table_ref, masked_ref)).astype(piece_ref.dtype)


def both_kernel(
    place, block, turned_ref, own_places_ref, own_ref, places_ref, masked_ref, _, kept_ref, piece_ref, table_ref
):
    waves = turned_ref[place * block : (place + 1) * block, :]
    fill_table(waves, own_places_ref, kept_ref.at[place])
    total = sums_of(kept_ref.at[place], own_ref)
    fill_table(waves, places_ref, table_ref)
    piece_ref[...] = (total + sums_of(table_ref, masked_ref)).astype(piece_ref.dtype)


def fill_edges(lines, last_ref, first_ref):
    slots = last_ref.shape[1]
    for line, rows_ref in enumerate(lines):
        last_ref[line] = rows_ref[rows_ref.shape[0] - slots :, :]
        first_ref[line] = rows_ref[:slots, :]


def rest_kernel(blocks, block, lines, turned_ref, places_ref, _, *refs):
    kept_ref, *outs = refs[lines + 1 if lines else 0 :]
    if lines:
        *edges, radial_ref, semaphores = outs
        source_ref = refs[lines]
        count = source_ref.shape[0]
        copies = begin([source_ref], [radial_ref.at[pl.ds(0, count)]], semaphores)
        radial_ref[count] = jnp.zeros_like(radial_ref[count])
        fill_edges(refs[:lines], *edges)
    for place in blocks:
        fill_table(turned_ref[place * block : (place + 1) * block, :], places_ref, kept_ref.at[place])
    if lines:
        finish(copies)


def short_kernel(lines, codes_ref, radial_ref, *refs):
    line_refs, refs = refs[:lines], refs[lines:]
    outer, (handed_ref, w_ref, message_ref, found_ref) = refs[:-4], refs[-4:]
    cells, slots, channels = message_ref.shape
    pairs = codes_ref.shape[0]
    slab, slabs = lax.axis_index("grp"), lax.axis_size("grp")

    def outer_cell(line, side):
        if slabs == 2:
            start = handed_ref.shape[0] - (4 - 2 * side - (1 - line)) * slots
            return jnp.where(slab == 1, outer[side][line], handed_ref[start : start + slots, :])
        return outer[side][line]

    nothing = cells * pairs
    for cell in range(cells):
        for code in range(9):
            found_ref[9 * cell + code] = nothing
        for pair in range(pairs):
            found_ref[9 * cell + codes_ref[pair, cell]] = cell * pairs + pair
    levels = [1, 2 - 2 * slab] if slabs == 2 else [1, 0, 2]
    carried = None
    for start in range(0, cells + 2, 2):
        takers = [cell for cell in range(start - 2, start + 2) if 0 <= cell < cells]
        total = None
        for line, level in enumerate(levels):
            rows = []
            for cell in takers:
                halves = []
                for place in (start, start + 1):
                    along = place - cell
                    index = found_ref[9 * cell + 3 * level + along] if 0 <= along < 3 else nothing
                    halves.append(radial_ref[index])
                rows.append(jnp.concatenate(halves, axis=1))
            span = slice(max(start - 1, 0) * slots, min(start + 1, cells) * slots)
            taken = [line_refs[line][span, :]]
            if start == 0:
                taken = [outer_cell(line, 0)] + taken
            if start == cells:
                taken = taken + [outer_cell(line, 1)]
            taken = jnp.concatenate(taken, axis=0)
            part = jnp.dot(jnp.concatenate(rows, axis=0), taken, preferred_element_type=F32)
            total = part if total is None else total + part
        if start:
            gathered = (carried + total[: 2 * slots]).astype(BF16)
            message = jnp.dot(gathered, w_ref[...], preferred_element_type=F32)
            message_ref[start - 2 : start] = message.reshape(2, slots, channels)
            total = total[2 * slots :]
        carried = total


def add_kernel(count, radix, *refs):
    pieces, outs = refs[:count], refs[count:]
    total = pieces[0][...].astype(F32)
    for piece in pieces[1:]:
        total = total + piece[...].astype(F32)
    rows = total.shape[1] // radix
    for place, out in enumerate(outs):
        out[...] = total[:, place * rows : (place + 1) * rows].astype(out.dtype)


def add_and_cut(pieces, radix, held):
    trig, rows, channels = pieces[0].shape
    part = (trig, rows // radix, channels)
    types = [F32] + [BF16] * (radix - 1)
    if part[1] % 16:
        total = functools.reduce(jnp.add, [piece.astype(F32) for piece in pieces])
        return [
            total[:, place * part[1] : (place + 1) * part[1]].astype(kind) for place, kind in enumerate(types)
        ]
    kernel = functools.partial(add_kernel, len(pieces), radix)
    return call(kernel, [(VMEM, (part, kind)) for kind in types], in_vmem(pieces), held=held)


def mixed(owned, waves, w_mix, factor_scale):
    waves = jnp.where(lax.broadcasted_iota(jnp.int32, waves.shape, 1) < 3, waves, 0.0)
    square = jnp.sum(waves * waves, axis=1, keepdims=True)
    kernel = jnp.exp(-square / 128.0) / (1.0 + square / 64.0)
    factors = (owned * factor_scale).astype(BF16)
    energy = jnp.dot(factors, w_mix, preferred_element_type=F32)
    return (energy * jnp.concatenate([kernel, kernel], axis=0)).astype(BF16)


def energy_kernel(count, factor_scale, *refs):
    pieces = refs[:count]
    turned_ref, w_mix_ref, energy_ref = refs[count:]
    trig, rows, channels = energy_ref.shape
    total = pieces[0][...].astype(F32)
    for piece in pieces[1:]:
        total = total + piece[...].astype(F32)
    owned = total.reshape(trig * rows, channels)
    energy = mixed(owned, turned_ref[:rows, :].astype(F32), w_mix_ref[...], factor_scale)
    energy_ref[...] = energy.reshape(trig, rows, channels)


def energy_of(pieces, turned, w_mix, factor_scale, held):
    trig, rows, channels = pieces[0].shape
    if rows % 16:
        total = functools.reduce(jnp.add, [piece.astype(F32) for piece in pieces])
        energy = mixed(total.reshape(trig * rows, channels), turned[:rows].astype(F32), w_mix, factor_scale)
        return energy.reshape(trig, rows, channels)
    (energy,) = call(
        functools.partial(energy_kernel, len(pieces), factor_scale),
        [(VMEM, ((trig, rows, channels), BF16))],
        in_vmem([*pieces, turned, w_mix]),
        held=held,
        flops=WEIGHT * 10**9,
    )
    return energy


def join_kernel(count, *refs):
    pieces, out_ref = refs[:count], refs[-1]
    rows = pieces[0].shape[1]
    for place, piece in enumerate(pieces):
        out_ref[:, place * rows : (place + 1) * rows, :] = piece[...]


def pack_kernel(count, *refs):
    pieces, extras, (out_ref, packed_ref) = refs[:count], refs[count:-2], refs[-2:]
    trig, rows, _ = pieces[0].shape
    for place, piece in enumerate(pieces):
        out_ref[:, place * rows : (place + 1) * rows, :] = piece[...]
        for part in range(trig):
            start = (part * count + place) * rows
            packed_ref[start : start + rows, :] = piece[part]
    start = trig * count * rows
    for extra in extras:
        for line in range(extra.shape[0]):
            packed_ref[start : start + extra.shape[1], :] = extra[line]
            start += extra.shape[1]


def joined(pieces, held):
    trig, rows, channels = pieces[0].shape
    if rows % 16:
        return jnp.concatenate(pieces, axis=1)
    whole = (VMEM, ((trig, rows * len(pieces), channels), BF16))
    (whole,) = call(functools.partial(join_kernel, len(pieces)), [whole], in_vmem(pieces), held=held)
    return whole


def packed(pieces, extras, held):
    trig, rows, channels = pieces[0].shape
    count = trig * rows * len(pieces) + sum(extra.shape[0] * extra.shape[1] for extra in extras)
    return call(
        functools.partial(pack_kernel, len(pieces)),
        [(VMEM, ((trig, rows * len(pieces), channels), BF16)), (VMEM, ((count, channels), BF16))],
        in_vmem([*pieces, *extras]),
        held=held,
    )


def near_kernel(blocks, *refs):
    energies, (table_ref, out_ref, turned_ref) = refs[:blocks], refs[blocks:]
    for place, energy in enumerate(energies):
        turned_ref[place] = energy[...].astype(F32).T.astype(BF16)
    atoms = out_ref.shape[1]
    tile = math.gcd(atoms, 512)
    for start in range(0, atoms, tile):
        total = None
        for place in range(blocks):
            part = jnp.dot(turned_ref[place], table_ref[place, :, start : start + tile], preferred_element_type=F32)
            total = part if total is None else total + part
        out_ref[:, start : start + tile] = total


def final_kernel(
    blocks, scale, counts_ref, masked_ref, near_ref, message_ref, energy_ref, rest_ref, table_ref, out_ref, turned_ref,
    result_ref, semaphores,
):
    cells, slots, channels = out_ref.shape
    rows = table_ref.shape[1]
    half = rows // 2
    turned_ref[0] = energy_ref[:rows, :].astype(F32).T.astype(BF16)
    for place in range(1, blocks):
        taken = rest_ref[:, (place - 1) * half : place * half, :].reshape(rows, channels)
        turned_ref[place] = taken.astype(F32).T.astype(BF16)
    slot_ids = lax.broadcasted_iota(jnp.int32, (slots, channels), 0)
    group = math.gcd(cells, 2)
    share = math.gcd(cells, 4)
    leaving = []
    for first in range(0, cells, group):
        span = slice(first * slots, (first + group) * slots)
        total = near_ref[:, span]
        for place in range(blocks):
            total = total + jnp.dot(turned_ref[place], table_ref[blocks + place, :, span], preferred_element_type=F32)
        for cell in range(first, first + group):
            value = total[:, (cell - first) * slots : (cell - first + 1) * slots].T * scale + message_ref[cell]
            value = value * (0.5 + 0.5 * jnp.tanh(0.5 * value))
            result = masked_ref[cell * slots : (cell + 1) * slots, :].astype(F32) + value
            result_ref[cell] = jnp.where(slot_ids < counts_ref[cell], result, 0.0).astype(BF16)
        if (first + group) % share == 0:
            done = pl.ds(first + group - share, share)
            leaving += begin([result_ref.at[done]], [out_ref.at[done]], semaphores, first // share)
    finish(leaving)


def final_call(counts, near, message, masked, energy, rest, table, scale):
    blocks, rows = table.shape[0] // 2, table.shape[1]
    cells, slots, channels = message.shape
    (result,) = call(
        functools.partial(final_kernel, blocks, scale),
        [(HBM, (message.shape, BF16))],
        [(SMEM, counts)] + in_vmem([masked, near, message, energy, rest, table]),
        [
            pltpu.VMEM((blocks, channels, rows), BF16),
            pltpu.VMEM(message.shape, BF16),
            pltpu.SemaphoreType.DMA((cells // math.gcd(cells, 4),)),
        ],
    )
    return result


def body(features, offsets, radial, neighbours, counts, wavevectors, w_msg, w_mix):
    _, cells, slots, channels = features.shape
    wave_count = wavevectors.shape[1]
    slabs, dev_count = lax.axis_size("grp"), lax.axis_size("dev")
    slab = lax.axis_index("grp")
    cell_line = cells * dev_count
    total_slots = slabs * cell_line * slots
    atoms = cells * slots
    lengths = (float(cell_line), float(slabs))
    features, offsets, counts = features[0], offsets[0].transpose(1, 0, 2), counts[0]

    swap = pairs_at("grp", 1, 1)
    sibling_offsets = lax.ppermute(offsets, "grp", swap)
    if slabs == 2:
        sibling_counts = lax.ppermute(counts, "grp", swap)
        sibling_features = lax.ppermute(features, "grp", swap)
    else:
        up = [(i, i + 1) for i in range(slabs - 1)]
        down = [(j, i) for i, j in up]
        near = [(lax.ppermute(counts, "grp", way), lax.ppermute(features, "grp", way)) for way in (up, down)]
        even = slab % 2 == 0
        sibling_counts = jnp.where(even, near[1][0], near[0][0])
        sibling_features = jnp.where(even, near[1][1], near[0][1])

    stages = [("dev", *digit) for digit in radices(dev_count)]
    stages += [("grp", 2 * stride, radix) for stride, radix in radices(slabs // 2)]
    digits = [("grp", 1, 2)] + stages
    half = wave_count // 2
    axis, stride, blocks = stages[0]
    block = half // blocks
    table = ((2 * block, atoms), BF16)
    sums = ((2 * block, channels), F32)
    piece = ((2 * block, channels), BF16)
    places_type = ((32, atoms), BF16)
    rows_type = ((atoms, channels), BF16)
    whole_table = (VMEM, ((2 * blocks,) + table[0], BF16))
    scratch = [pltpu.VMEM(*table)]
    block_flops = 2 * 2 * block * atoms * channels * COST

    def sent(part, place):
        return lax.ppermute(part.reshape(2, block, channels), axis, pairs_at(axis, stride, place))

    order = [*range(blocks - 1, 0, -1), 0]
    early = order[: min(2, blocks - 1)]
    masked, places, turned, tables, *outs = call(
        functools.partial(own_kernel, early, block, digits, lengths),
        [(VMEM, rows_type), (VMEM, places_type), (VMEM, ((wave_count, 32), BF16)), whole_table]
        + [(VMEM, sums)] * len(early),
        in_hbm([wavevectors, offsets, counts, features]),
        [
            pltpu.VMEM((32, wave_count), F32),
            pltpu.VMEM(wavevectors.shape, jnp.int32),
            pltpu.VMEM(offsets.shape, F32),
            pltpu.SMEM(counts.shape, jnp.int32),
            pltpu.VMEM(features.shape, BF16),
            pltpu.SemaphoreType.DMA((4,)),
        ],
    )
    started = dict(zip(early, outs))
    sibling, sibling_places, part = call(
        functools.partial(sibling_kernel, early[0], block, lengths),
        [(VMEM, rows_type), (VMEM, places_type), (VMEM, piece)],
        [(SMEM, sibling_counts)] + in_vmem([sibling_features, sibling_offsets, turned, started[early[0]]]),
        scratch,
    )
    received = {early[0]: sent(part, early[0])}
    for place in early[1:]:
        (part,) = call(
            functools.partial(continued_kernel, place, block),
            [(VMEM, piece)],
            in_vmem([turned, sibling_places, sibling, started[place]]),
            scratch,
            flops=block_flops,
        )
        received[place] = sent(part, place)
    for place in order[len(early) :]:
        tables, part = call(
            functools.partial(both_kernel, place, block),
            [whole_table, (VMEM, piece if place else sums)],
            in_vmem([turned, places, masked, sibling_places, sibling, tables]),
            scratch,
            [part] if place else [received[early[0]]],
            2 * block_flops,
            {5: 0},
        )
        if place:
            received[place] = sent(part, place)
    pieces = [part.reshape(2, block, channels)] + [received[place] for place in range(1, blocks)]

    if slabs == 2:
        lines = [masked, sibling]
    else:
        lines = [masked] + [
            jnp.where(jnp.arange(slots)[None, :, None] < count[:, None, None], cell, jnp.bfloat16(0)).reshape(
                atoms, channels
            )
            for count, cell in near
        ]
    edge = (VMEM, ((len(lines), slots, channels), BF16))

    def rest_of(tables, first, last, held, more=(), outs=(), scratch=(), weight=0):
        return call(
            functools.partial(rest_kernel, range(first, last), block, len(more[:-1])),
            [whole_table, *outs],
            in_vmem([turned, places, tables, *more[:-1]]) + in_hbm(more[-1:]),
            scratch,
            held,
            weight,
            {2: 0},
        )

    middle = blocks + blocks // 2
    (tables,) = rest_of(tables, blocks, middle, [part])

    for axis, stride, radix in stages[1:]:
        parts = add_and_cut(pieces, radix, [tables])
        pieces = [parts[0]] + [
            lax.ppermute(parts[place], axis, pairs_at(axis, stride, place)) for place in range(1, radix)
        ]

    radial = radial.reshape(-1, slots, slots)
    radial_type = (VMEM, ((radial.shape[0] + 1, slots, slots), BF16))
    tables, *edges, radial = rest_of(
        tables, middle, 2 * blocks, [parts[0]],
        [*lines, radial], [edge, edge, radial_type], [pltpu.SemaphoreType.DMA((1,))],
    )

    right = [(i, i + 1) for i in range(dev_count - 1)]
    left = [(j, i) for i, j in right]
    if slabs == 2:
        outer = [
            lax.ppermute(part, ("grp", "dev"), [(dev_count + i, dev_count + j) for i, j in way])
            for part, way in zip(edges, (right, left))
        ]
    else:
        outer = [lax.ppermute(part, "dev", way) for part, way in zip(edges, (right, left))]

    energy = energy_of(pieces, turned, w_mix, 1.0 / math.sqrt(total_slots), [tables, radial])

    for stage, (axis, stride, radix) in reversed(list(enumerate(stages))[1:]):
        pieces = [energy] + [
            lax.ppermute(energy, axis, pairs_at(axis, stride, place)) for place in range(1, radix)
        ]
        if stage > 1:
            energy = joined(pieces, [tables, radial])
    energy, handed = packed(pieces, outer if slabs == 2 else [], [tables, radial])
    handed = lax.ppermute(handed, "grp", swap)
    axis, stride, blocks = stages[0]
    energies = [energy] + [
        lax.ppermute(energy, axis, pairs_at(axis, stride, place)) for place in range(1, blocks)
    ]

    (message,) = call(
        functools.partial(short_kernel, len(lines)),
        [(VMEM, ((cells, slots, channels), F32))],
        [(SMEM, neighbours[0].T)] + in_vmem([radial, *lines, *outer, handed, w_msg]),
        [pltpu.SMEM((9 * cells,), jnp.int32)],
        [energy, tables],
        6 * block_flops,
    )
    rest = lax.ppermute(joined(energies[1:], [message]), "grp", swap)
    energies = [part.reshape(2 * block, channels) for part in energies]
    (near_sum,) = call(
        functools.partial(near_kernel, blocks),
        [(VMEM, ((channels, atoms), F32))],
        in_vmem([*energies, tables]),
        [pltpu.VMEM((blocks, channels, 2 * block), BF16)],
        [message],
        2 * block_flops,
    )
    scale = 8.0 / math.sqrt(wave_count)
    result = final_call(counts, near_sum, message, masked, handed, rest, tables, scale)
    return result[None]


def solution(mesh):
    in_specs = (
        P("grp", "dev", None, None),
        P("grp", "dev", None, None),
        P("grp", "dev", None, None, None),
        P("grp", "dev", None),
        P("grp", "dev"),
        P(),
        P(),
        P(),
    )
    out_specs = P("grp", "dev", None, None)
    return jax.shard_map(body, mesh=mesh, in_specs=in_specs, out_specs=out_specs, check_vma=False)
```

```python
import functools
import math

import jax
import jax.numpy as jnp
from jax import lax
from jax.experimental import pallas as pl
from jax.experimental.pallas import tpu as pltpu
from jax.sharding import PartitionSpec as P

F32 = jnp.float32
BF16 = jnp.bfloat16
VMEM = pl.BlockSpec(memory_space=pltpu.VMEM)
SMEM = pl.BlockSpec(memory_space=pltpu.SMEM)
HBM = pl.BlockSpec(memory_space=pltpu.HBM)
PARAMS = pltpu.CompilerParams(vmem_limit_bytes=14 * 1024 * 1024)
LANES = 128
COST = 0
WEIGHT = 0
SIN = (4.44287957, -7.30781668, 3.59777418, -0.79119939)
COS = (1.41420401, -6.97763732, 5.71518787, -1.72821389)


def call(kernel, outs, operands, scratch=(), held=(), flops=0, same=()):
    ahead = len(operands)
    operands = list(operands) + [(VMEM, array) for array in held]

    def without_held(*refs):
        kernel(*refs[:ahead], *refs[len(operands) :])

    return pl.pallas_call(
        without_held,
        in_specs=[place for place, _ in operands],
        out_specs=[place for place, _ in outs],
        out_shape=[place.memory_space(*kind) for place, kind in outs],
        scratch_shapes=list(scratch),
        input_output_aliases=dict(same),
        compiler_params=PARAMS,
        cost_estimate=pl.CostEstimate(flops=flops, bytes_accessed=flops // 300, transcendentals=0),
    )(
        *[
            array if place is SMEM else pltpu.with_memory_space_constraint(array, place.memory_space)
            for place, array in operands
        ]
    )


def in_vmem(arrays):
    return [(VMEM, array) for array in arrays]


def in_hbm(arrays):
    return [(HBM, array) for array in arrays]


def begin(sources, targets, semaphores, first=0):
    copies = [
        pltpu.make_async_copy(source, target, semaphores.at[first + index])
        for index, (source, target) in enumerate(zip(sources, targets))
    ]
    for copy in copies:
        copy.start()
    return copies


def finish(copies):
    for copy in copies:
        copy.wait()


def pairs_at(axis, stride, offset):
    return [(place, place ^ (offset * stride)) for place in range(lax.axis_size(axis))]


def fill_places(offsets_ref, places_ref, first, slab, cell_line, slabs):
    _, cells, slots = offsets_ref.shape
    line = lax.broadcasted_iota(jnp.int32, (8, slots), 0)
    along_z_base = slab.astype(F32)
    for cell in range(cells):
        along_x = ((first + cell).astype(F32) + offsets_ref[0, cell : cell + 1]) / cell_line
        along_y = offsets_ref[1, cell : cell + 1]
        along_z = (along_z_base + offsets_ref[2, cell : cell + 1]) / slabs
        full = jnp.where(line == 0, along_x, jnp.where(line == 1, along_y, jnp.where(line == 2, along_z, 0.0)))
        high = full.astype(BF16).astype(F32)
        middle = (full - high).astype(BF16).astype(F32)
        low = full - high - middle
        parts = jnp.concatenate([high, middle, low, jnp.zeros_like(low)], axis=0)
        places_ref[:, cell * slots : (cell + 1) * slots] = parts.astype(BF16)


def fill_masked(counts_ref, features_ref, masked_ref):
    cells, slots, channels = features_ref.shape
    slot_ids = lax.broadcasted_iota(jnp.int32, (slots, channels), 0)
    for cell in range(cells):
        kept = jnp.where(slot_ids < counts_ref[cell], features_ref[cell].astype(F32), 0.0)
        masked_ref[cell * slots : (cell + 1) * slots, :] = kept.astype(BF16)


def fill_waves(waves_ref, padded_ref, turned_ref, flips):
    count = waves_ref.shape[1]
    waves = waves_ref[...].astype(F32)
    padded_ref[...] = jnp.zeros_like(padded_ref)
    for part in range(3):
        padded_ref[8 * part : 8 * part + 3, :] = waves
    rows = lax.broadcasted_iota(jnp.int32, (LANES, LANES), 0)
    columns = lax.broadcasted_iota(jnp.int32, (LANES, LANES), 1)
    order = jnp.where((rows ^ (flips & (LANES - 1))) == columns, 1.0, 0.0).astype(BF16)
    for block in range(count // LANES):
        source = pl.multiple_of((block ^ (flips // LANES)) * LANES, LANES)
        taken = padded_ref[:, pl.ds(source, LANES)].astype(BF16)
        turned = lax.dot_general(order, taken, (((1,), (1,)), ((), ())), preferred_element_type=F32)
        turned_ref[block * LANES : (block + 1) * LANES, :] = turned.astype(BF16)


def fill_table(waves, places_ref, table_ref):
    block = waves.shape[0]
    atoms = places_ref.shape[1]
    tile = math.gcd(atoms, 256)
    for start in range(0, atoms, tile):
        span = slice(start, start + tile)
        turns = jnp.dot(waves, places_ref[:, span], preferred_element_type=F32)
        part = turns - jnp.round(turns)
        square = part * part
        sine = part * (SIN[0] + square * (SIN[1] + square * (SIN[2] + square * SIN[3])))
        cosine = COS[0] + square * (COS[1] + square * (COS[2] + square * COS[3]))
        table_ref[:block, span] = (1.0 - sine * sine).astype(BF16)
        table_ref[block:, span] = (sine * cosine).astype(BF16)


def sums_of(table_ref, rows_ref):
    return jnp.dot(table_ref[...], rows_ref[...], preferred_element_type=F32)


def own_kernel(early, block, digits, lengths, *refs):
    sources, refs = refs[:4], refs[4:]
    masked_ref, places_ref, turned_ref, table_ref = refs[:4]
    sums = refs[4 : 4 + len(early)]
    padded_ref, waves_ref, offsets_ref, counts_ref, features_ref, semaphores = refs[4 + len(early) :]
    copies = begin(sources, (waves_ref, offsets_ref, counts_ref, features_ref), semaphores)
    cells = features_ref.shape[0]
    dev, slab = lax.axis_index("dev"), lax.axis_index("grp")
    flips = jnp.int32(0)
    weight = waves_ref.shape[1]
    for axis, stride, radix in digits:
        weight //= radix
        flips += ((slab if axis == "grp" else dev) // stride % radix) * weight
    copies[0].wait()
    fill_waves(waves_ref, padded_ref, turned_ref, flips)
    copies[1].wait()
    fill_places(offsets_ref, places_ref, dev * cells, slab, *lengths)
    copies[2].wait()
    copies[3].wait()
    fill_masked(counts_ref, features_ref, masked_ref)
    for place, sums_ref in zip(early, sums):
        fill_table(turned_ref[place * block : (place + 1) * block, :], places_ref, table_ref.at[place])
        sums_ref[...] = sums_of(table_ref.at[place], masked_ref)


def sibling_kernel(
    place, block, lengths, counts_ref, features_ref, offsets_ref, turned_ref, start_ref,
    masked_ref, places_ref, piece_ref, table_ref,
):
    cells = features_ref.shape[0]
    fill_places(offsets_ref, places_ref, lax.axis_index("dev") * cells, lax.axis_index("grp") ^ 1, *lengths)
    fill_masked(counts_ref, features_ref, masked_ref)
    fill_table(turned_ref[place * block : (place + 1) * block, :], places_ref, table_ref)
    piece_ref[...] = (start_ref[...] + sums_of(table_ref, masked_ref)).astype(piece_ref.dtype)


def continued_kernel(place, block, turned_ref, places_ref, masked_ref, start_ref, piece_ref, table_ref):
    fill_table(turned_ref[place * block : (place + 1) * block, :], places_ref, table_ref)
    piece_ref[...] = (start_ref[...] + sums_of(table_ref, masked_ref)).astype(piece_ref.dtype)


def both_kernel(
    place, block, turned_ref, own_places_ref, own_ref, places_ref, masked_ref, _, kept_ref, piece_ref, table_ref
):
    waves = turned_ref[place * block : (place + 1) * block, :]
    fill_table(waves, own_places_ref, kept_ref.at[place])
    total = sums_of(kept_ref.at[place], own_ref)
    fill_table(waves, places_ref, table_ref)
    piece_ref[...] = (total + sums_of(table_ref, masked_ref)).astype(piece_ref.dtype)


def fill_edges(lines, last_ref, first_ref):
    slots = last_ref.shape[1]
    for line, rows_ref in enumerate(lines):
        last_ref[line] = rows_ref[rows_ref.shape[0] - slots :, :]
        first_ref[line] = rows_ref[:slots, :]


def rest_kernel(blocks, block, lines, turned_ref, places_ref, _, *refs):
    kept_ref, *outs = refs[lines + 1 if lines else 0 :]
    if lines:
        *edges, radial_ref, semaphores = outs
        source_ref = refs[lines]
        count = source_ref.shape[0]
        copies = begin([source_ref], [radial_ref.at[pl.ds(0, count)]], semaphores)
        radial_ref[count] = jnp.zeros_like(radial_ref[count])
        fill_edges(refs[:lines], *edges)
    for place in blocks:
        fill_table(turned_ref[place * block : (place + 1) * block, :], places_ref, kept_ref.at[place])
    if lines:
        finish(copies)


def short_kernel(lines, codes_ref, radial_ref, *refs):
    line_refs, refs = refs[:lines], refs[lines:]
    outer, (handed_ref, w_ref, message_ref, found_ref) = refs[:-4], refs[-4:]
    cells, slots, channels = message_ref.shape
    pairs = codes_ref.shape[0]
    slab, slabs = lax.axis_index("grp"), lax.axis_size("grp")

    def outer_cell(line, side):
        if slabs == 2:
            start = handed_ref.shape[0] - (4 - 2 * side - (1 - line)) * slots
            return jnp.where(slab == 1, outer[side][line], handed_ref[start : start + slots, :])
        return outer[side][line]

    nothing = cells * pairs
    for cell in range(cells):
        for code in range(9):
            found_ref[9 * cell + code] = nothing
        for pair in range(pairs):
            found_ref[9 * cell + codes_ref[pair, cell]] = cell * pairs + pair
    levels = [1, 2 - 2 * slab] if slabs == 2 else [1, 0, 2]
    carried = None
    for start in range(0, cells + 2, 2):
        takers = [cell for cell in range(start - 2, start + 2) if 0 <= cell < cells]
        total = None
        for line, level in enumerate(levels):
            rows = []
            for cell in takers:
                halves = []
                for place in (start, start + 1):
                    along = place - cell
                    index = found_ref[9 * cell + 3 * level + along] if 0 <= along < 3 else nothing
                    halves.append(radial_ref[index])
                rows.append(jnp.concatenate(halves, axis=1))
            span = slice(max(start - 1, 0) * slots, min(start + 1, cells) * slots)
            taken = [line_refs[line][span, :]]
            if start == 0:
                taken = [outer_cell(line, 0)] + taken
            if start == cells:
                taken = taken + [outer_cell(line, 1)]
            taken = jnp.concatenate(taken, axis=0)
            part = jnp.dot(jnp.concatenate(rows, axis=0), taken, preferred_element_type=F32)
            total = part if total is None else total + part
        if start:
            gathered = (carried + total[: 2 * slots]).astype(BF16)
            message = jnp.dot(gathered, w_ref[...], preferred_element_type=F32)
            message_ref[start - 2 : start] = message.reshape(2, slots, channels)
            total = total[2 * slots :]
        carried = total


def add_kernel(*refs):
    pieces, (total_ref, sent_ref) = refs[:-2], refs[-2:]
    total = pieces[0][...].astype(F32)
    for piece in pieces[1:]:
        total = total + piece[...].astype(F32)
    total_ref[...] = total
    sent_ref[...] = total.astype(sent_ref.dtype)


def added(pieces, held):
    shape = pieces[0].shape
    return call(add_kernel, [(VMEM, (shape, F32)), (VMEM, (shape, BF16))], in_vmem(pieces), held=held)


def mixed(owned, waves, w_mix, factor_scale):
    waves = jnp.where(lax.broadcasted_iota(jnp.int32, waves.shape, 1) < 3, waves, 0.0)
    square = jnp.sum(waves * waves, axis=1, keepdims=True)
    kernel = jnp.exp(-square / 128.0) / (1.0 + square / 64.0)
    factors = (owned * factor_scale).astype(BF16)
    energy = jnp.dot(factors, w_mix, preferred_element_type=F32)
    return (energy * jnp.concatenate([kernel, kernel], axis=0)).astype(BF16)


def energy_kernel(count, factor_scale, *refs):
    pieces = refs[:count]
    turned_ref, w_mix_ref, energy_ref = refs[count:]
    trig, rows, channels = energy_ref.shape
    total = pieces[0][...].astype(F32)
    for piece in pieces[1:]:
        total = total + piece[...].astype(F32)
    owned = total.reshape(trig * rows, channels)
    energy = mixed(owned, turned_ref[:rows, :].astype(F32), w_mix_ref[...], factor_scale)
    energy_ref[...] = energy.reshape(trig, rows, channels)


def energy_of(pieces, turned, w_mix, factor_scale, held):
    (energy,) = call(
        functools.partial(energy_kernel, len(pieces), factor_scale),
        [(VMEM, (pieces[0].shape, BF16))],
        in_vmem([*pieces, turned, w_mix]),
        held=held,
        flops=WEIGHT * 10**9,
    )
    return energy


def stack_kernel(*refs):
    pieces, out_ref = refs[:-1], refs[-1]
    start = 0
    for piece in pieces:
        for part in range(piece.shape[0]):
            out_ref[start : start + piece.shape[1], :] = piece[part]
            start += piece.shape[1]


def stacked(pieces, held):
    rows = sum(piece.shape[0] * piece.shape[1] for piece in pieces)
    (whole,) = call(stack_kernel, [(VMEM, ((rows, pieces[0].shape[2]), BF16))], in_vmem(pieces), held=held)
    return whole


def near_kernel(blocks, *refs):
    energies, (table_ref, out_ref, turned_ref) = refs[:blocks], refs[blocks:]
    for place, energy in enumerate(energies):
        turned_ref[place] = energy[...].astype(F32).T.astype(BF16)
    atoms = out_ref.shape[1]
    tile = math.gcd(atoms, 512)
    for start in range(0, atoms, tile):
        total = None
        for place in range(blocks):
            part = jnp.dot(turned_ref[place], table_ref[place, :, start : start + tile], preferred_element_type=F32)
            total = part if total is None else total + part
        out_ref[:, start : start + tile] = total


def final_kernel(
    blocks, scale, counts_ref, masked_ref, near_ref, message_ref, energy_ref, rest_ref, table_ref, out_ref, turned_ref,
    result_ref, semaphores,
):
    cells, slots, channels = out_ref.shape
    rows = table_ref.shape[1]
    turned_ref[0] = energy_ref[:rows, :].astype(F32).T.astype(BF16)
    for place in range(1, blocks):
        turned_ref[place] = rest_ref[(place - 1) * rows : place * rows, :].astype(F32).T.astype(BF16)
    slot_ids = lax.broadcasted_iota(jnp.int32, (slots, channels), 0)
    group = math.gcd(cells, 2)
    share = math.gcd(cells, 4)
    leaving = []
    for first in range(0, cells, group):
        span = slice(first * slots, (first + group) * slots)
        total = near_ref[:, span]
        for place in range(blocks):
            total = total + jnp.dot(turned_ref[place], table_ref[blocks + place, :, span], preferred_element_type=F32)
        for cell in range(first, first + group):
            value = total[:, (cell - first) * slots : (cell - first + 1) * slots].T * scale + message_ref[cell]
            value = value * (0.5 + 0.5 * jnp.tanh(0.5 * value))
            result = masked_ref[cell * slots : (cell + 1) * slots, :].astype(F32) + value
            result_ref[cell] = jnp.where(slot_ids < counts_ref[cell], result, 0.0).astype(BF16)
        if (first + group) % share == 0:
            done = pl.ds(first + group - share, share)
            leaving += begin([result_ref.at[done]], [out_ref.at[done]], semaphores, first // share)
    finish(leaving)


def final_call(counts, near, message, masked, energy, rest, table, scale):
    blocks, rows = table.shape[0] // 2, table.shape[1]
    cells, slots, channels = message.shape
    (result,) = call(
        functools.partial(final_kernel, blocks, scale),
        [(HBM, (message.shape, BF16))],
        [(SMEM, counts)] + in_vmem([masked, near, message, energy, rest, table]),
        [
            pltpu.VMEM((blocks, channels, rows), BF16),
            pltpu.VMEM(message.shape, BF16),
            pltpu.SemaphoreType.DMA((cells // math.gcd(cells, 4),)),
        ],
    )
    return result


def body(features, offsets, radial, neighbours, counts, wavevectors, w_msg, w_mix):
    _, cells, slots, channels = features.shape
    wave_count = wavevectors.shape[1]
    slabs, dev_count = lax.axis_size("grp"), lax.axis_size("dev")
    slab = lax.axis_index("grp")
    cell_line = cells * dev_count
    total_slots = slabs * cell_line * slots
    atoms = cells * slots
    lengths = (float(cell_line), float(slabs))
    features, offsets, counts = features[0], offsets[0].transpose(1, 0, 2), counts[0]

    swap = pairs_at("grp", 1, 1)
    sibling_offsets = lax.ppermute(offsets, "grp", swap)
    if slabs == 2:
        sibling_counts = lax.ppermute(counts, "grp", swap)
        sibling_features = lax.ppermute(features, "grp", swap)
    else:
        up = [(i, i + 1) for i in range(slabs - 1)]
        down = [(j, i) for i, j in up]
        near = [(lax.ppermute(counts, "grp", way), lax.ppermute(features, "grp", way)) for way in (up, down)]
        even = slab % 2 == 0
        sibling_counts = jnp.where(even, near[1][0], near[0][0])
        sibling_features = jnp.where(even, near[1][1], near[0][1])

    blocks = 4 if dev_count % 4 == 0 else 2
    digits = [("grp", 1, 2), ("dev", 1, blocks)]
    twos = [("dev", blocks << bit) for bit in range((dev_count // blocks).bit_length() - 1)]
    twos += [("grp", 2 << bit) for bit in range((slabs // 2).bit_length() - 1)]
    half = wave_count // 2
    block = half // blocks
    table = ((2 * block, atoms), BF16)
    sums = ((2 * block, channels), F32)
    piece = ((2 * block, channels), BF16)
    places_type = ((32, atoms), BF16)
    rows_type = ((atoms, channels), BF16)
    whole_table = (VMEM, ((2 * blocks,) + table[0], BF16))
    scratch = [pltpu.VMEM(*table)]
    block_flops = 2 * 2 * block * atoms * channels * COST

    def sent(part, place):
        return lax.ppermute(part.reshape(2, block, channels), "dev", pairs_at("dev", 1, place))

    order = [*range(blocks - 1, 0, -1), 0]
    early = order[: min(2, blocks - 1)]
    masked, places, turned, tables, *outs = call(
        functools.partial(own_kernel, early, block, digits, lengths),
        [(VMEM, rows_type), (VMEM, places_type), (VMEM, ((wave_count, 32), BF16)), whole_table]
        + [(VMEM, sums)] * len(early),
        in_hbm([wavevectors, offsets, counts, features]),
        [
            pltpu.VMEM((32, wave_count), F32),
            pltpu.VMEM(wavevectors.shape, jnp.int32),
            pltpu.VMEM(offsets.shape, F32),
            pltpu.SMEM(counts.shape, jnp.int32),
            pltpu.VMEM(features.shape, BF16),
            pltpu.SemaphoreType.DMA((4,)),
        ],
    )
    started = dict(zip(early, outs))
    sibling, sibling_places, part = call(
        functools.partial(sibling_kernel, early[0], block, lengths),
        [(VMEM, rows_type), (VMEM, places_type), (VMEM, piece)],
        [(SMEM, sibling_counts)] + in_vmem([sibling_features, sibling_offsets, turned, started[early[0]]]),
        scratch,
    )
    received = {early[0]: sent(part, early[0])}
    for place in early[1:]:
        (part,) = call(
            functools.partial(continued_kernel, place, block),
            [(VMEM, piece)],
            in_vmem([turned, sibling_places, sibling, started[place]]),
            scratch,
            flops=block_flops,
        )
        received[place] = sent(part, place)
    for place in order[len(early) :]:
        tables, part = call(
            functools.partial(both_kernel, place, block),
            [whole_table, (VMEM, piece if place else sums)],
            in_vmem([turned, places, masked, sibling_places, sibling, tables]),
            scratch,
            [part] if place else [received[early[0]]],
            2 * block_flops,
            {5: 0},
        )
        if place:
            received[place] = sent(part, place)
    pieces = [part.reshape(2, block, channels)] + [received[place] for place in range(1, blocks)]

    if slabs == 2:
        lines = [masked, sibling]
    else:
        lines = [masked] + [
            jnp.where(jnp.arange(slots)[None, :, None] < count[:, None, None], cell, jnp.bfloat16(0)).reshape(
                atoms, channels
            )
            for count, cell in near
        ]
    edge = (VMEM, ((len(lines), slots, channels), BF16))

    def rest_of(tables, first, last, held, more=(), outs=(), scratch=(), weight=0):
        return call(
            functools.partial(rest_kernel, range(first, last), block, len(more[:-1])),
            [whole_table, *outs],
            in_vmem([turned, places, tables, *more[:-1]]) + in_hbm(more[-1:]),
            scratch,
            held,
            weight,
            {2: 0},
        )

    middle = blocks + blocks // 2
    (tables,) = rest_of(tables, blocks, middle, [part])

    total, half_total = added(pieces, [tables])
    radial = radial.reshape(-1, slots, slots)
    radial_type = (VMEM, ((radial.shape[0] + 1, slots, slots), BF16))
    tables, *edges, radial = rest_of(
        tables, middle, 2 * blocks, [total],
        [*lines, radial], [edge, edge, radial_type], [pltpu.SemaphoreType.DMA((1,))],
    )

    right = [(i, i + 1) for i in range(dev_count - 1)]
    left = [(j, i) for i, j in right]
    if slabs == 2:
        outer = [
            lax.ppermute(part, ("grp", "dev"), [(dev_count + i, dev_count + j) for i, j in way])
            for part, way in zip(edges, (right, left))
        ]
    else:
        outer = [lax.ppermute(part, "dev", way) for part, way in zip(edges, (right, left))]

    held = [tables, radial]
    for axis, stride in twos[:-1]:
        total, half_total = added([total, lax.ppermute(half_total, axis, pairs_at(axis, stride, 1))], held)
        held = []
    axis, stride = twos[-1]
    pieces = [total, lax.ppermute(half_total, axis, pairs_at(axis, stride, 1))]
    energy = energy_of(pieces, turned, w_mix, 1.0 / math.sqrt(total_slots), [tables, radial])

    energies = [energy] + [
        lax.ppermute(energy, "dev", pairs_at("dev", 1, place)) for place in range(1, blocks)
    ]
    handed = lax.ppermute(stacked([energy, *(outer if slabs == 2 else [])], [radial]), "grp", swap)

    (message,) = call(
        functools.partial(short_kernel, len(lines)),
        [(VMEM, ((cells, slots, channels), F32))],
        [(SMEM, neighbours[0].T)] + in_vmem([radial, *lines, *outer, handed, w_msg]),
        [pltpu.SMEM((9 * cells,), jnp.int32)],
        [energy, tables],
        6 * block_flops,
    )
    rest = lax.ppermute(stacked(energies[1:], [message]), "grp", swap)
    energies = [part.reshape(2 * block, channels) for part in energies]
    (near_sum,) = call(
        functools.partial(near_kernel, blocks),
        [(VMEM, ((channels, atoms), F32))],
        in_vmem([*energies, tables]),
        [pltpu.VMEM((blocks, channels, 2 * block), BF16)],
        [message],
        2 * block_flops,
    )
    scale = 8.0 / math.sqrt(wave_count)
    result = final_call(counts, near_sum, message, masked, handed, rest, tables, scale)
    return result[None]


def solution(mesh):
    in_specs = (
        P("grp", "dev", None, None),
        P("grp", "dev", None, None),
        P("grp", "dev", None, None, None),
        P("grp", "dev", None),
        P("grp", "dev"),
        P(),
        P(),
        P(),
    )
    out_specs = P("grp", "dev", None, None)
    return jax.shard_map(body, mesh=mesh, in_specs=in_specs, out_specs=out_specs, check_vma=False)
```

```python
import functools
import math

import jax
import jax.numpy as jnp
from jax import lax
from jax.experimental import pallas as pl
from jax.experimental.pallas import tpu as pltpu
from jax.sharding import PartitionSpec as P

F32 = jnp.float32
BF16 = jnp.bfloat16
VMEM = pl.BlockSpec(memory_space=pltpu.VMEM)
SMEM = pl.BlockSpec(memory_space=pltpu.SMEM)
HBM = pl.BlockSpec(memory_space=pltpu.HBM)
PARAMS = pltpu.CompilerParams(vmem_limit_bytes=14 * 1024 * 1024)
LANES = 128
SIN = (4.44287957, -7.30781668, 3.59777418, -0.79119939)
COS = (1.41420401, -6.97763732, 5.71518787, -1.72821389)


def call(kernel, outs, operands, scratch=(), held=(), same=()):
    ahead = len(operands)
    operands = list(operands) + [(VMEM, array) for array in held]

    def without_held(*refs):
        kernel(*refs[:ahead], *refs[len(operands) :])

    return pl.pallas_call(
        without_held,
        in_specs=[place for place, _ in operands],
        out_specs=[place for place, _ in outs],
        out_shape=[place.memory_space(*kind) for place, kind in outs],
        scratch_shapes=list(scratch),
        input_output_aliases=dict(same),
        compiler_params=PARAMS,
        cost_estimate=pl.CostEstimate(flops=0, bytes_accessed=0, transcendentals=0),
    )(
        *[
            array if place is SMEM else pltpu.with_memory_space_constraint(array, place.memory_space)
            for place, array in operands
        ]
    )


def in_vmem(arrays):
    return [(VMEM, array) for array in arrays]


def in_hbm(arrays):
    return [(HBM, array) for array in arrays]


def begin(sources, targets, semaphores, first=0):
    copies = [
        pltpu.make_async_copy(source, target, semaphores.at[first + index])
        for index, (source, target) in enumerate(zip(sources, targets))
    ]
    for copy in copies:
        copy.start()
    return copies


def finish(copies):
    for copy in copies:
        copy.wait()


def pairs_at(axis, stride, offset):
    return [(place, place ^ (offset * stride)) for place in range(lax.axis_size(axis))]


def fill_places(offsets_ref, places_ref, first, slab, cell_line, slabs):
    _, cells, slots = offsets_ref.shape
    line = lax.broadcasted_iota(jnp.int32, (8, slots), 0)
    along_z_base = slab.astype(F32)
    for cell in range(cells):
        along_x = ((first + cell).astype(F32) + offsets_ref[0, cell : cell + 1]) / cell_line
        along_y = offsets_ref[1, cell : cell + 1]
        along_z = (along_z_base + offsets_ref[2, cell : cell + 1]) / slabs
        full = jnp.where(line == 0, along_x, jnp.where(line == 1, along_y, jnp.where(line == 2, along_z, 0.0)))
        high = full.astype(BF16).astype(F32)
        middle = (full - high).astype(BF16).astype(F32)
        low = full - high - middle
        parts = jnp.concatenate([high, middle, low, jnp.zeros_like(low)], axis=0)
        places_ref[:, cell * slots : (cell + 1) * slots] = parts.astype(BF16)


def fill_masked(counts_ref, features_ref, masked_ref):
    cells, slots, channels = features_ref.shape
    slot_ids = lax.broadcasted_iota(jnp.int32, (slots, channels), 0)
    for cell in range(cells):
        kept = jnp.where(slot_ids < counts_ref[cell], features_ref[cell].astype(F32), 0.0)
        masked_ref[cell * slots : (cell + 1) * slots, :] = kept.astype(BF16)


def fill_waves(waves_ref, padded_ref, turned_ref, flips):
    count = waves_ref.shape[1]
    waves = waves_ref[...].astype(F32)
    padded_ref[...] = jnp.zeros_like(padded_ref)
    for part in range(3):
        padded_ref[8 * part : 8 * part + 3, :] = waves
    rows = lax.broadcasted_iota(jnp.int32, (LANES, LANES), 0)
    columns = lax.broadcasted_iota(jnp.int32, (LANES, LANES), 1)
    order = jnp.where((rows ^ (flips & (LANES - 1))) == columns, 1.0, 0.0).astype(BF16)
    for block in range(count // LANES):
        source = pl.multiple_of((block ^ (flips // LANES)) * LANES, LANES)
        taken = padded_ref[:, pl.ds(source, LANES)].astype(BF16)
        turned = lax.dot_general(order, taken, (((1,), (1,)), ((), ())), preferred_element_type=F32)
        turned_ref[block * LANES : (block + 1) * LANES, :] = turned.astype(BF16)


def fill_table(waves, places_ref, table_ref):
    block = waves.shape[0]
    atoms = places_ref.shape[1]
    tile = math.gcd(atoms, 256)
    for start in range(0, atoms, tile):
        span = slice(start, start + tile)
        turns = jnp.dot(waves, places_ref[:, span], preferred_element_type=F32)
        part = turns - jnp.round(turns)
        square = part * part
        sine = part * (SIN[0] + square * (SIN[1] + square * (SIN[2] + square * SIN[3])))
        cosine = COS[0] + square * (COS[1] + square * (COS[2] + square * COS[3]))
        table_ref[:block, span] = (1.0 - sine * sine).astype(BF16)
        table_ref[block:, span] = (sine * cosine).astype(BF16)


def sums_of(table_ref, rows_ref):
    return jnp.dot(table_ref[...], rows_ref[...], preferred_element_type=F32)


def own_kernel(early, block, digits, lengths, *refs):
    sources, refs = refs[:4], refs[4:]
    masked_ref, places_ref, turned_ref, table_ref = refs[:4]
    sums = refs[4 : 4 + len(early)]
    padded_ref, waves_ref, offsets_ref, counts_ref, features_ref, semaphores = refs[4 + len(early) :]
    copies = begin(sources, (waves_ref, offsets_ref, counts_ref, features_ref), semaphores)
    cells = features_ref.shape[0]
    dev, slab = lax.axis_index("dev"), lax.axis_index("grp")
    flips = jnp.int32(0)
    weight = waves_ref.shape[1]
    for axis, stride, radix in digits:
        weight //= radix
        flips += ((slab if axis == "grp" else dev) // stride % radix) * weight
    copies[0].wait()
    fill_waves(waves_ref, padded_ref, turned_ref, flips)
    copies[1].wait()
    fill_places(offsets_ref, places_ref, dev * cells, slab, *lengths)
    copies[2].wait()
    copies[3].wait()
    fill_masked(counts_ref, features_ref, masked_ref)
    for place, sums_ref in zip(early, sums):
        fill_table(turned_ref[place * block : (place + 1) * block, :], places_ref, table_ref.at[place])
        sums_ref[...] = sums_of(table_ref.at[place], masked_ref)


def sibling_kernel(
    place, block, lengths, counts_ref, features_ref, offsets_ref, turned_ref, start_ref,
    masked_ref, places_ref, piece_ref, table_ref,
):
    cells = features_ref.shape[0]
    fill_places(offsets_ref, places_ref, lax.axis_index("dev") * cells, lax.axis_index("grp") ^ 1, *lengths)
    fill_masked(counts_ref, features_ref, masked_ref)
    fill_table(turned_ref[place * block : (place + 1) * block, :], places_ref, table_ref)
    piece_ref[...] = (start_ref[...] + sums_of(table_ref, masked_ref)).astype(piece_ref.dtype)


def continued_kernel(place, block, turned_ref, places_ref, masked_ref, start_ref, piece_ref, table_ref):
    fill_table(turned_ref[place * block : (place + 1) * block, :], places_ref, table_ref)
    piece_ref[...] = (start_ref[...] + sums_of(table_ref, masked_ref)).astype(piece_ref.dtype)


def both_kernel(
    place, block, turned_ref, own_places_ref, own_ref, places_ref, masked_ref, _, kept_ref, piece_ref, table_ref
):
    waves = turned_ref[place * block : (place + 1) * block, :]
    fill_table(waves, own_places_ref, kept_ref.at[place])
    total = sums_of(kept_ref.at[place], own_ref)
    fill_table(waves, places_ref, table_ref)
    piece_ref[...] = (total + sums_of(table_ref, masked_ref)).astype(piece_ref.dtype)


def fill_edges(lines, last_ref, first_ref):
    slots = last_ref.shape[1]
    for line, rows_ref in enumerate(lines):
        last_ref[line] = rows_ref[rows_ref.shape[0] - slots :, :]
        first_ref[line] = rows_ref[:slots, :]


def rest_kernel(blocks, block, lines, turned_ref, places_ref, _, *refs):
    kept_ref, *outs = refs[lines + 1 if lines else 0 :]
    if lines:
        *edges, radial_ref, semaphores = outs
        source_ref = refs[lines]
        count = source_ref.shape[0]
        copies = begin([source_ref], [radial_ref.at[pl.ds(0, count)]], semaphores)
        radial_ref[count] = jnp.zeros_like(radial_ref[count])
        fill_edges(refs[:lines], *edges)
    for place in blocks:
        fill_table(turned_ref[place * block : (place + 1) * block, :], places_ref, kept_ref.at[place])
    if lines:
        finish(copies)


def fill_found(codes_ref, found_ref):
    pairs, cells = codes_ref.shape
    for cell in range(cells):
        for code in range(9):
            found_ref[9 * cell + code] = cells * pairs
        for pair in range(pairs):
            found_ref[9 * cell + codes_ref[pair, cell]] = cell * pairs + pair


def window_sum(start, radial_ref, found_ref, lines, takers):
    slab, slabs = lax.axis_index("grp"), lax.axis_size("grp")
    nothing = radial_ref.shape[0] - 1
    levels = [1, 2 - 2 * slab] if slabs == 2 else [1, 0, 2]
    total = None
    for level, taken in zip(levels, lines):
        rows = []
        for cell in takers:
            halves = []
            for place in (start, start + 1):
                along = place - cell
                index = found_ref[9 * cell + 3 * level + along] if 0 <= along < 3 else nothing
                halves.append(radial_ref[index])
            rows.append(jnp.concatenate(halves, axis=1))
        part = jnp.dot(jnp.concatenate(rows, axis=0), taken, preferred_element_type=F32)
        total = part if total is None else total + part
    return total


def short_kernel(lines, codes_ref, radial_ref, *refs):
    line_refs, (w_ref, message_ref, found_ref) = refs[:lines], refs[lines:]
    cells, slots, channels = message_ref.shape
    fill_found(codes_ref, found_ref)
    carried = None
    for start in range(2, cells, 2):
        taken = [line_ref[(start - 1) * slots : (start + 1) * slots, :] for line_ref in line_refs]
        total = window_sum(start, radial_ref, found_ref, taken, range(start - 2, start + 2))
        gathered = total[: 2 * slots]
        if start > 2:
            gathered = carried + gathered
            gathered = jnp.dot(gathered.astype(BF16), w_ref[...], preferred_element_type=F32)
        message_ref[start - 2 : start] = gathered.reshape(2, slots, channels)
        carried = total[2 * slots :]
    message_ref[cells - 2 : cells] = carried.reshape(2, slots, channels)


def fill_ends(slots, codes_ref, radial_ref, line_refs, outer, handed_ref, base, w_ref, found_ref, ends_ref):
    slab, slabs = lax.axis_index("grp"), lax.axis_size("grp")
    cells = codes_ref.shape[1]
    fill_found(codes_ref, found_ref)
    for side, start in enumerate((0, cells)):
        taken = []
        for line, line_ref in enumerate(line_refs):
            cell = outer[side][line]
            if slabs == 2:
                first = base + (2 * side + 1 - line) * slots
                cell = jnp.where(slab == 1, cell, handed_ref[first : first + slots, :])
            if side == 0:
                taken.append(jnp.concatenate([cell, line_ref[:slots, :]], axis=0))
            else:
                taken.append(jnp.concatenate([line_ref[(cells - 1) * slots :, :], cell], axis=0))
        takers = (0, 1) if side == 0 else (cells - 2, cells - 1)
        total = window_sum(start, radial_ref, found_ref, taken, takers)
        span = slice(2 * side, 2 * side + 2)
        gathered = ends_ref[span].reshape(total.shape) + total
        message = jnp.dot(gathered.astype(BF16), w_ref[...], preferred_element_type=F32)
        ends_ref[span] = message.reshape(2, slots, total.shape[1])


def add_kernel(*refs):
    pieces, (total_ref, sent_ref) = refs[:-2], refs[-2:]
    total = pieces[0][...].astype(F32)
    for piece in pieces[1:]:
        total = total + piece[...].astype(F32)
    total_ref[...] = total
    sent_ref[...] = total.astype(sent_ref.dtype)


def added(pieces, held):
    shape = pieces[0].shape
    return call(add_kernel, [(VMEM, (shape, F32)), (VMEM, (shape, BF16))], in_vmem(pieces), held=held)


def mixed(owned, waves, w_mix, factor_scale):
    waves = jnp.where(lax.broadcasted_iota(jnp.int32, waves.shape, 1) < 3, waves, 0.0)
    square = jnp.sum(waves * waves, axis=1, keepdims=True)
    kernel = jnp.exp(-square / 128.0) / (1.0 + square / 64.0)
    factors = (owned * factor_scale).astype(BF16)
    energy = jnp.dot(factors, w_mix, preferred_element_type=F32)
    return (energy * jnp.concatenate([kernel, kernel], axis=0)).astype(BF16)


def energy_kernel(count, factor_scale, *refs):
    pieces = refs[:count]
    turned_ref, w_mix_ref, energy_ref = refs[count:]
    trig, rows, channels = energy_ref.shape
    total = pieces[0][...].astype(F32)
    for piece in pieces[1:]:
        total = total + piece[...].astype(F32)
    owned = total.reshape(trig * rows, channels)
    energy = mixed(owned, turned_ref[:rows, :].astype(F32), w_mix_ref[...], factor_scale)
    energy_ref[...] = energy.reshape(trig, rows, channels)


def energy_of(pieces, turned, w_mix, factor_scale, held):
    (energy,) = call(
        functools.partial(energy_kernel, len(pieces), factor_scale),
        [(VMEM, (pieces[0].shape, BF16))],
        in_vmem([*pieces, turned, w_mix]),
        held=held,
    )
    return energy


def stack_kernel(*refs):
    pieces, out_ref = refs[:-1], refs[-1]
    start = 0
    for piece in pieces:
        for part in range(piece.shape[0]):
            out_ref[start : start + piece.shape[1], :] = piece[part]
            start += piece.shape[1]


def stacked(pieces, held):
    rows = sum(piece.shape[0] * piece.shape[1] for piece in pieces)
    (whole,) = call(stack_kernel, [(VMEM, ((rows, pieces[0].shape[2]), BF16))], in_vmem(pieces), held=held)
    return whole


def near_kernel(blocks, *refs):
    energies, (table_ref, out_ref, turned_ref) = refs[:blocks], refs[blocks:]
    for place, energy in enumerate(energies):
        turned_ref[place] = energy[...].astype(F32).T.astype(BF16)
    atoms = out_ref.shape[1]
    tile = math.gcd(atoms, 512)
    for start in range(0, atoms, tile):
        total = None
        for place in range(blocks):
            part = jnp.dot(turned_ref[place], table_ref[place, :, start : start + tile], preferred_element_type=F32)
            total = part if total is None else total + part
        out_ref[:, start : start + tile] = total


def final_kernel(blocks, lines, scale, counts_ref, codes_ref, near_ref, message_ref, handed_ref, table_ref, *refs):
    radial_ref, line_refs, outer, w_ref = refs[0], refs[1 : 1 + lines], refs[1 + lines : 3 + lines], refs[3 + lines]
    out_ref, turned_ref, result_ref, found_ref, ends_ref, semaphores = refs[4 + lines :]
    masked_ref = line_refs[0]
    cells, slots, channels = out_ref.shape
    rows = table_ref.shape[1]
    for place in range(blocks):
        turned_ref[place] = handed_ref[place * rows : (place + 1) * rows, :].astype(F32).T.astype(BF16)
    ends_ref[:2] = message_ref[:2]
    ends_ref[2:] = message_ref[cells - 2 :]
    fill_ends(
        slots, codes_ref, radial_ref, line_refs, outer, handed_ref, blocks * rows, w_ref, found_ref, ends_ref
    )
    slot_ids = lax.broadcasted_iota(jnp.int32, (slots, channels), 0)
    group = math.gcd(cells, 2)
    share = math.gcd(cells, 4)
    leaving = []
    for first in range(0, cells, group):
        span = slice(first * slots, (first + group) * slots)
        total = near_ref[:, span]
        for place in range(blocks):
            total = total + jnp.dot(turned_ref[place], table_ref[blocks + place, :, span], preferred_element_type=F32)
        for cell in range(first, first + group):
            value = total[:, (cell - first) * slots : (cell - first + 1) * slots].T * scale
            value += ends_ref[cell] if cell < 2 else ends_ref[cell - cells + 4] if cell >= cells - 2 else message_ref[cell]
            value = value * (0.5 + 0.5 * jnp.tanh(0.5 * value))
            result = masked_ref[cell * slots : (cell + 1) * slots, :].astype(F32) + value
            result_ref[cell] = jnp.where(slot_ids < counts_ref[cell], result, 0.0).astype(BF16)
        if (first + group) % share == 0:
            done = pl.ds(first + group - share, share)
            leaving += begin([result_ref.at[done]], [out_ref.at[done]], semaphores, first // share)
    finish(leaving)


def final_call(counts, codes, near, message, handed, table, radial, lines, outer, w_msg, scale):
    blocks, rows = table.shape[0] // 2, table.shape[1]
    cells, slots, channels = message.shape
    (result,) = call(
        functools.partial(final_kernel, blocks, len(lines), scale),
        [(HBM, (message.shape, BF16))],
        [(SMEM, counts), (SMEM, codes)] + in_vmem([near, message, handed, table, radial, *lines, *outer, w_msg]),
        [
            pltpu.VMEM((blocks, channels, rows), BF16),
            pltpu.VMEM(message.shape, BF16),
            pltpu.SMEM((9 * cells,), jnp.int32),
            pltpu.VMEM((4, slots, channels), F32),
            pltpu.SemaphoreType.DMA((cells // math.gcd(cells, 4),)),
        ],
    )
    return result


def body(features, offsets, radial, neighbours, counts, wavevectors, w_msg, w_mix):
    _, cells, slots, channels = features.shape
    wave_count = wavevectors.shape[1]
    slabs, dev_count = lax.axis_size("grp"), lax.axis_size("dev")
    slab = lax.axis_index("grp")
    cell_line = cells * dev_count
    total_slots = slabs * cell_line * slots
    atoms = cells * slots
    lengths = (float(cell_line), float(slabs))
    features, offsets, counts = features[0], offsets[0].transpose(1, 0, 2), counts[0]

    swap = pairs_at("grp", 1, 1)
    sibling_offsets = lax.ppermute(offsets, "grp", swap)
    if slabs == 2:
        sibling_counts = lax.ppermute(counts, "grp", swap)
        sibling_features = lax.ppermute(features, "grp", swap)
    else:
        up = [(i, i + 1) for i in range(slabs - 1)]
        down = [(j, i) for i, j in up]
        near = [(lax.ppermute(counts, "grp", way), lax.ppermute(features, "grp", way)) for way in (up, down)]
        even = slab % 2 == 0
        sibling_counts = jnp.where(even, near[1][0], near[0][0])
        sibling_features = jnp.where(even, near[1][1], near[0][1])

    blocks = 4 if dev_count % 4 == 0 else 2
    digits = [("grp", 1, 2), ("dev", 1, blocks)]
    twos = [("dev", blocks << bit) for bit in range((dev_count // blocks).bit_length() - 1)]
    twos += [("grp", 2 << bit) for bit in range((slabs // 2).bit_length() - 1)]
    half = wave_count // 2
    block = half // blocks
    table = ((2 * block, atoms), BF16)
    sums = ((2 * block, channels), F32)
    piece = ((2 * block, channels), BF16)
    places_type = ((32, atoms), BF16)
    rows_type = ((atoms, channels), BF16)
    whole_table = (VMEM, ((2 * blocks,) + table[0], BF16))
    scratch = [pltpu.VMEM(*table)]

    def sent(part, place):
        return lax.ppermute(part.reshape(2, block, channels), "dev", pairs_at("dev", 1, place))

    order = [*range(blocks - 1, 0, -1), 0]
    early = order[: min(2, blocks - 1)]
    masked, places, turned, tables, *outs = call(
        functools.partial(own_kernel, early, block, digits, lengths),
        [(VMEM, rows_type), (VMEM, places_type), (VMEM, ((wave_count, 32), BF16)), whole_table]
        + [(VMEM, sums)] * len(early),
        in_hbm([wavevectors, offsets, counts, features]),
        [
            pltpu.VMEM((32, wave_count), F32),
            pltpu.VMEM(wavevectors.shape, jnp.int32),
            pltpu.VMEM(offsets.shape, F32),
            pltpu.SMEM(counts.shape, jnp.int32),
            pltpu.VMEM(features.shape, BF16),
            pltpu.SemaphoreType.DMA((4,)),
        ],
    )
    started = dict(zip(early, outs))
    sibling, sibling_places, part = call(
        functools.partial(sibling_kernel, early[0], block, lengths),
        [(VMEM, rows_type), (VMEM, places_type), (VMEM, piece)],
        [(SMEM, sibling_counts)] + in_vmem([sibling_features, sibling_offsets, turned, started[early[0]]]),
        scratch,
    )
    received = {early[0]: sent(part, early[0])}
    for place in early[1:]:
        (part,) = call(
            functools.partial(continued_kernel, place, block),
            [(VMEM, piece)],
            in_vmem([turned, sibling_places, sibling, started[place]]),
            scratch,
        )
        received[place] = sent(part, place)
    for place in order[len(early) :]:
        tables, part = call(
            functools.partial(both_kernel, place, block),
            [whole_table, (VMEM, piece if place else sums)],
            in_vmem([turned, places, masked, sibling_places, sibling, tables]),
            scratch,
            [part] if place else [received[early[0]]],
            same={5: 0},
        )
        if place:
            received[place] = sent(part, place)
    pieces = [part.reshape(2, block, channels)] + [received[place] for place in range(1, blocks)]

    if slabs == 2:
        lines = [masked, sibling]
    else:
        lines = [masked] + [
            jnp.where(jnp.arange(slots)[None, :, None] < count[:, None, None], cell, jnp.bfloat16(0)).reshape(
                atoms, channels
            )
            for count, cell in near
        ]
    edge = (VMEM, ((len(lines), slots, channels), BF16))

    def rest_of(tables, first, last, held, more=(), outs=(), scratch=()):
        return call(
            functools.partial(rest_kernel, range(first, last), block, len(more[:-1])),
            [whole_table, *outs],
            in_vmem([turned, places, tables, *more[:-1]]) + in_hbm(more[-1:]),
            scratch,
            held,
            {2: 0},
        )

    middle = blocks + blocks // 2
    (tables,) = rest_of(tables, blocks, middle, [part])

    total, half_total = added(pieces, [tables])
    radial = radial.reshape(-1, slots, slots)
    radial_type = (VMEM, ((radial.shape[0] + 1, slots, slots), BF16))
    tables, *edges, radial = rest_of(
        tables, middle, 2 * blocks, [total],
        [*lines, radial], [edge, edge, radial_type], [pltpu.SemaphoreType.DMA((1,))],
    )

    right = [(i, i + 1) for i in range(dev_count - 1)]
    left = [(j, i) for i, j in right]
    if slabs == 2:
        outer = [
            lax.ppermute(part, ("grp", "dev"), [(dev_count + i, dev_count + j) for i, j in way])
            for part, way in zip(edges, (right, left))
        ]
    else:
        outer = [lax.ppermute(part, "dev", way) for part, way in zip(edges, (right, left))]

    held = [tables, radial]
    for axis, stride in twos[:-1]:
        total, half_total = added([total, lax.ppermute(half_total, axis, pairs_at(axis, stride, 1))], held)
        held = []
    axis, stride = twos[-1]
    pieces = [total, lax.ppermute(half_total, axis, pairs_at(axis, stride, 1))]
    energy = energy_of(pieces, turned, w_mix, 1.0 / math.sqrt(total_slots), [tables, radial])

    energies = [energy] + [
        lax.ppermute(energy, "dev", pairs_at("dev", 1, place)) for place in range(1, blocks)
    ]

    codes = neighbours[0].T
    (message,) = call(
        functools.partial(short_kernel, len(lines)),
        [(VMEM, ((cells, slots, channels), F32))],
        [(SMEM, codes)] + in_vmem([radial, *lines, w_msg]),
        [pltpu.SMEM((9 * cells,), jnp.int32)],
        [energy, tables],
    )
    handed = lax.ppermute(stacked([*energies, *(outer if slabs == 2 else [])], [message]), "grp", swap)
    energies = [part.reshape(2 * block, channels) for part in energies]
    (near_sum,) = call(
        functools.partial(near_kernel, blocks),
        [(VMEM, ((channels, atoms), F32))],
        in_vmem([*energies, tables]),
        [pltpu.VMEM((blocks, channels, 2 * block), BF16)],
        [message],
    )
    scale = 8.0 / math.sqrt(wave_count)
    result = final_call(counts, codes, near_sum, message, handed, tables, radial, lines, outer, w_msg, scale)
    return result[None]


def solution(mesh):
    in_specs = (
        P("grp", "dev", None, None),
        P("grp", "dev", None, None),
        P("grp", "dev", None, None, None),
        P("grp", "dev", None),
        P("grp", "dev"),
        P(),
        P(),
        P(),
    )
    out_specs = P("grp", "dev", None, None)
    return jax.shard_map(body, mesh=mesh, in_specs=in_specs, out_specs=out_specs, check_vma=False)
```

```python
import functools
import math

import jax
import jax.numpy as jnp
from jax import lax
from jax.experimental import pallas as pl
from jax.experimental.pallas import tpu as pltpu
from jax.sharding import PartitionSpec as P

F32 = jnp.float32
BF16 = jnp.bfloat16
VMEM = pl.BlockSpec(memory_space=pltpu.VMEM)
SMEM = pl.BlockSpec(memory_space=pltpu.SMEM)
HBM = pl.BlockSpec(memory_space=pltpu.HBM)
PARAMS = pltpu.CompilerParams(vmem_limit_bytes=14 * 1024 * 1024)
LANES = 128
SIN = (4.44287957, -7.30781668, 3.59777418, -0.79119939)
COS = (1.41420401, -6.97763732, 5.71518787, -1.72821389)


def call(kernel, outs, operands, scratch=(), held=(), same=()):
    ahead = len(operands)
    operands = list(operands) + [(VMEM, array) for array in held]

    def without_held(*refs):
        kernel(*refs[:ahead], *refs[len(operands) :])

    return pl.pallas_call(
        without_held,
        in_specs=[place for place, _ in operands],
        out_specs=[place for place, _ in outs],
        out_shape=[place.memory_space(*kind) for place, kind in outs],
        scratch_shapes=list(scratch),
        input_output_aliases=dict(same),
        compiler_params=PARAMS,
        cost_estimate=pl.CostEstimate(flops=0, bytes_accessed=0, transcendentals=0),
    )(
        *[
            array if place is SMEM else pltpu.with_memory_space_constraint(array, place.memory_space)
            for place, array in operands
        ]
    )


def in_vmem(arrays):
    return [(VMEM, array) for array in arrays]


def in_hbm(arrays):
    return [(HBM, array) for array in arrays]


def begin(sources, targets, semaphores, first=0):
    copies = [
        pltpu.make_async_copy(source, target, semaphores.at[first + index])
        for index, (source, target) in enumerate(zip(sources, targets))
    ]
    for copy in copies:
        copy.start()
    return copies


def finish(copies):
    for copy in copies:
        copy.wait()


def pairs_at(axis, stride, offset):
    return [(place, place ^ (offset * stride)) for place in range(lax.axis_size(axis))]


def fill_places(offsets_ref, places_ref, first, slab, cell_line, slabs):
    _, cells, slots = offsets_ref.shape
    line = lax.broadcasted_iota(jnp.int32, (8, slots), 0)
    along_z_base = slab.astype(F32)
    for cell in range(cells):
        along_x = ((first + cell).astype(F32) + offsets_ref[0, cell : cell + 1]) / cell_line
        along_y = offsets_ref[1, cell : cell + 1]
        along_z = (along_z_base + offsets_ref[2, cell : cell + 1]) / slabs
        full = jnp.where(line == 0, along_x, jnp.where(line == 1, along_y, jnp.where(line == 2, along_z, 0.0)))
        high = full.astype(BF16).astype(F32)
        middle = (full - high).astype(BF16).astype(F32)
        low = full - high - middle
        parts = jnp.concatenate([high, middle, low, jnp.zeros_like(low)], axis=0)
        places_ref[:, cell * slots : (cell + 1) * slots] = parts.astype(BF16)


def fill_masked(counts_ref, features_ref, masked_ref):
    cells, slots, channels = features_ref.shape
    slot_ids = lax.broadcasted_iota(jnp.int32, (slots, channels), 0)
    for cell in range(cells):
        kept = jnp.where(slot_ids < counts_ref[cell], features_ref[cell].astype(F32), 0.0)
        masked_ref[cell * slots : (cell + 1) * slots, :] = kept.astype(BF16)


def fill_waves(waves_ref, padded_ref, turned_ref, flips):
    count = waves_ref.shape[1]
    waves = waves_ref[...].astype(F32)
    padded_ref[...] = jnp.zeros_like(padded_ref)
    for part in range(3):
        padded_ref[8 * part : 8 * part + 3, :] = waves
    rows = lax.broadcasted_iota(jnp.int32, (LANES, LANES), 0)
    columns = lax.broadcasted_iota(jnp.int32, (LANES, LANES), 1)
    order = jnp.where((rows ^ (flips & (LANES - 1))) == columns, 1.0, 0.0).astype(BF16)
    for block in range(count // LANES):
        source = pl.multiple_of((block ^ (flips // LANES)) * LANES, LANES)
        taken = padded_ref[:, pl.ds(source, LANES)].astype(BF16)
        turned = lax.dot_general(order, taken, (((1,), (1,)), ((), ())), preferred_element_type=F32)
        turned_ref[block * LANES : (block + 1) * LANES, :] = turned.astype(BF16)


def fill_table(waves, places_ref, table_ref):
    block = waves.shape[0]
    atoms = places_ref.shape[1]
    tile = math.gcd(atoms, 256)
    for start in range(0, atoms, tile):
        span = slice(start, start + tile)
        turns = jnp.dot(waves, places_ref[:, span], preferred_element_type=F32)
        part = turns - jnp.round(turns)
        square = part * part
        sine = part * (SIN[0] + square * (SIN[1] + square * (SIN[2] + square * SIN[3])))
        cosine = COS[0] + square * (COS[1] + square * (COS[2] + square * COS[3]))
        table_ref[:block, span] = (1.0 - sine * sine).astype(BF16)
        table_ref[block:, span] = (sine * cosine).astype(BF16)


def sums_of(table_ref, rows_ref):
    return jnp.dot(table_ref[...], rows_ref[...], preferred_element_type=F32)


def own_kernel(early, block, digits, lengths, *refs):
    sources, refs = refs[:4], refs[4:]
    masked_ref, places_ref, turned_ref, table_ref = refs[:4]
    sums = refs[4 : 4 + len(early)]
    padded_ref, waves_ref, offsets_ref, counts_ref, features_ref, semaphores = refs[4 + len(early) :]
    copies = begin(sources, (waves_ref, offsets_ref, counts_ref, features_ref), semaphores)
    cells = features_ref.shape[0]
    dev, slab = lax.axis_index("dev"), lax.axis_index("grp")
    flips = jnp.int32(0)
    weight = waves_ref.shape[1]
    for axis, stride, radix in digits:
        weight //= radix
        flips += ((slab if axis == "grp" else dev) // stride % radix) * weight
    copies[0].wait()
    fill_waves(waves_ref, padded_ref, turned_ref, flips)
    copies[1].wait()
    fill_places(offsets_ref, places_ref, dev * cells, slab, *lengths)
    copies[2].wait()
    copies[3].wait()
    fill_masked(counts_ref, features_ref, masked_ref)
    for place, sums_ref in zip(early, sums):
        fill_table(turned_ref[place * block : (place + 1) * block, :], places_ref, table_ref.at[place])
        sums_ref[...] = sums_of(table_ref.at[place], masked_ref)


def sibling_kernel(
    place, block, lengths, counts_ref, features_ref, offsets_ref, turned_ref, start_ref,
    masked_ref, places_ref, piece_ref, table_ref,
):
    cells = features_ref.shape[0]
    fill_places(offsets_ref, places_ref, lax.axis_index("dev") * cells, lax.axis_index("grp") ^ 1, *lengths)
    fill_masked(counts_ref, features_ref, masked_ref)
    fill_table(turned_ref[place * block : (place + 1) * block, :], places_ref, table_ref)
    piece_ref[...] = (start_ref[...] + sums_of(table_ref, masked_ref)).astype(piece_ref.dtype)


def continued_kernel(place, block, turned_ref, places_ref, masked_ref, start_ref, piece_ref, table_ref):
    fill_table(turned_ref[place * block : (place + 1) * block, :], places_ref, table_ref)
    piece_ref[...] = (start_ref[...] + sums_of(table_ref, masked_ref)).astype(piece_ref.dtype)


def both_kernel(
    place, block, turned_ref, own_places_ref, own_ref, places_ref, masked_ref, _, kept_ref, piece_ref, table_ref
):
    waves = turned_ref[place * block : (place + 1) * block, :]
    fill_table(waves, own_places_ref, kept_ref.at[place])
    total = sums_of(kept_ref.at[place], own_ref)
    fill_table(waves, places_ref, table_ref)
    piece_ref[...] = (total + sums_of(table_ref, masked_ref)).astype(piece_ref.dtype)


def fill_edges(lines, last_ref, first_ref):
    slots = last_ref.shape[1]
    for line, rows_ref in enumerate(lines):
        last_ref[line] = rows_ref[rows_ref.shape[0] - slots :, :]
        first_ref[line] = rows_ref[:slots, :]


def rest_kernel(blocks, block, lines, turned_ref, places_ref, _, *refs):
    kept_ref, *outs = refs[lines + 1 if lines else 0 :]
    if lines:
        *edges, radial_ref, semaphores = outs
        source_ref = refs[lines]
        count = source_ref.shape[0]
        copies = begin([source_ref], [radial_ref.at[pl.ds(0, count)]], semaphores)
        radial_ref[count] = jnp.zeros_like(radial_ref[count])
        fill_edges(refs[:lines], *edges)
    for place in blocks:
        fill_table(turned_ref[place * block : (place + 1) * block, :], places_ref, kept_ref.at[place])
    if lines:
        finish(copies)


def fill_found(codes_ref, found_ref, wanted):
    pairs, cells = codes_ref.shape
    for cell in wanted:
        for code in range(9):
            found_ref[9 * cell + code] = cells * pairs
        for pair in range(pairs):
            found_ref[9 * cell + codes_ref[pair, cell]] = cell * pairs + pair


def window_sum(start, radial_ref, found_ref, lines, takers):
    slab, slabs = lax.axis_index("grp"), lax.axis_size("grp")
    nothing = radial_ref.shape[0] - 1
    levels = [1, 2 - 2 * slab] if slabs == 2 else [1, 0, 2]
    total = None
    for level, taken in zip(levels, lines):
        rows = []
        for cell in takers:
            halves = []
            for place in (start, start + 1):
                along = place - cell
                index = found_ref[9 * cell + 3 * level + along] if 0 <= along < 3 else nothing
                halves.append(radial_ref[index])
            rows.append(jnp.concatenate(halves, axis=1))
        part = jnp.dot(jnp.concatenate(rows, axis=0), taken, preferred_element_type=F32)
        total = part if total is None else total + part
    return total


def short_kernel(lines, codes_ref, radial_ref, *refs):
    line_refs, (w_ref, message_ref, found_ref) = refs[:lines], refs[lines:]
    cells, slots, channels = message_ref.shape
    fill_found(codes_ref, found_ref, range(cells))
    carried = None
    for start in range(2, cells, 2):
        taken = [line_ref[(start - 1) * slots : (start + 1) * slots, :] for line_ref in line_refs]
        total = window_sum(start, radial_ref, found_ref, taken, range(start - 2, start + 2))
        gathered = total[: 2 * slots]
        if start > 2:
            gathered = carried + gathered
            gathered = jnp.dot(gathered.astype(BF16), w_ref[...], preferred_element_type=F32)
        message_ref[start - 2 : start] = gathered.reshape(2, slots, channels)
        carried = total[2 * slots :]
    message_ref[cells - 2 : cells] = carried.reshape(2, slots, channels)


def fill_ends(slots, codes_ref, radial_ref, line_refs, outer, handed_ref, base, w_ref, found_ref, ends_ref):
    slab, slabs = lax.axis_index("grp"), lax.axis_size("grp")
    cells = codes_ref.shape[1]
    fill_found(codes_ref, found_ref, (0, 1, cells - 2, cells - 1))
    for side, start in enumerate((0, cells)):
        taken = []
        for line, line_ref in enumerate(line_refs):
            cell = outer[side][line]
            if slabs == 2:
                first = base + (2 * side + 1 - line) * slots
                cell = jnp.where(slab == 1, cell, handed_ref[first : first + slots, :])
            if side == 0:
                taken.append(jnp.concatenate([cell, line_ref[:slots, :]], axis=0))
            else:
                taken.append(jnp.concatenate([line_ref[(cells - 1) * slots :, :], cell], axis=0))
        takers = (0, 1) if side == 0 else (cells - 2, cells - 1)
        total = window_sum(start, radial_ref, found_ref, taken, takers)
        span = slice(2 * side, 2 * side + 2)
        gathered = ends_ref[span].reshape(total.shape) + total
        message = jnp.dot(gathered.astype(BF16), w_ref[...], preferred_element_type=F32)
        ends_ref[span] = message.reshape(2, slots, total.shape[1])


def add_kernel(*refs):
    pieces, (total_ref, sent_ref) = refs[:-2], refs[-2:]
    total = pieces[0][...].astype(F32)
    for piece in pieces[1:]:
        total = total + piece[...].astype(F32)
    total_ref[...] = total
    sent_ref[...] = total.astype(sent_ref.dtype)


def added(pieces, held):
    shape = pieces[0].shape
    return call(add_kernel, [(VMEM, (shape, F32)), (VMEM, (shape, BF16))], in_vmem(pieces), held=held)


def mixed(owned, waves, w_mix, factor_scale):
    waves = jnp.where(lax.broadcasted_iota(jnp.int32, waves.shape, 1) < 3, waves, 0.0)
    square = jnp.sum(waves * waves, axis=1, keepdims=True)
    kernel = jnp.exp(-square / 128.0) / (1.0 + square / 64.0)
    factors = (owned * factor_scale).astype(BF16)
    energy = jnp.dot(factors, w_mix, preferred_element_type=F32)
    return (energy * jnp.concatenate([kernel, kernel], axis=0)).astype(BF16)


def energy_kernel(count, factor_scale, *refs):
    pieces = refs[:count]
    turned_ref, w_mix_ref, energy_ref = refs[count:]
    trig, rows, channels = energy_ref.shape
    total = pieces[0][...].astype(F32)
    for piece in pieces[1:]:
        total = total + piece[...].astype(F32)
    owned = total.reshape(trig * rows, channels)
    energy = mixed(owned, turned_ref[:rows, :].astype(F32), w_mix_ref[...], factor_scale)
    energy_ref[...] = energy.reshape(trig, rows, channels)


def energy_of(pieces, turned, w_mix, factor_scale, held):
    (energy,) = call(
        functools.partial(energy_kernel, len(pieces), factor_scale),
        [(VMEM, (pieces[0].shape, BF16))],
        in_vmem([*pieces, turned, w_mix]),
        held=held,
    )
    return energy


def stack_kernel(*refs):
    pieces, out_ref = refs[:-1], refs[-1]
    start = 0
    for piece in pieces:
        for part in range(piece.shape[0]):
            out_ref[start : start + piece.shape[1], :] = piece[part]
            start += piece.shape[1]


def stacked(pieces, held):
    rows = sum(piece.shape[0] * piece.shape[1] for piece in pieces)
    (whole,) = call(stack_kernel, [(VMEM, ((rows, pieces[0].shape[2]), BF16))], in_vmem(pieces), held=held)
    return whole


def near_kernel(own, others, *refs):
    refs = list(refs)
    energies = [refs.pop(0) for _ in own]
    handed_ref = refs.pop(0) if others else None
    start_ref = refs.pop(0) if others else None
    table_ref, out_ref, turned_ref = refs
    rows = table_ref.shape[1]
    places = [*own, *others]
    for index in range(len(places)):
        if index < len(own):
            energy = energies[index][...]
        else:
            first = (index - len(own)) * rows
            energy = handed_ref[first : first + rows, :]
        turned_ref[index] = energy.astype(F32).T.astype(BF16)
    atoms = out_ref.shape[1]
    tile = math.gcd(atoms, 512)
    for start in range(0, atoms, tile):
        span = slice(start, start + tile)
        total = start_ref[:, span] if others else None
        for index, place in enumerate(places):
            part = jnp.dot(turned_ref[index], table_ref[place, :, span], preferred_element_type=F32)
            total = part if total is None else total + part
        out_ref[:, span] = total


def near_call(own, others, energies, table, handed=(), start=(), held=()):
    rows, atoms = table.shape[1:]
    channels = energies[0].shape[-1]
    (total,) = call(
        functools.partial(near_kernel, own, others),
        [(VMEM, ((channels, atoms), F32))],
        in_vmem([*[energy.reshape(rows, channels) for energy in energies], *handed, *start, table]),
        [pltpu.VMEM((len(own) + len(others), channels, rows), BF16)],
        held,
    )
    return total


def final_kernel(
    places, base, lines, scale, counts_ref, codes_ref, near_ref, message_ref, handed_ref, ends_from_ref, table_ref, *refs
):
    radial_ref, line_refs, outer, w_ref = refs[0], refs[1 : 1 + lines], refs[1 + lines : 3 + lines], refs[3 + lines]
    out_ref, turned_ref, result_ref, found_ref, ends_ref, semaphores = refs[4 + lines :]
    masked_ref = line_refs[0]
    cells, slots, channels = out_ref.shape
    rows = table_ref.shape[1]
    for index in range(len(places)):
        turned_ref[index] = handed_ref[index * rows : (index + 1) * rows, :].astype(F32).T.astype(BF16)
    ends_ref[:2] = message_ref[:2]
    ends_ref[2:] = message_ref[cells - 2 :]
    fill_ends(
        slots, codes_ref, radial_ref, line_refs, outer, ends_from_ref, base, w_ref, found_ref, ends_ref
    )
    slot_ids = lax.broadcasted_iota(jnp.int32, (slots, channels), 0)
    group = math.gcd(cells, 2)
    share = math.gcd(cells, 4)
    leaving = []
    for first in range(0, cells, group):
        span = slice(first * slots, (first + group) * slots)
        total = near_ref[:, span]
        for index, place in enumerate(places):
            total = total + jnp.dot(turned_ref[index], table_ref[place, :, span], preferred_element_type=F32)
        for cell in range(first, first + group):
            value = total[:, (cell - first) * slots : (cell - first + 1) * slots].T * scale
            value += ends_ref[cell] if cell < 2 else ends_ref[cell - cells + 4] if cell >= cells - 2 else message_ref[cell]
            value = value * (0.5 + 0.5 * jnp.tanh(0.5 * value))
            result = masked_ref[cell * slots : (cell + 1) * slots, :].astype(F32) + value
            result_ref[cell] = jnp.where(slot_ids < counts_ref[cell], result, 0.0).astype(BF16)
        if (first + group) % share == 0:
            done = pl.ds(first + group - share, share)
            leaving += begin([result_ref.at[done]], [out_ref.at[done]], semaphores, first // share)
    finish(leaving)


def final_call(
    places, base, counts, codes, near, message, handed, ends_from, table, radial, lines, outer, w_msg, scale
):
    cells, slots, channels = message.shape
    (result,) = call(
        functools.partial(final_kernel, places, base, len(lines), scale),
        [(HBM, (message.shape, BF16))],
        [(SMEM, counts), (SMEM, codes)] + in_vmem([near, message, handed, ends_from, table, radial, *lines, *outer, w_msg]),
        [
            pltpu.VMEM((len(places), channels, table.shape[1]), BF16),
            pltpu.VMEM(message.shape, BF16),
            pltpu.SMEM((9 * cells,), jnp.int32),
            pltpu.VMEM((4, slots, channels), F32),
            pltpu.SemaphoreType.DMA((cells // math.gcd(cells, 4),)),
        ],
    )
    return result


def body(features, offsets, radial, neighbours, counts, wavevectors, w_msg, w_mix):
    _, cells, slots, channels = features.shape
    wave_count = wavevectors.shape[1]
    slabs, dev_count = lax.axis_size("grp"), lax.axis_size("dev")
    slab = lax.axis_index("grp")
    cell_line = cells * dev_count
    total_slots = slabs * cell_line * slots
    atoms = cells * slots
    lengths = (float(cell_line), float(slabs))
    features, offsets, counts = features[0], offsets[0].transpose(1, 0, 2), counts[0]

    swap = pairs_at("grp", 1, 1)
    sibling_offsets = lax.ppermute(offsets, "grp", swap)
    if slabs == 2:
        sibling_counts = lax.ppermute(counts, "grp", swap)
        sibling_features = lax.ppermute(features, "grp", swap)
    else:
        up = [(i, i + 1) for i in range(slabs - 1)]
        down = [(j, i) for i, j in up]
        near = [(lax.ppermute(counts, "grp", way), lax.ppermute(features, "grp", way)) for way in (up, down)]
        even = slab % 2 == 0
        sibling_counts = jnp.where(even, near[1][0], near[0][0])
        sibling_features = jnp.where(even, near[1][1], near[0][1])

    blocks = 4
    digits = [("grp", 1, 2), ("dev", 1, blocks)]
    twos = [("dev", blocks << bit) for bit in range((dev_count // blocks).bit_length() - 1)]
    twos += [("grp", 2 << bit) for bit in range((slabs // 2).bit_length() - 1)]
    half = wave_count // 2
    block = half // blocks
    table = ((2 * block, atoms), BF16)
    sums = ((2 * block, channels), F32)
    piece = ((2 * block, channels), BF16)
    places_type = ((32, atoms), BF16)
    rows_type = ((atoms, channels), BF16)
    whole_table = (VMEM, ((2 * blocks,) + table[0], BF16))
    scratch = [pltpu.VMEM(*table)]

    def sent(part, place):
        return lax.ppermute(part.reshape(2, block, channels), "dev", pairs_at("dev", 1, place))

    order = [*range(blocks - 1, 0, -1), 0]
    early = order[: min(2, blocks - 1)]
    masked, places, turned, tables, *outs = call(
        functools.partial(own_kernel, early, block, digits, lengths),
        [(VMEM, rows_type), (VMEM, places_type), (VMEM, ((wave_count, 32), BF16)), whole_table]
        + [(VMEM, sums)] * len(early),
        in_hbm([wavevectors, offsets, counts, features]),
        [
            pltpu.VMEM((32, wave_count), F32),
            pltpu.VMEM(wavevectors.shape, jnp.int32),
            pltpu.VMEM(offsets.shape, F32),
            pltpu.SMEM(counts.shape, jnp.int32),
            pltpu.VMEM(features.shape, BF16),
            pltpu.SemaphoreType.DMA((4,)),
        ],
    )
    started = dict(zip(early, outs))
    sibling, sibling_places, part = call(
        functools.partial(sibling_kernel, early[0], block, lengths),
        [(VMEM, rows_type), (VMEM, places_type), (VMEM, piece)],
        [(SMEM, sibling_counts)] + in_vmem([sibling_features, sibling_offsets, turned, started[early[0]]]),
        scratch,
    )
    received = {early[0]: sent(part, early[0])}
    for place in early[1:]:
        (part,) = call(
            functools.partial(continued_kernel, place, block),
            [(VMEM, piece)],
            in_vmem([turned, sibling_places, sibling, started[place]]),
            scratch,
        )
        received[place] = sent(part, place)
    for place in order[len(early) :]:
        tables, part = call(
            functools.partial(both_kernel, place, block),
            [whole_table, (VMEM, piece if place else sums)],
            in_vmem([turned, places, masked, sibling_places, sibling, tables]),
            scratch,
            [part] if place else [received[early[0]]],
            same={5: 0},
        )
        if place:
            received[place] = sent(part, place)
    pieces = [part.reshape(2, block, channels)] + [received[place] for place in range(1, blocks)]

    if slabs == 2:
        lines = [masked, sibling]
    else:
        lines = [masked] + [
            jnp.where(jnp.arange(slots)[None, :, None] < count[:, None, None], cell, jnp.bfloat16(0)).reshape(
                atoms, channels
            )
            for count, cell in near
        ]
    edge = (VMEM, ((len(lines), slots, channels), BF16))

    def rest_of(tables, first, last, held, more=(), outs=(), scratch=()):
        return call(
            functools.partial(rest_kernel, range(first, last), block, len(more[:-1])),
            [whole_table, *outs],
            in_vmem([turned, places, tables, *more[:-1]]) + in_hbm(more[-1:]),
            scratch,
            held,
            {2: 0},
        )

    middle = blocks + blocks // 2
    (tables,) = rest_of(tables, blocks, middle, [part])

    total, half_total = added(pieces, [tables])
    radial = radial.reshape(-1, slots, slots)
    radial_type = (VMEM, ((radial.shape[0] + 1, slots, slots), BF16))
    tables, *edges, radial = rest_of(
        tables, middle, 2 * blocks, [total],
        [*lines, radial], [edge, edge, radial_type], [pltpu.SemaphoreType.DMA((1,))],
    )

    right = [(i, i + 1) for i in range(dev_count - 1)]
    left = [(j, i) for i, j in right]
    if slabs == 2:
        outer = [
            lax.ppermute(part, ("grp", "dev"), [(dev_count + i, dev_count + j) for i, j in way])
            for part, way in zip(edges, (right, left))
        ]
    else:
        outer = [lax.ppermute(part, "dev", way) for part, way in zip(edges, (right, left))]

    held = [tables, radial]
    for axis, stride in twos[:-1]:
        total, half_total = added([total, lax.ppermute(half_total, axis, pairs_at(axis, stride, 1))], held)
        held = []
    axis, stride = twos[-1]
    pieces = [total, lax.ppermute(half_total, axis, pairs_at(axis, stride, 1))]
    energy = energy_of(pieces, turned, w_mix, 1.0 / math.sqrt(total_slots), [tables, radial])

    energies = [energy] + [
        lax.ppermute(energy, "dev", pairs_at("dev", 1, place)) for place in range(1, blocks)
    ]

    codes = neighbours[0].T
    (message,) = call(
        functools.partial(short_kernel, len(lines)),
        [(VMEM, ((cells, slots, channels), F32))],
        [(SMEM, codes)] + in_vmem([radial, *lines, w_msg]),
        [pltpu.SMEM((9 * cells,), jnp.int32)],
        [energy, tables],
    )
    soon, late = [0], list(range(1, blocks))
    soon_energies, late_energies = [energies[place] for place in soon], [energies[place] for place in late]
    handed = lax.ppermute(stacked([*soon_energies, *(outer if slabs == 2 else [])], [message]), "grp", swap)
    near_sum = near_call(soon, [], soon_energies, tables, held=[message])
    handed_late = lax.ppermute(stacked(late_energies, [near_sum]), "grp", swap)
    near_sum = near_call(
        late, [blocks + place for place in soon], late_energies, tables, [handed], [near_sum]
    )
    scale = 8.0 / math.sqrt(wave_count)
    result = final_call(
        [blocks + place for place in late], len(soon) * 2 * block, counts, codes, near_sum, message, handed_late, handed,
        tables, radial, lines, outer, w_msg, scale,
    )
    return result[None]


def solution(mesh):
    in_specs = (
        P("grp", "dev", None, None),
        P("grp", "dev", None, None),
        P("grp", "dev", None, None, None),
        P("grp", "dev", None),
        P("grp", "dev"),
        P(),
        P(),
        P(),
    )
    out_specs = P("grp", "dev", None, None)
    return jax.shard_map(body, mesh=mesh, in_specs=in_specs, out_specs=out_specs, check_vma=False)
```

```python
import functools
import math

import jax
import jax.numpy as jnp
from jax import lax
from jax.experimental import pallas as pl
from jax.experimental.pallas import tpu as pltpu
from jax.sharding import PartitionSpec as P

F32 = jnp.float32
BF16 = jnp.bfloat16
VMEM = pl.BlockSpec(memory_space=pltpu.VMEM)
SMEM = pl.BlockSpec(memory_space=pltpu.SMEM)
HBM = pl.BlockSpec(memory_space=pltpu.HBM)
PARAMS = pltpu.CompilerParams(vmem_limit_bytes=14 * 1024 * 1024)
LANES = 128
SIN = (4.44287957, -7.30781668, 3.59777418, -0.79119939)
COS = (1.41420401, -6.97763732, 5.71518787, -1.72821389)


def call(kernel, outs, operands, scratch=(), held=(), same=()):
    ahead = len(operands)
    operands = list(operands) + [(VMEM, array) for array in held]

    def without_held(*refs):
        kernel(*refs[:ahead], *refs[len(operands) :])

    return pl.pallas_call(
        without_held,
        in_specs=[place for place, _ in operands],
        out_specs=[place for place, _ in outs],
        out_shape=[place.memory_space(*kind) for place, kind in outs],
        scratch_shapes=list(scratch),
        input_output_aliases=dict(same),
        compiler_params=PARAMS,
        cost_estimate=pl.CostEstimate(flops=0, bytes_accessed=0, transcendentals=0),
    )(
        *[
            array if place is SMEM else pltpu.with_memory_space_constraint(array, place.memory_space)
            for place, array in operands
        ]
    )


def in_vmem(arrays):
    return [(VMEM, array) for array in arrays]


def in_hbm(arrays):
    return [(HBM, array) for array in arrays]


def begin(sources, targets, semaphores, first=0):
    copies = [
        pltpu.make_async_copy(source, target, semaphores.at[first + index])
        for index, (source, target) in enumerate(zip(sources, targets))
    ]
    for copy in copies:
        copy.start()
    return copies


def finish(copies):
    for copy in copies:
        copy.wait()


def pairs_at(axis, stride, offset):
    return [(place, place ^ (offset * stride)) for place in range(lax.axis_size(axis))]


def fill_places(offsets_ref, places_ref, first, slab, cell_line, slabs):
    _, cells, slots = offsets_ref.shape
    line = lax.broadcasted_iota(jnp.int32, (8, slots), 0)
    along_z_base = slab.astype(F32)
    for cell in range(cells):
        along_x = ((first + cell).astype(F32) + offsets_ref[0, cell : cell + 1]) / cell_line
        along_y = offsets_ref[1, cell : cell + 1]
        along_z = (along_z_base + offsets_ref[2, cell : cell + 1]) / slabs
        full = jnp.where(line == 0, along_x, jnp.where(line == 1, along_y, jnp.where(line == 2, along_z, 0.0)))
        high = full.astype(BF16).astype(F32)
        middle = (full - high).astype(BF16).astype(F32)
        low = full - high - middle
        parts = jnp.concatenate([high, middle, low, jnp.zeros_like(low)], axis=0)
        places_ref[:, cell * slots : (cell + 1) * slots] = parts.astype(BF16)


def fill_masked(counts_ref, features_ref, masked_ref):
    cells, slots, channels = features_ref.shape
    slot_ids = lax.broadcasted_iota(jnp.int32, (slots, channels), 0)
    for cell in range(cells):
        kept = jnp.where(slot_ids < counts_ref[cell], features_ref[cell].astype(F32), 0.0)
        masked_ref[cell * slots : (cell + 1) * slots, :] = kept.astype(BF16)


def fill_waves(waves_ref, padded_ref, turned_ref, flips):
    count = waves_ref.shape[1]
    waves = waves_ref[...].astype(F32)
    padded_ref[...] = jnp.zeros_like(padded_ref)
    for part in range(3):
        padded_ref[8 * part : 8 * part + 3, :] = waves
    rows = lax.broadcasted_iota(jnp.int32, (LANES, LANES), 0)
    columns = lax.broadcasted_iota(jnp.int32, (LANES, LANES), 1)
    order = jnp.where((rows ^ (flips & (LANES - 1))) == columns, 1.0, 0.0).astype(BF16)
    for block in range(count // LANES):
        source = pl.multiple_of((block ^ (flips // LANES)) * LANES, LANES)
        taken = padded_ref[:, pl.ds(source, LANES)].astype(BF16)
        turned = lax.dot_general(order, taken, (((1,), (1,)), ((), ())), preferred_element_type=F32)
        turned_ref[block * LANES : (block + 1) * LANES, :] = turned.astype(BF16)


def fill_table(waves, places_ref, table_ref):
    block = waves.shape[0]
    atoms = places_ref.shape[1]
    tile = math.gcd(atoms, 256)
    for start in range(0, atoms, tile):
        span = slice(start, start + tile)
        turns = jnp.dot(waves, places_ref[:, span], preferred_element_type=F32)
        part = turns - jnp.round(turns)
        square = part * part
        sine = part * (SIN[0] + square * (SIN[1] + square * (SIN[2] + square * SIN[3])))
        cosine = COS[0] + square * (COS[1] + square * (COS[2] + square * COS[3]))
        table_ref[:block, span] = (1.0 - sine * sine).astype(BF16)
        table_ref[block:, span] = (sine * cosine).astype(BF16)


def sums_of(table_ref, rows_ref):
    return jnp.dot(table_ref[...], rows_ref[...], preferred_element_type=F32)


def own_kernel(early, block, digits, lengths, *refs):
    sources, refs = refs[:4], refs[4:]
    masked_ref, places_ref, turned_ref, table_ref = refs[:4]
    sums = refs[4 : 4 + len(early)]
    padded_ref, waves_ref, offsets_ref, counts_ref, features_ref, semaphores = refs[4 + len(early) :]
    copies = begin(sources, (waves_ref, offsets_ref, counts_ref, features_ref), semaphores)
    cells = features_ref.shape[0]
    dev, slab = lax.axis_index("dev"), lax.axis_index("grp")
    flips = jnp.int32(0)
    weight = waves_ref.shape[1]
    for axis, stride, radix in digits:
        weight //= radix
        flips += ((slab if axis == "grp" else dev) // stride % radix) * weight
    copies[0].wait()
    fill_waves(waves_ref, padded_ref, turned_ref, flips)
    copies[1].wait()
    fill_places(offsets_ref, places_ref, dev * cells, slab, *lengths)
    for index, (place, sums_ref) in enumerate(zip(early, sums)):
        fill_table(turned_ref[place * block : (place + 1) * block, :], places_ref, table_ref.at[place])
        if index == 0:
            copies[2].wait()
            copies[3].wait()
            fill_masked(counts_ref, features_ref, masked_ref)
        sums_ref[...] = sums_of(table_ref.at[place], masked_ref)


def sibling_kernel(
    place, block, lengths, counts_ref, features_ref, offsets_ref, turned_ref, start_ref,
    masked_ref, places_ref, piece_ref, table_ref,
):
    cells = features_ref.shape[0]
    fill_places(offsets_ref, places_ref, lax.axis_index("dev") * cells, lax.axis_index("grp") ^ 1, *lengths)
    fill_masked(counts_ref, features_ref, masked_ref)
    fill_table(turned_ref[place * block : (place + 1) * block, :], places_ref, table_ref)
    piece_ref[...] = (start_ref[...] + sums_of(table_ref, masked_ref)).astype(piece_ref.dtype)


def continued_kernel(place, block, turned_ref, places_ref, masked_ref, start_ref, piece_ref, table_ref):
    fill_table(turned_ref[place * block : (place + 1) * block, :], places_ref, table_ref)
    piece_ref[...] = (start_ref[...] + sums_of(table_ref, masked_ref)).astype(piece_ref.dtype)


def both_kernel(
    place, block, turned_ref, own_places_ref, own_ref, places_ref, masked_ref, _, kept_ref, piece_ref, table_ref
):
    waves = turned_ref[place * block : (place + 1) * block, :]
    fill_table(waves, own_places_ref, kept_ref.at[place])
    total = sums_of(kept_ref.at[place], own_ref)
    fill_table(waves, places_ref, table_ref)
    piece_ref[...] = (total + sums_of(table_ref, masked_ref)).astype(piece_ref.dtype)


def fill_edges(lines, last_ref, first_ref):
    slots = last_ref.shape[1]
    for line, rows_ref in enumerate(lines):
        last_ref[line] = rows_ref[rows_ref.shape[0] - slots :, :]
        first_ref[line] = rows_ref[:slots, :]


def rest_kernel(blocks, block, lines, turned_ref, places_ref, _, *refs):
    kept_ref, *outs = refs[lines + 1 if lines else 0 :]
    if lines:
        *edges, radial_ref, semaphores = outs
        source_ref = refs[lines]
        count = source_ref.shape[0]
        copies = begin([source_ref], [radial_ref.at[pl.ds(0, count)]], semaphores)
        radial_ref[count] = jnp.zeros_like(radial_ref[count])
        fill_edges(refs[:lines], *edges)
    for place in blocks:
        fill_table(turned_ref[place * block : (place + 1) * block, :], places_ref, kept_ref.at[place])
    if lines:
        finish(copies)


def fill_found(codes_ref, found_ref, wanted):
    pairs, cells = codes_ref.shape
    for cell in wanted:
        for code in range(9):
            found_ref[9 * cell + code] = cells * pairs
        for pair in range(pairs):
            found_ref[9 * cell + codes_ref[pair, cell]] = cell * pairs + pair


def window_sum(start, radial_ref, found_ref, lines, takers):
    slab, slabs = lax.axis_index("grp"), lax.axis_size("grp")
    nothing = radial_ref.shape[0] - 1
    levels = [1, 2 - 2 * slab] if slabs == 2 else [1, 0, 2]
    total = None
    for level, taken in zip(levels, lines):
        rows = []
        for cell in takers:
            halves = []
            for place in (start, start + 1):
                along = place - cell
                index = found_ref[9 * cell + 3 * level + along] if 0 <= along < 3 else nothing
                halves.append(radial_ref[index])
            rows.append(jnp.concatenate(halves, axis=1))
        part = jnp.dot(jnp.concatenate(rows, axis=0), taken, preferred_element_type=F32)
        total = part if total is None else total + part
    return total


def short_kernel(lines, codes_ref, radial_ref, *refs):
    line_refs, (w_ref, message_ref, found_ref) = refs[:lines], refs[lines:]
    cells, slots, channels = message_ref.shape
    fill_found(codes_ref, found_ref, range(cells))
    carried = None
    for start in range(2, cells, 2):
        taken = [line_ref[(start - 1) * slots : (start + 1) * slots, :] for line_ref in line_refs]
        total = window_sum(start, radial_ref, found_ref, taken, range(start - 2, start + 2))
        gathered = total[: 2 * slots]
        if start > 2:
            gathered = carried + gathered
            gathered = jnp.dot(gathered.astype(BF16), w_ref[...], preferred_element_type=F32)
        message_ref[start - 2 : start] = gathered.reshape(2, slots, channels)
        carried = total[2 * slots :]
    message_ref[cells - 2 : cells] = carried.reshape(2, slots, channels)


def fill_ends(slots, codes_ref, radial_ref, line_refs, outer, handed_ref, base, w_ref, found_ref, ends_ref):
    slab, slabs = lax.axis_index("grp"), lax.axis_size("grp")
    cells = codes_ref.shape[1]
    fill_found(codes_ref, found_ref, (0, 1, cells - 2, cells - 1))
    for side, start in enumerate((0, cells)):
        taken = []
        for line, line_ref in enumerate(line_refs):
            cell = outer[side][line]
            if slabs == 2:
                first = base + (2 * side + 1 - line) * slots
                cell = jnp.where(slab == 1, cell, handed_ref[first : first + slots, :])
            if side == 0:
                taken.append(jnp.concatenate([cell, line_ref[:slots, :]], axis=0))
            else:
                taken.append(jnp.concatenate([line_ref[(cells - 1) * slots :, :], cell], axis=0))
        takers = (0, 1) if side == 0 else (cells - 2, cells - 1)
        total = window_sum(start, radial_ref, found_ref, taken, takers)
        span = slice(2 * side, 2 * side + 2)
        gathered = ends_ref[span].reshape(total.shape) + total
        message = jnp.dot(gathered.astype(BF16), w_ref[...], preferred_element_type=F32)
        ends_ref[span] = message.reshape(2, slots, total.shape[1])


def add_kernel(*refs):
    pieces, (total_ref, sent_ref) = refs[:-2], refs[-2:]
    total = pieces[0][...].astype(F32)
    for piece in pieces[1:]:
        total = total + piece[...].astype(F32)
    total_ref[...] = total
    sent_ref[...] = total.astype(sent_ref.dtype)


def added(pieces, held):
    shape = pieces[0].shape
    return call(add_kernel, [(VMEM, (shape, F32)), (VMEM, (shape, BF16))], in_vmem(pieces), held=held)


def mixed(owned, waves, w_mix, factor_scale):
    waves = jnp.where(lax.broadcasted_iota(jnp.int32, waves.shape, 1) < 3, waves, 0.0)
    square = jnp.sum(waves * waves, axis=1, keepdims=True)
    kernel = jnp.exp(-square / 128.0) / (1.0 + square / 64.0)
    factors = (owned * factor_scale).astype(BF16)
    energy = jnp.dot(factors, w_mix, preferred_element_type=F32)
    return (energy * jnp.concatenate([kernel, kernel], axis=0)).astype(BF16)


def energy_kernel(count, factor_scale, *refs):
    pieces = refs[:count]
    turned_ref, w_mix_ref, energy_ref = refs[count:]
    trig, rows, channels = energy_ref.shape
    total = pieces[0][...].astype(F32)
    for piece in pieces[1:]:
        total = total + piece[...].astype(F32)
    owned = total.reshape(trig * rows, channels)
    energy = mixed(owned, turned_ref[:rows, :].astype(F32), w_mix_ref[...], factor_scale)
    energy_ref[...] = energy.reshape(trig, rows, channels)


def energy_of(pieces, turned, w_mix, factor_scale, held):
    (energy,) = call(
        functools.partial(energy_kernel, len(pieces), factor_scale),
        [(VMEM, (pieces[0].shape, BF16))],
        in_vmem([*pieces, turned, w_mix]),
        held=held,
    )
    return energy


def stack_kernel(*refs):
    pieces, out_ref = refs[:-1], refs[-1]
    start = 0
    for piece in pieces:
        for part in range(piece.shape[0]):
            out_ref[start : start + piece.shape[1], :] = piece[part]
            start += piece.shape[1]


def stacked(pieces, held):
    rows = sum(piece.shape[0] * piece.shape[1] for piece in pieces)
    (whole,) = call(stack_kernel, [(VMEM, ((rows, pieces[0].shape[2]), BF16))], in_vmem(pieces), held=held)
    return whole


def near_kernel(own, others, *refs):
    refs = list(refs)
    energies = [refs.pop(0) for _ in own]
    handed_ref = refs.pop(0) if others else None
    start_ref = refs.pop(0) if others else None
    table_ref, out_ref, turned_ref = refs
    rows = table_ref.shape[1]
    places = [*own, *others]
    for index in range(len(places)):
        if index < len(own):
            energy = energies[index][...]
        else:
            first = (index - len(own)) * rows
            energy = handed_ref[first : first + rows, :]
        turned_ref[index] = energy.astype(F32).T.astype(BF16)
    atoms = out_ref.shape[1]
    tile = math.gcd(atoms, 512)
    for start in range(0, atoms, tile):
        span = slice(start, start + tile)
        total = start_ref[:, span] if others else None
        for index, place in enumerate(places):
            part = jnp.dot(turned_ref[index], table_ref[place, :, span], preferred_element_type=F32)
            total = part if total is None else total + part
        out_ref[:, span] = total


def near_call(own, others, energies, table, handed=(), start=(), held=()):
    rows, atoms = table.shape[1:]
    channels = energies[0].shape[-1]
    (total,) = call(
        functools.partial(near_kernel, own, others),
        [(VMEM, ((channels, atoms), F32))],
        in_vmem([*[energy.reshape(rows, channels) for energy in energies], *handed, *start, table]),
        [pltpu.VMEM((len(own) + len(others), channels, rows), BF16)],
        held,
    )
    return total


def final_kernel(
    places, base, lines, scale, counts_ref, codes_ref, near_ref, message_ref, handed_ref, ends_from_ref, table_ref, *refs
):
    radial_ref, line_refs, outer, w_ref = refs[0], refs[1 : 1 + lines], refs[1 + lines : 3 + lines], refs[3 + lines]
    out_ref, turned_ref, result_ref, found_ref, ends_ref, semaphores = refs[4 + lines :]
    masked_ref = line_refs[0]
    cells, slots, channels = out_ref.shape
    rows = table_ref.shape[1]
    for index in range(len(places)):
        turned_ref[index] = handed_ref[index * rows : (index + 1) * rows, :].astype(F32).T.astype(BF16)
    ends_ref[:2] = message_ref[:2]
    ends_ref[2:] = message_ref[cells - 2 :]
    fill_ends(
        slots, codes_ref, radial_ref, line_refs, outer, ends_from_ref, base, w_ref, found_ref, ends_ref
    )
    slot_ids = lax.broadcasted_iota(jnp.int32, (slots, channels), 0)
    group = math.gcd(cells, 2)
    share = math.gcd(cells, 4)
    leaving = []
    for first in range(0, cells, group):
        span = slice(first * slots, (first + group) * slots)
        total = near_ref[:, span]
        for index, place in enumerate(places):
            total = total + jnp.dot(turned_ref[index], table_ref[place, :, span], preferred_element_type=F32)
        for cell in range(first, first + group):
            value = total[:, (cell - first) * slots : (cell - first + 1) * slots].T * scale
            value += ends_ref[cell] if cell < 2 else ends_ref[cell - cells + 4] if cell >= cells - 2 else message_ref[cell]
            value = value * (0.5 + 0.5 * jnp.tanh(0.5 * value))
            result = masked_ref[cell * slots : (cell + 1) * slots, :].astype(F32) + value
            result_ref[cell] = jnp.where(slot_ids < counts_ref[cell], result, 0.0).astype(BF16)
        if (first + group) % share == 0:
            done = pl.ds(first + group - share, share)
            leaving += begin([result_ref.at[done]], [out_ref.at[done]], semaphores, first // share)
    finish(leaving)


def final_call(
    places, base, counts, codes, near, message, handed, ends_from, table, radial, lines, outer, w_msg, scale
):
    cells, slots, channels = message.shape
    (result,) = call(
        functools.partial(final_kernel, places, base, len(lines), scale),
        [(HBM, (message.shape, BF16))],
        [(SMEM, counts), (SMEM, codes)] + in_vmem([near, message, handed, ends_from, table, radial, *lines, *outer, w_msg]),
        [
            pltpu.VMEM((len(places), channels, table.shape[1]), BF16),
            pltpu.VMEM(message.shape, BF16),
            pltpu.SMEM((9 * cells,), jnp.int32),
            pltpu.VMEM((4, slots, channels), F32),
            pltpu.SemaphoreType.DMA((cells // math.gcd(cells, 4),)),
        ],
    )
    return result


def body(features, offsets, radial, neighbours, counts, wavevectors, w_msg, w_mix):
    _, cells, slots, channels = features.shape
    wave_count = wavevectors.shape[1]
    slabs, dev_count = lax.axis_size("grp"), lax.axis_size("dev")
    slab = lax.axis_index("grp")
    cell_line = cells * dev_count
    total_slots = slabs * cell_line * slots
    atoms = cells * slots
    lengths = (float(cell_line), float(slabs))
    features, offsets, counts = features[0], offsets[0].transpose(1, 0, 2), counts[0]

    swap = pairs_at("grp", 1, 1)
    sibling_offsets = lax.ppermute(offsets, "grp", swap)
    if slabs == 2:
        sibling_counts = lax.ppermute(counts, "grp", swap)
        sibling_features = lax.ppermute(features, "grp", swap)
    else:
        up = [(i, i + 1) for i in range(slabs - 1)]
        down = [(j, i) for i, j in up]
        near = [(lax.ppermute(counts, "grp", way), lax.ppermute(features, "grp", way)) for way in (up, down)]
        even = slab % 2 == 0
        sibling_counts = jnp.where(even, near[1][0], near[0][0])
        sibling_features = jnp.where(even, near[1][1], near[0][1])

    blocks = 4
    digits = [("grp", 1, 2), ("dev", 1, blocks)]
    twos = [("dev", blocks << bit) for bit in range((dev_count // blocks).bit_length() - 1)]
    twos += [("grp", 2 << bit) for bit in range((slabs // 2).bit_length() - 1)]
    half = wave_count // 2
    block = half // blocks
    table = ((2 * block, atoms), BF16)
    sums = ((2 * block, channels), F32)
    piece = ((2 * block, channels), BF16)
    places_type = ((32, atoms), BF16)
    rows_type = ((atoms, channels), BF16)
    whole_table = (VMEM, ((2 * blocks,) + table[0], BF16))
    scratch = [pltpu.VMEM(*table)]

    def sent(part, place):
        return lax.ppermute(part.reshape(2, block, channels), "dev", pairs_at("dev", 1, place))

    order = [*range(blocks - 1, 0, -1), 0]
    early = order[: min(2, blocks - 1)]
    masked, places, turned, tables, *outs = call(
        functools.partial(own_kernel, early, block, digits, lengths),
        [(VMEM, rows_type), (VMEM, places_type), (VMEM, ((wave_count, 32), BF16)), whole_table]
        + [(VMEM, sums)] * len(early),
        in_hbm([wavevectors, offsets, counts, features]),
        [
            pltpu.VMEM((32, wave_count), F32),
            pltpu.VMEM(wavevectors.shape, jnp.int32),
            pltpu.VMEM(offsets.shape, F32),
            pltpu.SMEM(counts.shape, jnp.int32),
            pltpu.VMEM(features.shape, BF16),
            pltpu.SemaphoreType.DMA((4,)),
        ],
    )
    started = dict(zip(early, outs))
    sibling, sibling_places, part = call(
        functools.partial(sibling_kernel, early[0], block, lengths),
        [(VMEM, rows_type), (VMEM, places_type), (VMEM, piece)],
        [(SMEM, sibling_counts)] + in_vmem([sibling_features, sibling_offsets, turned, started[early[0]]]),
        scratch,
    )
    received = {early[0]: sent(part, early[0])}
    for place in early[1:]:
        (part,) = call(
            functools.partial(continued_kernel, place, block),
            [(VMEM, piece)],
            in_vmem([turned, sibling_places, sibling, started[place]]),
            scratch,
        )
        received[place] = sent(part, place)
    for place in order[len(early) :]:
        tables, part = call(
            functools.partial(both_kernel, place, block),
            [whole_table, (VMEM, piece if place else sums)],
            in_vmem([turned, places, masked, sibling_places, sibling, tables]),
            scratch,
            [part] if place else [received[early[0]]],
            same={5: 0},
        )
        if place:
            received[place] = sent(part, place)
    pieces = [part.reshape(2, block, channels)] + [received[place] for place in range(1, blocks)]

    if slabs == 2:
        lines = [masked, sibling]
    else:
        lines = [masked] + [
            jnp.where(jnp.arange(slots)[None, :, None] < count[:, None, None], cell, jnp.bfloat16(0)).reshape(
                atoms, channels
            )
            for count, cell in near
        ]
    edge = (VMEM, ((len(lines), slots, channels), BF16))

    def rest_of(tables, first, last, held, more=(), outs=(), scratch=()):
        return call(
            functools.partial(rest_kernel, range(first, last), block, len(more[:-1])),
            [whole_table, *outs],
            in_vmem([turned, places, tables, *more[:-1]]) + in_hbm(more[-1:]),
            scratch,
            held,
            {2: 0},
        )

    middle = blocks + blocks // 2
    (tables,) = rest_of(tables, blocks, middle, [part])

    total, half_total = added(pieces, [tables])
    radial = radial.reshape(-1, slots, slots)
    radial_type = (VMEM, ((radial.shape[0] + 1, slots, slots), BF16))
    tables, *edges, radial = rest_of(
        tables, middle, 2 * blocks, [total],
        [*lines, radial], [edge, edge, radial_type], [pltpu.SemaphoreType.DMA((1,))],
    )

    right = [(i, i + 1) for i in range(dev_count - 1)]
    left = [(j, i) for i, j in right]
    if slabs == 2:
        outer = [
            lax.ppermute(part, ("grp", "dev"), [(dev_count + i, dev_count + j) for i, j in way])
            for part, way in zip(edges, (right, left))
        ]
    else:
        outer = [lax.ppermute(part, "dev", way) for part, way in zip(edges, (right, left))]

    held = [tables, radial]
    for axis, stride in twos[:-1]:
        total, half_total = added([total, lax.ppermute(half_total, axis, pairs_at(axis, stride, 1))], held)
        held = []
    axis, stride = twos[-1]
    pieces = [total, lax.ppermute(half_total, axis, pairs_at(axis, stride, 1))]
    energy = energy_of(pieces, turned, w_mix, 1.0 / math.sqrt(total_slots), [tables, radial])

    energies = [energy] + [
        lax.ppermute(energy, "dev", pairs_at("dev", 1, place)) for place in range(1, blocks)
    ]

    codes = neighbours[0].T
    (message,) = call(
        functools.partial(short_kernel, len(lines)),
        [(VMEM, ((cells, slots, channels), F32))],
        [(SMEM, codes)] + in_vmem([radial, *lines, w_msg]),
        [pltpu.SMEM((9 * cells,), jnp.int32)],
        [energy, tables],
    )
    soon, late = [0], list(range(1, blocks))
    soon_energies, late_energies = [energies[place] for place in soon], [energies[place] for place in late]
    handed = lax.ppermute(stacked([*soon_energies, *(outer if slabs == 2 else [])], [message]), "grp", swap)
    near_sum = near_call(soon, [], soon_energies, tables, held=[message])
    handed_late = lax.ppermute(stacked(late_energies, [near_sum]), "grp", swap)
    near_sum = near_call(
        late, [blocks + place for place in soon], late_energies, tables, [handed], [near_sum]
    )
    scale = 8.0 / math.sqrt(wave_count)
    result = final_call(
        [blocks + place for place in late], len(soon) * 2 * block, counts, codes, near_sum, message, handed_late, handed,
        tables, radial, lines, outer, w_msg, scale,
    )
    return result[None]


def solution(mesh):
    in_specs = (
        P("grp", "dev", None, None),
        P("grp", "dev", None, None),
        P("grp", "dev", None, None, None),
        P("grp", "dev", None),
        P("grp", "dev"),
        P(),
        P(),
        P(),
    )
    out_specs = P("grp", "dev", None, None)
    return jax.shard_map(body, mesh=mesh, in_specs=in_specs, out_specs=out_specs, check_vma=False)
```
